32 devices in a mesh: section: 2 (over y), dp: 16 (over z, x, core).
Axes of the slice: x: 2, y: 2, z: 4, core: 2. Of those that a mesh axis runs over, the one named last changes fastest.
Arguments:
- layer_input: bfloat16 [2, 2, 16, 256, 512], P('section', None, 'dp'), may hold values from -6 to 6
- lengths: int32 [2, 16], P(None, 'dp'), may hold values from 64 to 256, as said below
- attn_qkv: bfloat16 [2, 512, 1536], P('section'), may hold values from -0.25 to 0.25
- attn_out: bfloat16 [2, 512, 512], P('section'), may hold values from -2 to 2
- ffn_in: bfloat16 [2, 512, 2048], P('section'), may hold values from -0.25 to 0.25
- ffn_out: bfloat16 [2, 2048, 512], P('section'), may hold values from -0.125 to 0.125
- cross_weight: bfloat16 [2, 512, 1024], P('section'), as said below
- norm_gain: float32 [2, 3, 512], P('section'), may hold values from 0.5 to 1.5
- norm_bias: float32 [2, 3, 512], P('section'), may hold values from -3 to 3
- cotangent: bfloat16 [2, 2, 16, 256, 512], P('section', None, 'dp'), may hold values from -6 to 6
Outputs:
- layer_output: bfloat16 [2, 2, 16, 256, 512], P('section', None, 'dp')
- input_grad: bfloat16 [2, 2, 16, 256, 512], P('section', None, 'dp')
- grad_attn_qkv: float32 [2, 512, 1536], P('section')
- grad_attn_out: float32 [2, 512, 512], P('section')
- grad_ffn_in: float32 [2, 512, 2048], P('section')
- grad_ffn_out: float32 [2, 2048, 512], P('section')
- grad_cross: float32 [2, 512, 1024], P('section')
- grad_norm_gain: float32 [2, 3, 512], P('section')
- grad_norm_bias: float32 [2, 3, 512], P('section')
The draws below stay inside these ranges and needn't reach their ends.
Inputs may be any that keep to these rules, and one draw needn't show every extreme that they name: `lengths`: in every micro-batch one sentence has the full length 256. `cross_weight`: independent normal entries of mean zero.
All inputs are finite; a program needn't handle non-finite values.
Results may differ from the reference program's by a relative error of at most 0.019.
Values may be sent and summed in bfloat16 or wider, within the bound.
A program may use at most 192 MiB of HBM per device.

```python
import jax
import jax.numpy as jnp
from jax import lax

D = 512
HEADS = 8
FF = 2048
SEQ = 256
MB = 2
SENTS = 16


def draw_lengths(key, part):
    key = jax.random.fold_in(key, 11)
    base_key, pick_key = jax.random.split(key)
    random_lengths = jax.random.randint(base_key, (MB, SENTS), SEQ // 4, SEQ + 1, dtype=jnp.int32)
    chosen = jax.random.randint(pick_key, (MB, 1), 0, SENTS, dtype=jnp.int32)
    columns = jnp.arange(SENTS, dtype=jnp.int32)[None, :]
    return jnp.where(columns == chosen, SEQ, random_lengths).astype(jnp.int32)


def draw_cross_weight(key, part):
    key = jax.random.fold_in(key, 23)
    normal_values = jax.random.normal(key, (2, D, 2 * D), jnp.float32)
    slot_index = jnp.arange(2)[:, None, None]
    column_index = jnp.arange(2 * D)[None, None, :]
    wide_scale = max(D * 4 // SEQ, 1) ** (-0.5)
    drawn_scale = D ** (-0.5)
    factors = jnp.where((slot_index == 1) & (column_index >= D), wide_scale, drawn_scale)
    return (normal_values * factors).astype(jnp.bfloat16)


def block_scale(key, shape, cuts, smallest, largest):
    def one(axis_at, parts):
        steps = jax.random.uniform(jax.random.fold_in(jax.random.fold_in(key, 6), axis_at), (parts,), jnp.float32, smallest / len(cuts), largest / len(cuts))
        return jnp.repeat(jnp.exp(steps), shape[axis_at] // parts).reshape((-1,) + (1,) * (len(shape) - axis_at - 1))

    level = one(*cuts[0])
    for cut in cuts[1:]:
        level = level * one(*cut)
    return level


def scatter_about(stream_key, shape, scale, limit, pieces=(), kind=jnp.bfloat16):
    values = jax.random.normal(stream_key, shape, jnp.float32) * scale
    if len(pieces) > 0:
        values = block_scale(stream_key, shape, pieces, -0.22, 0.18) * values
    return jnp.clip(values, min=-limit, max=limit).astype(kind)


def setup_inputs(seed: int = 0) -> dict:
    arg_keys = jax.random.split(jax.random.key(seed), 11)
    layer_input = scatter_about(arg_keys[0], (2, MB, SENTS, SEQ, D), 1.0, 6.0, ((0, 2), (2, 16)))
    lengths = draw_lengths(jax.random.fold_in(arg_keys[10], 71), 0)
    attn_qkv = scatter_about(arg_keys[2], (2, D, 3 * D), D ** -0.5, 0.25, ((0, 2),))
    attn_out = scatter_about(arg_keys[3], (2, D, D), (max(D * 4 // SEQ, 1)) ** -0.5, 2.0, ((0, 2),))
    ffn_in = scatter_about(arg_keys[4], (2, D, FF), D ** -0.5, 0.25, ((0, 2),))
    ffn_out = scatter_about(arg_keys[5], (2, FF, D), FF ** -0.5, 0.125, ((0, 2),))
    cross_weight = draw_cross_weight(jax.random.fold_in(arg_keys[10], 71), 0)
    norm_gain = jnp.clip(1.0 + 0.1 * jax.random.normal(arg_keys[7], (2, 3, D), jnp.float32), 0.5, 1.5)
    norm_bias = scatter_about(arg_keys[8], (2, 3, D), 0.5, 3.0, ((0, 2),), jnp.float32)
    cotangent = scatter_about(arg_keys[9], (2, MB, SENTS, SEQ, D), 1.0, 6.0, ((0, 2), (2, 16)))
    return dict(layer_input=layer_input, lengths=lengths, attn_qkv=attn_qkv, attn_out=attn_out, ffn_in=ffn_in, ffn_out=ffn_out, cross_weight=cross_weight, norm_gain=norm_gain, norm_bias=norm_bias, cotangent=cotangent)


@jax.custom_vjp
def low(v):
    return lax.optimization_barrier(v.astype(jnp.bfloat16)).astype(jnp.float32)

@jax.custom_vjp
def low_back(v):
    return v

def low_keep(v):
    return (low(v), None)

def low_pass(kept, grad):
    return (grad,)

def back_keep(v):
    return (v, None)

def back_low(kept, grad):
    return (low(grad),)
low.defvjp(low_keep, low_pass)
low_back.defvjp(back_keep, back_low)
FULL_PRECISION = lax.Precision.HIGHEST

def matmul(left_side, right_side):
    return jnp.matmul(left_side, right_side, precision=FULL_PRECISION)

def layer_norm(source, norm_scale, norm_shift):
    center = source - lax.optimization_barrier(jnp.mean(source, axis=-1, keepdims=True))
    spread = lax.optimization_barrier(jnp.mean(center * center, axis=-1, keepdims=True))
    return center * lax.rsqrt(spread + 1e-05) * norm_scale + norm_shift

def split_heads(matrix):
    return matrix.reshape(matrix.shape[:-1] + (HEADS, matrix.shape[-1] // HEADS))

def attend(queries, key_rows, value_rows, usable):
    head_size = queries.shape[-1] // HEADS
    scores = jnp.einsum('gqhd,gkhd->ghqk', split_heads(queries), split_heads(key_rows), precision=FULL_PRECISION) * head_size ** (-0.5)
    scores = jnp.where(usable[:, None, None, :], low_back(scores), -1e+30)
    highest = lax.optimization_barrier(jnp.max(scores, axis=-1, keepdims=True))
    weights = jnp.exp(scores - highest)
    chances = low(weights / lax.optimization_barrier(jnp.sum(weights, axis=-1, keepdims=True)))
    blended = jnp.einsum('ghqk,gkhd->gqhd', chances, split_heads(value_rows), precision=FULL_PRECISION)
    return low(low_back(blended.reshape(queries.shape)))

def self_block(inputs, usable, weight_qkv, weight_out, norm_scale, norm_shift):
    breadth = inputs.shape[-1]
    normed = low(layer_norm(inputs, norm_scale, norm_shift))
    packed = low(low_back(matmul(normed, weight_qkv)))
    blended = attend(packed[..., :breadth], packed[..., breadth:2 * breadth], packed[..., 2 * breadth:], usable)
    return inputs + low_back(matmul(blended, weight_out))

def feed_forward(residual, weight_up, weight_down, norm_scale, norm_shift):
    normed = low(layer_norm(residual, norm_scale, norm_shift))
    hidden = low(jax.nn.gelu(low_back(matmul(normed, weight_up)), approximate=False))
    return residual + low_back(matmul(hidden, weight_down))

def layers_forward(enc_in, dec_in, usable, params):
    weight_qkv, weight_out, weight_up, weight_down, weight_cross, gains, biases = params
    breadth = enc_in.shape[-1]
    residual = self_block(enc_in, usable, weight_qkv[0], weight_out[0], gains[0, 0], biases[0, 0])
    residual = feed_forward(residual, weight_up[0], weight_down[0], gains[0, 1], biases[0, 1])
    states = layer_norm(residual, gains[0, 2], biases[0, 2])
    pairs = low(low_back(matmul(low(low_back(states)), weight_cross[0])))
    current = self_block(dec_in, usable, weight_qkv[1], weight_out[1], gains[1, 0], biases[1, 0])
    normed = low(layer_norm(current, gains[1, 1], biases[1, 1]))
    queries = low(low_back(matmul(normed, weight_cross[1, :, :breadth])))
    blended = attend(queries, pairs[..., :breadth], pairs[..., breadth:], usable)
    current = current + low_back(matmul(blended, weight_cross[1, :, breadth:]))
    current = feed_forward(current, weight_up[1], weight_down[1], gains[1, 2], biases[1, 2])
    return (states, current)

def reference(layer_input, lengths, attn_qkv, attn_out, ffn_in, ffn_out, cross_weight, norm_gain, norm_bias, cotangent):
    sentence_total = MB * SENTS
    group_size = min(4096 // SEQ, sentence_total)
    group_count = sentence_total // group_size
    inputs = layer_input.astype(jnp.float32).reshape(2, group_count, group_size, SEQ, D)
    cotangents = cotangent.astype(jnp.float32).reshape(2, group_count, group_size, SEQ, D)
    sentence_lengths = lengths.astype(jnp.int32).reshape(group_count, group_size)
    params = tuple((weight.astype(jnp.float32) for weight in (attn_qkv, attn_out, ffn_in, ffn_out, cross_weight, norm_gain, norm_bias)))
    zero_grads = tuple((jnp.zeros_like(weight) for weight in params))
    positions = jnp.arange(SEQ, dtype=jnp.int32)

    def one_group(running, portion):
        enc_in, dec_in, enc_cot, dec_cot, group_lengths = portion
        usable = positions[None, :] < group_lengths[:, None]

        def forward_only(enc_value, dec_value, weights):
            return layers_forward(enc_value, dec_value, usable, weights)
        outputs, pullback = jax.vjp(forward_only, enc_in, dec_in, params)
        grad_enc, grad_dec, grad_params = pullback((enc_cot, dec_cot))
        running = tuple((old_term + new_term for old_term, new_term in zip(running, grad_params)))
        emitted = (outputs[0].astype(jnp.bfloat16), outputs[1].astype(jnp.bfloat16), grad_enc.astype(jnp.bfloat16), grad_dec.astype(jnp.bfloat16))
        return (running, emitted)
    grads, emitted = lax.scan(one_group, zero_grads, (inputs[0], inputs[1], cotangents[0], cotangents[1], sentence_lengths))
    states, result, grad_enc, grad_dec = emitted
    layer_output = jnp.stack([states, result]).reshape(2, MB, SENTS, SEQ, D)
    input_grad = jnp.stack([grad_enc, grad_dec]).reshape(2, MB, SENTS, SEQ, D)
    return (layer_output, input_grad, grads[0], grads[1], grads[2], grads[3], grads[4], grads[5], grads[6])
```

```python
import functools
import jax
import jax.numpy as jnp
from jax import lax
from jax.experimental import pallas as pl
from jax.experimental.pallas import tpu as pltpu
from jax.sharding import PartitionSpec as P
MESH = pl.DeviceIdType.MESH

def peers():
    sec = lax.axis_index("section"); dp = lax.axis_index("dp")
    n = lax.axis_size("dp") // 2
    core = lax.rem(dp, 2); chip = dp // 2
    x = lax.rem(chip, 2); z = chip // 2
    pos = jnp.where(x == 0, z, n - 1 - z)
    def at(q):
        q = lax.rem(q + n, n)
        zz = jnp.where(q < n // 2, q, n - 1 - q)
        xx = jnp.where(q < n // 2, 0, 1)
        return (zz * 2 + xx) * 2 + core
    return sec, dp, n, core, pos, at(pos + 1), at(pos - 1), dp + 1 - 2 * core

def barrier(sec, targets):
    bar = pltpu.get_barrier_semaphore()
    for t in targets:
        pl.semaphore_signal(bar, inc=1, device_id=(sec, t), device_id_type=MESH)
    pl.semaphore_wait(bar, len(targets))

def ring_kernel(n, units, g0, g1, ng, o0, o1, o_norm,
                G0, G1, NG, S0, S1, NS, R0, R1, NR, E0, E1, NE,
                ld_sem, sib_s, sib_r, rs_s, rs_r, ag_s, ag_r, sh_s, sh_r, o_sem):
    sec, dp, _, core, pos, nxt, prv, sibling = peers()
    loads = [pltpu.make_async_copy(g0, G0, ld_sem.at[0]), pltpu.make_async_copy(g1, G1, ld_sem.at[1]), pltpu.make_async_copy(ng, NG, ld_sem.at[2])]
    for c in loads: c.start()
    barrier(sec, [nxt, prv, sibling])
    for c in loads: c.wait()
    half = 16 * n
    def rows(d, k, c=core):
        return pl.ds(pl.multiple_of(c * 2 * half + d * half + k * 16, 16), 16)
    def srows(d, k):
        return pl.ds(pl.multiple_of(d * half + k * 16, 16), 16)
    class Stream: pass
    streams = []
    for gi, (G, S, R, E) in enumerate(((G0, S0, R0, E0), (G1, S1, R1, E1))):
        for d in (0, 1):
            st = Stream(); st.i = gi * 2 + d; st.d = d; st.g = gi
            st.own = lambda k, G=G, d=d: G.at[:, rows(d, k), :]
            st.other = lambda k, G=G, d=d: G.at[:, rows(d, k, 1 - core), :]
            st.sib = lambda k, S=S, d=d: S.at[:, srows(d, k), :]
            st.rs = lambda s, R=R, d=d: R.at[d, s]
            st.res = lambda k, E=E, d=d: E.at[:, rows(d, k), :]
            st.res_other = lambda k, E=E, d=d: E.at[:, rows(d, k, 1 - core), :]
            st.to = nxt if d == 0 else prv
            streams.append(st)
    st = Stream(); st.i = 4; st.d = 0; st.g = 2
    st.own = lambda k: NG.at[core, k]; st.other = lambda k: NG.at[1 - core, k]; st.sib = lambda k: NS.at[k]
    st.rs = lambda s: NR.at[s]; st.res = lambda k: NE.at[core, k]; st.res_other = lambda k: NE.at[1 - core, k]; st.to = nxt
    streams.append(st)
    def chunk(st, s):
        return lax.rem(pos - s + 2 * n, n) if st.d == 0 else lax.rem(pos + s, n)
    def remote(src, dst, ss, rs, to):
        return pltpu.make_async_remote_copy(src_ref=src, dst_ref=dst, send_sem=ss, recv_sem=rs, device_id=(sec, to), device_id_type=MESH)
    def sib_copy(st, k): return remote(st.other(k), st.sib(k), sib_s.at[st.i, k], sib_r.at[st.i, k], sibling)
    def rs_copy(st, s): return remote(st.own(chunk(st, s)), st.rs(s), rs_s.at[st.i, s], rs_r.at[st.i, s], st.to)
    def ag_copy(st, t):
        k = chunk(st, t + n - 1)
        return remote(st.res(k), st.res(k), ag_s.at[st.i, t], ag_r.at[st.i, t], st.to)
    def sh_copy(st, t):
        k = chunk(st, t + n - 1)
        return remote(st.res(k), st.res(k), sh_s.at[st.i, t], sh_r.at[st.i, t], sibling)
    def loop(a, b, f):
        lax.fori_loop(a, b, lambda i, c: (f(i), c)[1], 0)
    def f32(r): return r[...].astype(jnp.float32)
    def share(s):
        for st in streams: sib_copy(st, chunk(st, s)).start()
    loop(0, n, share)
    def first():
        for st in streams:
            k = chunk(st, 0)
            sib_copy(st, k).wait_recv()
            own = st.own(k)
            own[...] = (f32(own) + f32(st.sib(k))).astype(own.dtype)
            rs_copy(st, 0).start()
    first()
    def middle(s):
        for st in streams:
            k = chunk(st, s)
            sib_copy(st, k).wait_recv()
            rs_copy(st, s - 1).wait_recv()
            own = st.own(k)
            own[...] = (f32(own) + f32(st.sib(k)) + f32(st.rs(s - 1))).astype(own.dtype)
            rs_copy(st, s).start()
    loop(1, n - 1, middle)
    for st in streams:
        k = chunk(st, n - 1)
        sib_copy(st, k).wait_recv()
        rs_copy(st, n - 2).wait_recv()
        own = st.own(k); res = st.res(k)
        res[...] = (f32(own) + f32(st.sib(k)) + f32(st.rs(n - 2))).astype(own.dtype)
        ag_copy(st, 0).start()
        sh_copy(st, 0).start()
    def out_copy(st, k, c, slot):
        src = st.res(k) if c == 0 else st.res_other(k)
        if st.g == 2:
            return pltpu.make_async_copy(src, o_norm.at[core if c == 0 else 1 - core, k], o_sem.at[st.i, slot])
        row = rows(st.d, k, core if c == 0 else 1 - core)
        return pltpu.make_async_copy(src, (o0, o1)[st.g].at[:, row, :], o_sem.at[st.i, slot])
    def emit(st, t):
        k = chunk(st, t + n - 1)
        sh_copy(st, t).wait_recv()
        out_copy(st, k, 0, 2 * t).start()
        out_copy(st, k, 1, 2 * t + 1).start()
    def gather(t):
        for st in streams:
            ag_copy(st, t).wait_recv()
            @pl.when(t < n - 2)
            def _(): ag_copy(st, t + 1).start()
            sh_copy(st, t + 1).start()
        for st in streams:
            emit(st, t)
    loop(0, n - 1, gather)
    for st in streams:
        emit(st, n - 1)
    def drain(s):
        for st in streams:
            sib_copy(st, s).wait_send(); sh_copy(st, s).wait_send()
            out_copy(st, chunk(st, s + n - 1), 0, 2 * s).wait(); out_copy(st, chunk(st, s + n - 1), 1, 2 * s + 1).wait()
            @pl.when(s < n - 1)
            def _():
                rs_copy(st, s).wait_send(); ag_copy(st, s).wait_send()
    loop(0, n, drain)

def all_reduce(g0, g1, ng, n):
    u0, u1 = g0.shape[0], g1.shape[0]
    bf, f4 = jnp.bfloat16, jnp.float32
    any_ = pl.BlockSpec(memory_space=pl.ANY)
    V = pltpu.VMEM; D = pltpu.SemaphoreType.DMA
    return pl.pallas_call(
        functools.partial(ring_kernel, n, (u0, u1)),
        out_shape=[jax.ShapeDtypeStruct(a.shape, a.dtype) for a in (g0, g1, ng)], in_specs=[any_] * 3, out_specs=[any_] * 3,
        scratch_shapes=[V(g0.shape, bf), V(g1.shape, bf), V(ng.shape, f4),
            V((u0, 32 * n, 512), bf), V((u1, 32 * n, 512), bf), V((n, 8, 128), f4),
            V((2, n - 1, u0, 16, 512), bf), V((2, n - 1, u1, 16, 512), bf), V((n - 1, 8, 128), f4),
            V(g0.shape, bf), V(g1.shape, bf), V(ng.shape, f4),
            D((3,)), D((5, n)), D((5, n)), D((5, n)), D((5, n)), D((5, n)), D((5, n)), D((5, n)), D((5, n)), D((5, 2 * n))],
        compiler_params=pltpu.CompilerParams(collective_id=0, has_side_effects=True, vmem_limit_bytes=60 * 2**20),
        name="ring",
    )(g0, g1, ng)


def pack_blocks(blocks, n):
    flat = jnp.concatenate(blocks, axis=0).astype(jnp.bfloat16)
    units = -(-flat.shape[0] // (64 * n))
    flat = jnp.pad(flat, ((0, units * 64 * n - flat.shape[0]), (0, 0)))
    return flat.reshape(units, 64 * n, 512)

def columns(weight):
    return [weight[:, 512 * j:512 * (j + 1)] for j in range(weight.shape[1] // 512)]

def pack_norm(gain, bias, n):
    both = jnp.stack([gain, bias]).reshape(2, 3, 4, 128).transpose(0, 2, 1, 3)
    return jnp.pad(both, ((0, 0), (0, n - 4), (0, 5), (0, 0)))

def sum_gradients(grads, n):
    g_qkv, g_out, g_up, g_down, g_cross, g_gain, g_bias = grads[:7]
    e0, e1, en = all_reduce(pack_blocks(columns(g_up) + [g_down], n), pack_blocks(columns(g_qkv) + [g_out] + columns(g_cross), n), pack_norm(g_gain, g_bias, n), n)
    e0 = e0.reshape(-1, 512)[:8 * 512].reshape(8, 512, 512)
    e1 = e1.reshape(-1, 512)[:6 * 512].reshape(6, 512, 512)
    def wide(blocks):
        return blocks.transpose(1, 0, 2).reshape(512, -1).astype(jnp.float32)
    en = en[:, :4, :3].transpose(0, 2, 1, 3).reshape(2, 3, 512)
    return (wide(e1[:3]), e1[3].astype(jnp.float32), wide(e0[:4]), e0[4:].reshape(2048, 512).astype(jnp.float32), wide(e1[4:]), en[0], en[1])

HEADS = 8


def shifted(value, axis, steps):
    count = lax.axis_size(axis)
    leading, last = (max(0, -steps), min(count, count - steps))
    return lax.ppermute(value, axis, [(source, source + steps) for source in range(leading, last)])


def product(left_side, right_side):
    return jnp.dot(left_side, right_side, preferred_element_type=jnp.float32)


def product_tn(left_side, right_side):
    return lax.dot_general(
        left_side, right_side, (((0,), (0,)), ((), ())), preferred_element_type=jnp.float32
    )


def product_nt(left_side, right_side):
    return lax.dot_general(
        left_side, right_side, (((1,), (1,)), ((), ())), preferred_element_type=jnp.float32
    )


def gelu_exact(pre_act):
    return jax.nn.gelu(pre_act, approximate=False)


def layer_norm(source, norm_scale, norm_shift):
    center = source - jnp.mean(source, axis=-1, keepdims=True)
    spread = jnp.mean(center * center, axis=-1, keepdims=True)
    return center * lax.rsqrt(spread + 1e-05) * norm_scale + norm_shift


def split_heads(matrix):
    return matrix.reshape(matrix.shape[:-1] + (HEADS, matrix.shape[-1] // HEADS))


def masked_scores(queries, key_rows, usable):
    head_size = queries.shape[-1] // HEADS
    scores = jnp.einsum(
        "qhd,khd->hqk",
        split_heads(queries),
        split_heads(key_rows),
        preferred_element_type=jnp.float32,
    ) * head_size ** (-0.5)
    return jnp.where(usable[None, None, :], scores, -1e30)


def attend(queries, key_rows, value_rows, usable):
    scores = masked_scores(queries, key_rows, usable)
    highest = jnp.max(scores, axis=-1, keepdims=True)
    weights = jnp.exp(scores - highest)
    denominator = jnp.sum(weights, axis=-1, keepdims=True)
    chances = (weights / denominator).astype(jnp.bfloat16)
    blended = jnp.einsum(
        "hqk,khd->qhd", chances, split_heads(value_rows), preferred_element_type=jnp.float32
    )
    return (blended.reshape(queries.shape).astype(jnp.bfloat16), highest + jnp.log(denominator))


def attend_back(grad_blended, queries, key_rows, value_rows, usable, log_total):
    factor = (queries.shape[-1] // HEADS) ** (-0.5)
    scores = masked_scores(queries, key_rows, usable)
    chances = jnp.exp(scores - log_total)
    heads_grad = split_heads(grad_blended)
    grad_values = jnp.einsum(
        "hqk,qhd->khd", chances.astype(jnp.bfloat16), heads_grad, preferred_element_type=jnp.float32
    )
    grad_chances = jnp.einsum(
        "qhd,khd->hqk", heads_grad, split_heads(value_rows), preferred_element_type=jnp.float32
    )
    grad_scores = (
        chances * (grad_chances - jnp.sum(chances * grad_chances, axis=-1, keepdims=True))
    ).astype(jnp.bfloat16)
    grad_queries = (
        jnp.einsum(
            "hqk,khd->qhd", grad_scores, split_heads(key_rows), preferred_element_type=jnp.float32
        )
        * factor
    )
    grad_keys = (
        jnp.einsum(
            "hqk,qhd->khd", grad_scores, split_heads(queries), preferred_element_type=jnp.float32
        )
        * factor
    )
    row_shape = queries.shape
    return (
        grad_queries.reshape(row_shape),
        grad_keys.reshape(row_shape),
        grad_values.reshape(row_shape),
    )


def self_forward(inputs, usable, weight_qkv, weight_out, norm_scale, norm_shift):
    breadth = inputs.shape[-1]
    normed = layer_norm(inputs, norm_scale, norm_shift).astype(jnp.bfloat16)
    packed = product(normed, weight_qkv).astype(jnp.bfloat16)
    blended, log_total = attend(
        packed[:, :breadth], packed[:, breadth : 2 * breadth], packed[:, 2 * breadth :], usable
    )
    residual = inputs + product(blended, weight_out)
    return (residual, (normed, packed, blended, log_total))


def self_backward(upstream, inputs, usable, stored, weight_qkv, weight_out, norm_scale, norm_shift):
    normed, packed, blended, log_total = stored
    breadth = inputs.shape[-1]
    low_grad = upstream.astype(jnp.bfloat16)
    out_term = product_tn(blended, low_grad)
    grad_blended = product_nt(low_grad, weight_out).astype(jnp.bfloat16)
    grad_queries, grad_keys, grad_values = attend_back(
        grad_blended,
        packed[:, :breadth],
        packed[:, breadth : 2 * breadth],
        packed[:, 2 * breadth :],
        usable,
        log_total,
    )
    grad_packed = jnp.concatenate([grad_queries, grad_keys, grad_values], axis=1).astype(
        jnp.bfloat16
    )
    qkv_term = product_tn(normed, grad_packed)
    _, pullback = jax.vjp(layer_norm, inputs, norm_scale, norm_shift)
    grad_inner, gain_term, bias_term = pullback(product_nt(grad_packed, weight_qkv))
    return (upstream + grad_inner, qkv_term, out_term, gain_term, bias_term)


def ffn_forward(residual, weight_up, weight_down, norm_scale, norm_shift):
    normed = layer_norm(residual, norm_scale, norm_shift).astype(jnp.bfloat16)
    pre_act = product(normed, weight_up)
    hidden = gelu_exact(pre_act).astype(jnp.bfloat16)
    return (residual + product(hidden, weight_down), (normed, pre_act, hidden))


def ffn_backward(upstream, residual, stored, weight_up, weight_down, norm_scale, norm_shift):
    normed, pre_act, hidden = stored
    low_grad = upstream.astype(jnp.bfloat16)
    down_term = product_tn(hidden, low_grad)
    _, gelu_pullback = jax.vjp(gelu_exact, pre_act)
    grad_pre = gelu_pullback(product_nt(low_grad, weight_down))[0].astype(jnp.bfloat16)
    up_term = product_tn(normed, grad_pre)
    _, pullback = jax.vjp(layer_norm, residual, norm_scale, norm_shift)
    grad_inner, gain_term, bias_term = pullback(product_nt(grad_pre, weight_up))
    return (upstream + grad_inner, up_term, down_term, gain_term, bias_term)


def send_ahead(payload):
    return shifted(payload, "section", 1)


def send_behind(payload):
    return shifted(payload, "section", -1)


def local(
    layer_input,
    lengths,
    attn_qkv,
    attn_out,
    ffn_in,
    ffn_out,
    cross_weight,
    norm_gain,
    norm_bias,
    cotangent,
):
    is_encoder = lax.axis_index("section") == 0
    inputs = layer_input[0, :, 0].astype(jnp.float32)
    cotangents = cotangent[0, :, 0].astype(jnp.float32)
    micro_count, length, breadth = inputs.shape
    positions = jnp.arange(length, dtype=jnp.int32)
    key_masks = positions[None, :] < lengths[:, 0][:, None]
    w_qkv = attn_qkv[0]
    w_out = attn_out[0]
    w_up = ffn_in[0]
    w_down = ffn_out[0]
    w_cross = cross_weight[0]
    gains = norm_gain[0]
    biases = norm_bias[0]
    pair_width = 2 * breadth

    def encoder_forward(index):
        residual, self_kept = self_forward(
            inputs[index], key_masks[index], w_qkv, w_out, gains[0], biases[0]
        )
        after, ffn_kept = ffn_forward(residual, w_up, w_down, gains[1], biases[1])
        states = layer_norm(after, gains[2], biases[2]).astype(jnp.bfloat16)
        outgoing = product(states, w_cross).astype(jnp.bfloat16)
        return (outgoing, states, (residual, after, states, self_kept, ffn_kept))

    def encoder_top(index, stored, returned, grads):
        g_qkv, g_out, g_up, g_down, g_cross, g_gain, g_bias, g_pair = grads
        residual, after, states, self_kept, ffn_kept = stored
        g_cross = g_cross + product_tn(states, returned)
        from_cross = lax.optimization_barrier(
            product_nt(returned, w_cross).astype(jnp.bfloat16)
        ).astype(jnp.float32)
        _, pullback = jax.vjp(layer_norm, after, gains[2], biases[2])
        grad_after, gain_last, bias_last = pullback(cotangents[index] + from_cross)
        grad_residual, up_term, down_term, gain_ffn, bias_ffn = ffn_backward(
            grad_after, residual, ffn_kept, w_up, w_down, gains[1], biases[1]
        )
        g_gain = g_gain.at[1].add(gain_ffn).at[2].add(gain_last)
        g_bias = g_bias.at[1].add(bias_ffn).at[2].add(bias_last)
        return (
            grad_residual,
            (g_qkv, g_out, g_up + up_term, g_down + down_term, g_cross, g_gain, g_bias, g_pair),
        )

    def encoder_bottom(index, stored, grad_residual, in_grads, grads):
        g_qkv, g_out, g_up, g_down, g_cross, g_gain, g_bias, g_pair = grads
        residual, after, states, self_kept, ffn_kept = stored
        grad_input, qkv_term, out_term, gain_self, bias_self = self_backward(
            grad_residual,
            inputs[index],
            key_masks[index],
            self_kept,
            w_qkv,
            w_out,
            gains[0],
            biases[0],
        )
        in_grads = in_grads.at[index].set(grad_input.astype(jnp.bfloat16))
        grads = (
            g_qkv + qkv_term,
            g_out + out_term,
            g_up,
            g_down,
            g_cross,
            g_gain.at[0].add(gain_self),
            g_bias.at[0].add(bias_self),
            g_pair,
        )
        return (in_grads, grads)

    def decoder_step(index, incoming, grads):
        g_qkv, g_out, g_up, g_down, g_cross, g_gain, g_bias, g_pair = grads
        usable = key_masks[index]
        residual, self_kept = self_forward(inputs[index], usable, w_qkv, w_out, gains[0], biases[0])
        normed = layer_norm(residual, gains[1], biases[1]).astype(jnp.bfloat16)
        queries = product(normed, w_cross[:, :breadth]).astype(jnp.bfloat16)
        blended, log_total = attend(queries, incoming[:, :breadth], incoming[:, breadth:], usable)
        middle = residual + product(blended, w_cross[:, breadth:])
        after, ffn_kept = ffn_forward(middle, w_up, w_down, gains[2], biases[2])
        grad_middle, up_term, down_term, gain_ffn, bias_ffn = ffn_backward(
            cotangents[index], middle, ffn_kept, w_up, w_down, gains[2], biases[2]
        )
        low_grad = grad_middle.astype(jnp.bfloat16)
        cross_out_term = product_tn(blended, low_grad)
        grad_blended = product_nt(low_grad, w_cross[:, breadth:]).astype(jnp.bfloat16)
        grad_queries, grad_keys, grad_values = attend_back(
            grad_blended, queries, incoming[:, :breadth], incoming[:, breadth:], usable, log_total
        )
        low_queries = grad_queries.astype(jnp.bfloat16)
        grad_pairs = jnp.concatenate([grad_keys, grad_values], axis=1).astype(jnp.bfloat16)
        cross_in_term = product_tn(normed, low_queries)
        _, pullback = jax.vjp(layer_norm, residual, gains[1], biases[1])
        grad_inner, gain_cross, bias_cross = pullback(product_nt(low_queries, w_cross[:, :breadth]))
        grad_input, qkv_term, out_term, gain_self, bias_self = self_backward(
            grad_middle + grad_inner,
            inputs[index],
            usable,
            self_kept,
            w_qkv,
            w_out,
            gains[0],
            biases[0],
        )
        grads = (
            g_qkv + qkv_term,
            g_out + out_term,
            g_up + up_term,
            g_down + down_term,
            g_cross + jnp.concatenate([cross_in_term, cross_out_term], axis=1),
            g_gain + jnp.stack([gain_self, gain_cross, gain_ffn]),
            g_bias + jnp.stack([bias_self, bias_cross, bias_ffn]),
            g_pair,
        )
        return (after.astype(jnp.bfloat16), grad_input.astype(jnp.bfloat16), grads, grad_pairs)

    blank_send = jnp.zeros((length, pair_width), jnp.bfloat16)
    blank_store = jax.tree.map(jnp.zeros_like, encoder_forward(0)[2])
    results = jnp.zeros((micro_count, length, breadth), jnp.bfloat16)
    in_grads = jnp.zeros((micro_count, length, breadth), jnp.bfloat16)
    grads = (
        jnp.zeros(w_qkv.shape, jnp.float32),
        jnp.zeros(w_out.shape, jnp.float32),
        jnp.zeros(w_up.shape, jnp.float32),
        jnp.zeros(w_down.shape, jnp.float32),
        jnp.zeros(w_cross.shape, jnp.float32),
        jnp.zeros(gains.shape, jnp.float32),
        jnp.zeros(biases.shape, jnp.float32),
        jnp.zeros(w_cross.shape, jnp.float32),
    )
    arrived_ahead = blank_send
    arrived_back = blank_send
    stored_list = []

    def make_ticks(tick_now):

        def encoder_tick(operands):
            results_now, in_grads_now, grads_now, ahead_now, back_now, stored_old = operands
            outgoing = blank_send
            stored_new = blank_store
            if tick_now < micro_count:
                outgoing, states, stored_new = encoder_forward(tick_now)
                results_now = results_now.at[tick_now].set(states)
            if tick_now >= 2:
                grad_residual, grads_now = encoder_top(
                    tick_now - 2, stored_old, back_now, grads_now
                )
                in_grads_now, grads_now = encoder_bottom(
                    tick_now - 2, stored_old, grad_residual, in_grads_now, grads_now
                )
            return (results_now, in_grads_now, grads_now, outgoing, blank_send, stored_new)

        def decoder_tick(operands):
            results_now, in_grads_now, grads_now, ahead_now, back_now, stored_old = operands
            outgoing = blank_send
            if 1 <= tick_now <= micro_count:
                result, grad_input, grads_now, outgoing = decoder_step(
                    tick_now - 1, ahead_now, grads_now
                )
                results_now = results_now.at[tick_now - 1].set(result)
                in_grads_now = in_grads_now.at[tick_now - 1].set(grad_input)
            return (results_now, in_grads_now, grads_now, blank_send, outgoing, blank_store)

        return (encoder_tick, decoder_tick)

    for tick_now in range(micro_count + 1):
        encoder_tick, decoder_tick = make_ticks(tick_now)
        stored_old = stored_list[tick_now - 2] if tick_now >= 2 else blank_store
        operands = (results, in_grads, grads, arrived_ahead, arrived_back, stored_old)
        results, in_grads, grads, ahead_value, behind_value, stored_new = lax.cond(
            is_encoder, encoder_tick, decoder_tick, operands
        )
        if tick_now < micro_count:
            stored_list.append(stored_new)
            arrived_ahead = send_ahead(ahead_value)
        if tick_now >= 1:
            arrived_back = send_behind(behind_value)
    last_index = micro_count - 1
    last_store = stored_list[last_index]

    def full_encoder(operands):
        in_grads_now, grads_now, back_now = operands
        residual_grad, grads_now = encoder_top(last_index, last_store, back_now, grads_now)
        return encoder_bottom(last_index, last_store, residual_grad, in_grads_now, grads_now)

    def full_decoder(operands):
        in_grads_now, grads_now, back_now = operands
        return (in_grads_now, grads_now)

    in_grads, grads = lax.cond(
        is_encoder, full_encoder, full_decoder, (in_grads, grads, arrived_back)
    )
    sum_qkv, sum_out, sum_up, sum_down, sum_cross, sum_gain, sum_bias = sum_gradients(grads, lax.axis_size("dp") // 2)
    return (
        results[None, :, None],
        in_grads[None, :, None],
        sum_qkv[None],
        sum_out[None],
        sum_up[None],
        sum_down[None],
        sum_cross[None],
        sum_gain[None],
        sum_bias[None],
    )


def solution(mesh):
    placed = (
        P("section", None, "dp", None, None),
        P(None, "dp"),
        P("section", None, None),
        P("section", None, None),
        P("section", None, None),
        P("section", None, None),
        P("section", None, None),
        P("section", None, None),
        P("section", None, None),
        P("section", None, "dp", None, None),
    )
    return jax.shard_map(
        local,
        mesh=mesh,
        in_specs=placed,
        out_specs=(
            P("section", None, "dp", None, None),
            P("section", None, "dp", None, None),
            P("section", None, None),
            P("section", None, None),
            P("section", None, None),
            P("section", None, None),
            P("section", None, None),
            P("section", None, None),
            P("section", None, None),
        ),
        check_vma=False,
    )
```

```python
import functools
import jax
import jax.numpy as jnp
from jax import lax
from jax.experimental import pallas as pl
from jax.experimental.pallas import tpu as pltpu
from jax.sharding import PartitionSpec as P
MESH = pl.DeviceIdType.MESH

def peers():
    sec = lax.axis_index("section"); dp = lax.axis_index("dp")
    n = lax.axis_size("dp") // 2
    core = lax.rem(dp, 2); chip = dp // 2
    x = lax.rem(chip, 2); z = chip // 2
    pos = jnp.where(x == 0, z, n - 1 - z)
    def at(q):
        q = lax.rem(q + n, n)
        zz = jnp.where(q < n // 2, q, n - 1 - q)
        xx = jnp.where(q < n // 2, 0, 1)
        return (zz * 2 + xx) * 2 + core
    return sec, dp, n, core, pos, at(pos + 1), at(pos - 1), dp + 1 - 2 * core

def barrier(sec, targets):
    bar = pltpu.get_barrier_semaphore()
    for t in targets:
        pl.semaphore_signal(bar, inc=1, device_id=(sec, t), device_id_type=MESH)
    pl.semaphore_wait(bar, len(targets))

def ring_kernel(n, units, g0, g1, ng, o0, o1, o_norm,
                G0, G1, NG, S0, S1, NS, R0, R1, NR, E0, E1, NE,
                ld_sem, sib_s, sib_r, rs_s, rs_r, ag_s, ag_r, sh_s, sh_r, o_sem):
    sec, dp, _, core, pos, nxt, prv, sibling = peers()
    loads = [pltpu.make_async_copy(g0, G0, ld_sem.at[0]), pltpu.make_async_copy(g1, G1, ld_sem.at[1]), pltpu.make_async_copy(ng, NG, ld_sem.at[2])]
    for c in loads: c.start()
    barrier(sec, [nxt, prv, sibling])
    for c in loads: c.wait()
    half = 16 * n
    def rows(d, k, c=core):
        return pl.ds(pl.multiple_of(c * 2 * half + d * half + k * 16, 16), 16)
    def srows(d, k):
        return pl.ds(pl.multiple_of(d * half + k * 16, 16), 16)
    class Stream: pass
    streams = []
    for gi, (G, S, R, E) in enumerate(((G0, S0, R0, E0), (G1, S1, R1, E1))):
        for d in (0, 1):
            st = Stream(); st.i = gi * 2 + d; st.d = d; st.g = gi
            st.own = lambda k, G=G, d=d: G.at[:, rows(d, k), :]
            st.other = lambda k, G=G, d=d: G.at[:, rows(d, k, 1 - core), :]
            st.sib = lambda k, S=S, d=d: S.at[:, srows(d, k), :]
            st.rs = lambda s, R=R, d=d: R.at[d, s]
            st.res = lambda k, E=E, d=d: E.at[:, rows(d, k), :]
            st.res_other = lambda k, E=E, d=d: E.at[:, rows(d, k, 1 - core), :]
            st.to = nxt if d == 0 else prv
            streams.append(st)
    st = Stream(); st.i = 4; st.d = 0; st.g = 2
    st.own = lambda k: NG.at[core, k]; st.other = lambda k: NG.at[1 - core, k]; st.sib = lambda k: NS.at[k]
    st.rs = lambda s: NR.at[s]; st.res = lambda k: NE.at[core, k]; st.res_other = lambda k: NE.at[1 - core, k]; st.to = nxt
    streams.append(st)
    def chunk(st, s):
        return lax.rem(pos - s + 2 * n, n) if st.d == 0 else lax.rem(pos + s, n)
    def remote(src, dst, ss, rs, to):
        return pltpu.make_async_remote_copy(src_ref=src, dst_ref=dst, send_sem=ss, recv_sem=rs, device_id=(sec, to), device_id_type=MESH)
    def sib_copy(st, k): return remote(st.other(k), st.sib(k), sib_s.at[st.i, k], sib_r.at[st.i, k], sibling)
    def rs_copy(st, s): return remote(st.own(chunk(st, s)), st.rs(s), rs_s.at[st.i, s], rs_r.at[st.i, s], st.to)
    def ag_copy(st, t):
        k = chunk(st, t + n - 1)
        return remote(st.res(k), st.res(k), ag_s.at[st.i, t], ag_r.at[st.i, t], st.to)
    def sh_copy(st, t):
        k = chunk(st, t + n - 1)
        return remote(st.res(k), st.res(k), sh_s.at[st.i, t], sh_r.at[st.i, t], sibling)
    def loop(a, b, f):
        lax.fori_loop(a, b, lambda i, c: (f(i), c)[1], 0)
    def f32(r): return r[...].astype(jnp.float32)
    def share(s):
        for st in streams: sib_copy(st, chunk(st, s)).start()
    loop(0, n, share)
    def first():
        for st in streams:
            k = chunk(st, 0)
            sib_copy(st, k).wait_recv()
            own = st.own(k)
            own[...] = (f32(own) + f32(st.sib(k))).astype(own.dtype)
            rs_copy(st, 0).start()
    first()
    def middle(s):
        for st in streams:
            k = chunk(st, s)
            sib_copy(st, k).wait_recv()
            rs_copy(st, s - 1).wait_recv()
            own = st.own(k)
            own[...] = (f32(own) + f32(st.sib(k)) + f32(st.rs(s - 1))).astype(own.dtype)
            rs_copy(st, s).start()
    loop(1, n - 1, middle)
    for st in streams:
        k = chunk(st, n - 1)
        sib_copy(st, k).wait_recv()
        rs_copy(st, n - 2).wait_recv()
        own = st.own(k); res = st.res(k)
        res[...] = (f32(own) + f32(st.sib(k)) + f32(st.rs(n - 2))).astype(own.dtype)
        ag_copy(st, 0).start()
        sh_copy(st, 0).start()
    def out_copy(st, k, c, slot):
        src = st.res(k) if c == 0 else st.res_other(k)
        if st.g == 2:
            return pltpu.make_async_copy(src, o_norm.at[core if c == 0 else 1 - core, k], o_sem.at[st.i, slot])
        row = rows(st.d, k, core if c == 0 else 1 - core)
        return pltpu.make_async_copy(src, (o0, o1)[st.g].at[:, row, :], o_sem.at[st.i, slot])
    def emit(st, t):
        k = chunk(st, t + n - 1)
        sh_copy(st, t).wait_recv()
        out_copy(st, k, 0, 2 * t).start()
        out_copy(st, k, 1, 2 * t + 1).start()
    def gather(t):
        for st in streams:
            ag_copy(st, t).wait_recv()
            @pl.when(t < n - 2)
            def _(): ag_copy(st, t + 1).start()
            sh_copy(st, t + 1).start()
        for st in streams:
            emit(st, t)
    loop(0, n - 1, gather)
    for st in streams:
        emit(st, n - 1)
    def drain(s):
        for st in streams:
            sib_copy(st, s).wait_send(); sh_copy(st, s).wait_send()
            out_copy(st, chunk(st, s + n - 1), 0, 2 * s).wait(); out_copy(st, chunk(st, s + n - 1), 1, 2 * s + 1).wait()
            @pl.when(s < n - 1)
            def _():
                rs_copy(st, s).wait_send(); ag_copy(st, s).wait_send()
    loop(0, n, drain)

def all_reduce(g0, g1, ng, n):
    u0, u1 = g0.shape[0], g1.shape[0]
    bf, f4 = jnp.bfloat16, jnp.float32
    any_ = pl.BlockSpec(memory_space=pl.ANY)
    V = pltpu.VMEM; D = pltpu.SemaphoreType.DMA
    return pl.pallas_call(
        functools.partial(ring_kernel, n, (u0, u1)),
        out_shape=[jax.ShapeDtypeStruct(a.shape, a.dtype) for a in (g0, g1, ng)], in_specs=[any_] * 3, out_specs=[any_] * 3,
        scratch_shapes=[V(g0.shape, bf), V(g1.shape, bf), V(ng.shape, f4),
            V((u0, 32 * n, 512), bf), V((u1, 32 * n, 512), bf), V((n, 8, 128), f4),
            V((2, n - 1, u0, 16, 512), bf), V((2, n - 1, u1, 16, 512), bf), V((n - 1, 8, 128), f4),
            V(g0.shape, bf), V(g1.shape, bf), V(ng.shape, f4),
            D((3,)), D((5, n)), D((5, n)), D((5, n)), D((5, n)), D((5, n)), D((5, n)), D((5, n)), D((5, n)), D((5, 2 * n))],
        compiler_params=pltpu.CompilerParams(collective_id=0, has_side_effects=True, vmem_limit_bytes=60 * 2**20),
        name="ring",
    )(g0, g1, ng)


def transpose(value):
    return value.T


def dot(a, b):
    return jnp.dot(a, b, preferred_element_type=jnp.float32)


def dot_nt(a, b):
    return lax.dot_general(a, b, (((1,), (1,)), ((), ())), preferred_element_type=jnp.float32)


def gelu_parts(u):
    size = jnp.abs(u)
    t = 1.0 / (1.0 + (0.3275911 * 0.5 ** 0.5) * size)
    bell = jnp.exp(-0.5 * u * u)
    poly = t * (0.127414796 + t * (-0.142248368 + t * (0.7107068705 + t * (-0.7265760135 + t * 0.5307027145))))
    tail = poly * bell
    cdf = jnp.where(u >= 0, 1.0 - tail, tail)
    return u * cdf, cdf + u * bell * 0.3989422804014327


def normalize(value):
    center = value - jnp.mean(value, axis=-1, keepdims=True)
    spread = jnp.mean(center * center, axis=-1, keepdims=True)
    scale = lax.rsqrt(spread + 1e-05)
    return center * scale, scale


def norm_back(grad, unit, scale, gain):
    inner = grad * gain
    mean = jnp.mean(inner, axis=-1, keepdims=True)
    along = jnp.mean(inner * unit, axis=-1, keepdims=True)
    return scale * (inner - mean - unit * along)


def loop(start, stop, body):
    lax.fori_loop(start, stop, lambda i, carry: (body(i), carry)[1], 0)


ROWS = 64


def compute_kernel(n, lens, x, ct, wq, wo, w1, w2, wc, gn, bs, g0, g1, ng, out, gin,
                   X, CT, WQ, WO, W1, W2, WC, WC0, GN, BS,
                   H1, QKV, PT, O, RR, ST, HQ, CQ, KV, PT2, O2, N2, A, GP, AFT, D, LOW, LOWC, LOWS, DO, DQKV, DCQ, DKV, DST,
                   TT, G0, G1, NG, PG, PB,
                   ld, wc_s, wc_r, sh_s, sh_r, st_s, st_r, ds_s, ds_r, dk_s, dk_r, o_sem):
    sec, dp = lax.axis_index("section"), lax.axis_index("dp")
    core = lax.rem(dp, 2)
    sibling = dp + 1 - 2 * core
    other = 1 - sec
    enc = sec == 0
    dec = sec == 1
    bf = jnp.bfloat16
    length = X.shape[1]
    width = X.shape[2]
    heads = width // 64
    pairs = heads // 2
    loads = {}
    for i, (name, src, dst) in enumerate((("x", x, X), ("gn", gn, GN), ("bs", bs, BS), ("wq", wq, WQ), ("wo", wo, WO), ("w1", w1, W1), ("w2", w2, W2),
                                          ("ct", ct, CT), ("wc", wc, WC))):
        loads[name] = pltpu.make_async_copy(src, dst, ld.at[i])
        loads[name].start()
    bar = pltpu.get_barrier_semaphore()
    for target in ((other, dp), (sec, sibling)):
        pl.semaphore_signal(bar, inc=1, device_id=target, device_id_type=MESH)
    pl.semaphore_wait(bar, 2)

    def remote(src, dst, ss, rs, to):
        return pltpu.make_async_remote_copy(src_ref=src, dst_ref=dst, send_sem=ss, recv_sem=rs, device_id=to, device_id_type=MESH)

    half = pl.ds(pl.multiple_of(core * (width // 2), 16), width // 2)
    other_half = pl.ds(pl.multiple_of((1 - core) * (width // 2), 16), width // 2)
    wc_copy = remote(wc.at[half], WC0.at[half], wc_s, wc_r, (other, dp))
    wc_share = remote(WC0.at[half], WC0.at[half], sh_s, sh_r, (sec, sibling))

    def mrows(m):
        return pl.ds(pl.multiple_of(m * length, length), length)

    def st_copy(m): return remote(ST.at[mrows(m)], ST.at[mrows(m)], st_s.at[m], st_r.at[m], (other, dp))
    def ds_copy(m): return remote(DST.at[mrows(m)], DST.at[mrows(m)], ds_s.at[m], ds_r.at[m], (other, dp))
    def dk_copy(m): return remote(DKV.at[mrows(m)], DKV.at[mrows(m)], dk_s.at[m], dk_r.at[m], (other, dp))

    @pl.when(enc)
    def _(): wc_copy.start()

    PG[...] = jnp.zeros_like(PG)
    PB[...] = jnp.zeros_like(PB)

    def by_rows(m, body):
        loop(0, length // ROWS, lambda i: body(pl.ds(pl.multiple_of(m * length + i * ROWS, ROWS), ROWS), pl.ds(pl.multiple_of(i * ROWS, ROWS), ROWS)))

    def gain_at(i): return GN[pl.ds(i, 1), :]
    def bias_at(i): return BS[pl.ds(i, 1), :]

    def add_norm_grads(i, grad, unit):
        at = pl.ds(i, 1)
        PG[at, :] = PG[at, :] + jnp.sum(grad * unit, axis=0, keepdims=True)
        PB[at, :] = PB[at, :] + jnp.sum(grad, axis=0, keepdims=True)

    lane_low = lax.broadcasted_iota(jnp.int32, (length, 128), 1) < 64
    lane_row = lax.broadcasted_iota(jnp.int32, (1, 128), 1) < 64
    head_masks = (jnp.where(lane_row, 1.0, 0.0).astype(bf), jnp.where(lane_row, 0.0, 1.0).astype(bf))

    def attention(m, q, q0, k, k0, v, v0, P, out_ref):
        rows = mrows(m)
        usable = lax.broadcasted_iota(jnp.int32, (length, length), 0) < lens[m]
        def pair(j):
            def cols(c0): return pl.ds(pl.multiple_of(c0 + j * 128, 128), 128)
            q2, k2, vt = q[rows, cols(q0)], k[rows, cols(k0)], transpose(v[rows, cols(v0)])
            parts = []
            for e in (0, 1):
                s = dot_nt(k2, q2 * head_masks[e]) * 0.125
                s = jnp.where(usable, s, -1e30)
                w = jnp.exp(s - jnp.max(s, axis=0, keepdims=True))
                p = (w * (1.0 / jnp.sum(w, axis=0, keepdims=True))).astype(bf)
                P[m * heads + 2 * j + e] = p
                parts.append(dot(vt[64 * e:64 * (e + 1)], p))
            out_ref[rows, cols(0)] = transpose(jnp.concatenate(parts, axis=0)).astype(bf)
        loop(0, pairs, pair)

    def attention_back(m, do, q, q0, k, k0, v, v0, P, dq, dq0, dk, dk0, dv, dv0):
        rows = mrows(m)
        def pair(j):
            def cols(c0): return pl.ds(pl.multiple_of(c0 + j * 128, 128), 128)
            q2, k2, v2, do2 = q[rows, cols(q0)], k[rows, cols(k0)], v[rows, cols(v0)], do[rows, cols(0)]
            kt = transpose(k2)
            dvs, dks, dqs = [], [], []
            for e in (0, 1):
                p = P[m * heads + 2 * j + e]
                pf = p.astype(jnp.float32)
                dpr = dot_nt(v2, do2 * head_masks[e])
                t = pf * dpr
                ds = (t - pf * jnp.sum(t, axis=0, keepdims=True)).astype(bf)
                dvs.append(dot(p, do2))
                dks.append(dot(ds, q2))
                dqs.append(dot(kt[64 * e:64 * (e + 1)], ds))
            dv[rows, cols(dv0)] = jnp.where(lane_low, dvs[0], dvs[1]).astype(bf)
            dk[rows, cols(dk0)] = (jnp.where(lane_low, dks[0], dks[1]) * 0.125).astype(bf)
            dq[rows, cols(dq0)] = (transpose(jnp.concatenate(dqs, axis=0)) * 0.125).astype(bf)
        loop(0, pairs, pair)

    def product(src, weight, cols, m, store, tile=256):
        rows = mrows(m)
        def one(j):
            at = pl.ds(pl.multiple_of(j * tile, tile), tile)
            store(rows, at, dot(src[rows, :], weight[:, at]))
        loop(0, cols // tile, one)

    def product_nt(src, s0, sw, weight, w0, m, store, tile=256):
        rows = mrows(m)
        def one(j):
            at = pl.ds(pl.multiple_of(j * tile, tile), tile)
            store(rows, at, dot_nt(src[rows, s0:s0 + sw], weight[at, w0:w0 + sw]))
        loop(0, weight.shape[0] // tile, one)

    def norm_into(source, m, index, target):
        def one(rows, _):
            unit, _ = normalize(source[rows, :])
            target[rows, :] = (unit * gain_at(index) + bias_at(index)).astype(bf)
        by_rows(m, one)

    def self_forward(m):
        def one(rows, local):
            unit, _ = normalize(X[m, local, :].astype(jnp.float32))
            H1[rows, :] = (unit * gain_at(0) + bias_at(0)).astype(bf)
        by_rows(m, one)
        def put(rows, at, value): QKV[rows, at] = value.astype(bf)
        product(H1, WQ, 3 * width, m, put)
        attention(m, QKV, 0, QKV, width, QKV, 2 * width, PT, O)
        def add(rows, at, value): RR[0, rows, at] = value + X[m, :, at].astype(jnp.float32)
        product(O, WO, width, m, add)

    def ffn_forward(m, source, index, last):
        norm_into(source, m, index, N2)
        def act(rows, at, value):
            A[rows, at], GP[rows, at] = (part.astype(bf) for part in gelu_parts(value))
        product(N2, W1, W1.shape[1], m, act)
        product(A, W2, width, m, last)

    for name in ("x", "gn", "bs", "wq", "wo"): loads[name].wait()
    def front(m):
        self_forward(m)
        @pl.when(enc)
        def _():
            @pl.when(m == 0)
            def _():
                loads["w1"].wait()
                loads["w2"].wait()
            def last(rows, at, value): AFT[rows, at] = value + RR[0, rows, at]
            ffn_forward(m, RR.at[0], 1, last)
            norm_into(AFT, m, 2, ST)
            st_copy(m).start()
    loop(0, 2, front)
    for name in ("ct", "wc"): loads[name].wait()
    @pl.when(dec)
    def _():
        loads["w1"].wait()
        loads["w2"].wait()
        wc_copy.wait_recv()
        wc_share.start()
        wc_share.wait_recv()

    def middle(m):
        rows = mrows(m)
        @pl.when(enc)
        def _():
            ds_copy(m).wait_recv()
            def one(r, local):
                unit, scale = normalize(AFT[r, :])
                grad = CT[m, local, :].astype(jnp.float32) + DST[r, :].astype(jnp.float32)
                add_norm_grads(2, grad, unit)
                back = norm_back(grad, unit, scale, gain_at(2))
                D[r, :] = back
                LOW[r, :] = back.astype(bf)
            by_rows(m, one)
        @pl.when(dec)
        def _():
            norm_into(RR.at[0], m, 1, HQ)
            def put_q(rows, at, value): CQ[rows, at] = value.astype(bf)
            product(HQ, WC.at[:, pl.ds(0, width)], width, m, put_q)
            st_copy(m).wait_recv()
            def put_kv(rows, at, value): KV[rows, at] = value.astype(bf)
            product(ST, WC0, 2 * width, m, put_kv)
            attention(m, CQ, 0, KV, 0, KV, width, PT2, O2)
            def add(rows, at, value): RR[1, rows, at] = value + RR[0, rows, at]
            product(O2, WC.at[:, pl.ds(width, width)], width, m, add)
            def last(rows, at, value): AFT[rows, at] = value + RR[1, rows, at]
            ffn_forward(m, RR.at[1], 2, last)
            def one(r, local):
                D[r, :] = CT[m, local, :].astype(jnp.float32)
                LOW[r, :] = CT[m, local, :]
            by_rows(m, one)
        def put_du(rows, at, value): GP[rows, at] = (value * GP[rows, at].astype(jnp.float32)).astype(bf)
        product_nt(LOW, 0, width, W2, 0, m, put_du)
        def put_dn(rows, at, value): AFT[rows, at] = value
        def emit(r, local):
            @pl.when(enc)
            def _(): out_v(m, local, ST[r, :])
            @pl.when(dec)
            def _(): out_v(m, local, AFT[r, :].astype(bf))
        by_rows(m, emit)
        product_nt(GP, 0, W1.shape[1], W1, 0, m, put_dn)
        def one(r, local):
            unit, scale = normalize(RR[sec, r, :])
            grad = AFT[r, :]
            add_norm_grads(1 + sec, grad, unit)
            D[r, :] = D[r, :] + norm_back(grad, unit, scale, gain_at(1 + sec))
        by_rows(m, one)
        @pl.when(dec)
        def _():
            def low(r, local): LOWC[r, :] = D[r, :].astype(bf)
            by_rows(m, low)
            def put_do(rows, at, value): DO[rows, at] = value.astype(bf)
            product_nt(LOWC, 0, width, WC.at[:, pl.ds(width, width)], 0, m, put_do)
            attention_back(m, DO, CQ, 0, KV, 0, KV, width, PT2, DCQ, 0, DKV, 0, DKV, width)
            def put_ds(rows, at, value): DST[rows, at] = value.astype(bf)
            product_nt(DKV, 0, 2 * width, WC0, 0, m, put_ds)
            ds_copy(m).start()
            @pl.when(m == 1)
            def _():
                dk_copy(0).start()
                dk_copy(1).start()
            def put_dh(rows, at, value): AFT[rows, at] = value
            product_nt(DCQ, 0, width, WC.at[:, pl.ds(0, width)], 0, m, put_dh)
            def two(r, local):
                unit, scale = normalize(RR[0, r, :])
                grad = AFT[r, :]
                add_norm_grads(1, grad, unit)
                D[r, :] = D[r, :] + norm_back(grad, unit, scale, gain_at(1))
            by_rows(m, two)

    OUT, GIN = TT[1], TT[2]
    def out_v(m, local, value): OUT[m, local, :] = value
    loop(0, 2, middle)
    outs = [pltpu.make_async_copy(OUT, out, o_sem.at[0])]
    outs[0].start()

    T = TT[0]
    def block(G, b):
        if 64 * n == 512: return G.at[b]
        return G.at[b * 512 // (64 * n), pl.ds(pl.multiple_of(lax.rem(b * 512, 64 * n), 512), 512)]
    def weight_grads(source, grad, c0, count, G, b0):
        T[...] = transpose(source[...])
        def one(i):
            at = pl.ds(pl.multiple_of(c0 + i * 512, 512), 512)
            block(G, b0 + i)[...] = dot(T[...], grad[:, at]).astype(bf)
        loop(0, count, one)

    weight_grads(N2, GP, 0, 4, G0, 0)
    def down(i):
        at = pl.ds(pl.multiple_of(i * 512, 512), 512)
        block(G0, 4 + i)[...] = dot(transpose(A[:, at]), LOW[...]).astype(bf)
    loop(0, 4, down)

    def bottom(m):
        def low(r, local): LOWS[r, :] = D[r, :].astype(bf)
        by_rows(m, low)
        def put_do(rows, at, value): DO[rows, at] = value.astype(bf)
        product_nt(LOWS, 0, width, WO, 0, m, put_do)
        attention_back(m, DO, QKV, 0, QKV, width, QKV, 2 * width, PT, DQKV, 0, DQKV, width, DQKV, 2 * width)
        def put_dh(rows, at, value): AFT[rows, at] = value
        product_nt(DQKV, 0, 3 * width, WQ, 0, m, put_dh)
        def one(r, local):
            unit, scale = normalize(X[m, local, :].astype(jnp.float32))
            grad = AFT[r, :]
            add_norm_grads(0, grad, unit)
            GIN[m, local, :] = (D[r, :] + norm_back(grad, unit, scale, gain_at(0))).astype(bf)
        by_rows(m, one)
    loop(0, 2, bottom)
    outs.append(pltpu.make_async_copy(GIN, gin, o_sem.at[1]))
    outs[1].start()
    weight_grads(H1, DQKV, 0, 3, G1, 0)
    weight_grads(O, LOWS, 0, 1, G1, 3)
    @pl.when(enc)
    def _():
        dk_copy(0).wait_recv()
        dk_copy(1).wait_recv()
        weight_grads(ST, DKV, 0, 2, G1, 4)
    @pl.when(dec)
    def _():
        weight_grads(HQ, DCQ, 0, 1, G1, 4)
        weight_grads(O2, LOWC, 0, 1, G1, 5)
    NG[...] = jnp.zeros_like(NG)
    for j in range(4):
        NG[0, j] = PG[:, 128 * j:128 * (j + 1)]
        NG[1, j] = PB[:, 128 * j:128 * (j + 1)]
    for i, (src, dst) in enumerate(((G0, g0), (G1, g1), (NG, ng))):
        outs.append(pltpu.make_async_copy(src, dst, o_sem.at[2 + i]))
        outs[-1].start()
    for c in outs: c.wait()
    @pl.when(enc)
    def _():
        wc_copy.wait_send()
        st_copy(0).wait_send()
        st_copy(1).wait_send()
    @pl.when(dec)
    def _():
        wc_share.wait_send()
        for m in (0, 1):
            ds_copy(m).wait_send()
            dk_copy(m).wait_send()


def layers(lens, x, ct, wq, wo, w1, w2, wc, gn, bs, n):
    bf, f4 = jnp.bfloat16, jnp.float32
    micro, length, width = x.shape
    rows, hidden = micro * length, w1.shape[1]
    any_ = pl.BlockSpec(memory_space=pl.ANY)
    V, DMA = pltpu.VMEM, pltpu.SemaphoreType.DMA
    def units(count): return (-(-count * 512 // (64 * n)), 64 * n, 512)
    shapes = [units(8), units(6)]
    sq = V((rows, width), bf)
    probs = V((micro * width // 64, length, length), bf)
    scratch = [V(a.shape, a.dtype) for a in (x, ct, wq, wo, w1, w2, wc)] + [V(wc.shape, bf), V(gn.shape, f4), V(bs.shape, f4)]
    scratch += [sq, V((rows, 3 * width), bf), probs, sq, V((2, rows, width), f4), sq, sq, sq, V((rows, 2 * width), bf), probs, sq, sq,
                V((rows, hidden), bf), V((rows, hidden), bf), V((rows, width), f4), V((rows, width), f4),
                sq, sq, sq, sq, V((rows, 3 * width), bf), sq, V((rows, 2 * width), bf), sq]
    scratch += [[V((width, rows), bf), V(x.shape, bf), V(x.shape, bf)], V(shapes[0], bf), V(shapes[1], bf), V((2, n, 8, 128), f4), V((8, width), f4), V((8, width), f4)]
    scratch += [DMA((9,)), DMA, DMA, DMA, DMA] + [DMA((2,))] * 6 + [DMA((5,))]
    return pl.pallas_call(
        functools.partial(compute_kernel, n),
        out_shape=[jax.ShapeDtypeStruct(s, bf) for s in shapes] + [jax.ShapeDtypeStruct((2, n, 8, 128), f4), jax.ShapeDtypeStruct(x.shape, bf), jax.ShapeDtypeStruct(x.shape, bf)],
        in_specs=[pl.BlockSpec(memory_space=pltpu.SMEM)] + [any_] * 9,
        out_specs=[any_] * 5,
        scratch_shapes=scratch,
        compiler_params=pltpu.CompilerParams(collective_id=1, has_side_effects=True, vmem_limit_bytes=62 * 2**20),
        name="layers",
    )(lens, x, ct, wq, wo, w1, w2, wc, gn, bs)


def pack_norm(en):
    return en[:, :4, :3].transpose(0, 2, 1, 3).reshape(2, 3, 512)


def local(layer_input, lengths, attn_qkv, attn_out, ffn_in, ffn_out, cross_weight, norm_gain, norm_bias, cotangent):
    n = lax.axis_size("dp") // 2
    g0, g1, ng, out, gin = layers(lengths[:, 0], layer_input[0, :, 0], cotangent[0, :, 0], attn_qkv[0], attn_out[0], ffn_in[0], ffn_out[0],
                                  cross_weight[0], norm_gain[0], norm_bias[0], n)
    e0, e1, en = all_reduce(g0, g1, ng, n)
    e0 = e0.reshape(-1, 512)[:8 * 512].reshape(8, 512, 512)
    e1 = e1.reshape(-1, 512)[:6 * 512].reshape(6, 512, 512)
    def wide(blocks):
        return blocks.transpose(1, 0, 2).reshape(1, 512, -1).astype(jnp.float32)
    en = pack_norm(en)
    return (out[None, :, None], gin[None, :, None], wide(e1[:3]), e1[3:4].astype(jnp.float32), wide(e0[:4]),
            e0[4:].reshape(1, 2048, 512).astype(jnp.float32), wide(e1[4:]), en[0:1], en[1:2])


def solution(mesh):
    data = P("section", None, "dp", None, None)
    weight = P("section", None, None)
    return jax.shard_map(
        local, mesh=mesh,
        in_specs=(data, P(None, "dp")) + (weight,) * 7 + (data,),
        out_specs=(data, data) + (weight,) * 7,
        check_vma=False,
    )
```

```python
import functools

import jax
import jax.numpy as jnp
from jax import lax
from jax.experimental import pallas as pl
from jax.experimental.pallas import tpu as pltpu
from jax.sharding import PartitionSpec as P

MESH = pl.DeviceIdType.MESH
BF = jnp.bfloat16
F4 = jnp.float32
SIDE = 512
TILE = 256


def dot(a, b):
    return jnp.dot(a, b, preferred_element_type=F4)


def dot_nt(a, b):
    return lax.dot_general(a, b, (((1,), (1,)), ((), ())), preferred_element_type=F4)


def gelu_parts(u):
    size = jnp.abs(u)
    t = 1.0 / (1.0 + (0.3275911 * 0.5 ** 0.5) * size)
    bell = jnp.exp(-0.5 * u * u)
    poly = t * (0.127414796 + t * (-0.142248368 + t * (0.7107068705 + t * (-0.7265760135 + t * 0.5307027145))))
    tail = poly * bell
    cdf = jnp.where(u >= 0, 1.0 - tail, tail)
    return u * cdf, cdf + u * bell * 0.3989422804014327


def normalize(value):
    center = value - jnp.mean(value, axis=-1, keepdims=True)
    spread = jnp.mean(center * center, axis=-1, keepdims=True)
    scale = lax.rsqrt(spread + 1e-05)
    return center * scale, scale


def norm_back(grad, unit, scale, gain):
    inner = grad * gain
    mean = jnp.mean(inner, axis=-1, keepdims=True)
    along = jnp.mean(inner * unit, axis=-1, keepdims=True)
    return scale * (inner - mean - unit * along)


def loop(start, stop, body, unroll=1):
    lax.fori_loop(start, stop, lambda i, carry: (body(i), carry)[1], 0, unroll=unroll)


def ds(start, size):
    return pl.ds(pl.multiple_of(start, size), size)


def block(ref, b):
    rows = ref.shape[1]
    return ref.at[b * SIDE // rows, pl.ds(b * SIDE % rows, SIDE)]


def remote(src, dst, ss, rs, to):
    return pltpu.make_async_remote_copy(src_ref=src, dst_ref=dst, send_sem=ss, recv_sem=rs, device_id=to, device_id_type=MESH)


class Stream:
    pass


def layers_kernel(n, lens, x, ct, wq, wo, w1, w2, wc, gn, bs,
                  WF, WR, EN, OUT, GIN,
                  X, CT, WC0, GN, BS, H1, QKV, PT, O, RR, ST, HQ, CQ, KV, PT2, O2, N2, A, GP, AFT, D, LOW, LOWC, DO, DQKV, DCQ, DKV, DST, T,
                  G0, G1, NG, S0, S1, NS, R0, R1, NR, PG, PB,
                  ld, wc_s, wc_r, wh_s, wh_r, st_s, st_r, ds_s, ds_r, dk_s, dk_r,
                  sib_s, sib_r, rs_s, rs_r, ag_s, ag_r, sh_s, sh_r):
    sec, dp = lax.axis_index("section"), lax.axis_index("dp")
    core, chip = lax.rem(dp, 2), dp // 2
    side, line = lax.rem(chip, 2), chip // 2
    pos = jnp.where(side == 0, line, n - 1 - line)

    def ring_at(q):
        q = lax.rem(q + n, n)
        return (jnp.where(q < n // 2, q, n - 1 - q) * 2 + jnp.where(q < n // 2, 0, 1)) * 2 + core

    sibling = dp + 1 - 2 * core
    partner, beside, after, before = (1 - sec, dp), (sec, sibling), (sec, ring_at(pos + 1)), (sec, ring_at(pos - 1))
    enc, dec = sec == 0, sec == 1
    length, width = X.shape[1], X.shape[2]
    hidden = A.shape[1]
    heads = width // 64
    pairs = heads // 2

    loads = {}

    def load(name, src, dst):
        loads.setdefault(name, []).append(pltpu.make_async_copy(src, dst, ld.at[sum(map(len, loads.values()))]))
        loads[name][-1].start()

    def columns(b): return pl.ds(b * SIDE, SIDE)
    load("first", x, X)
    load("first", gn, GN)
    load("first", bs, BS)
    for b in range(3): load("first", wq.at[:, columns(b)], block(WR, b))
    load("first", wo, block(WR, 3))
    for b in range(4): load("ffn", w1.at[:, columns(b)], block(WF, b))
    for b in range(4): load("ffn", w2.at[columns(b), :], block(WF, 4 + b))
    for b in range(2): load("cross", wc.at[:, columns(b)], block(WR, 4 + b))
    load("cross", ct, CT)

    def arrived(name):
        for copy in loads[name]: copy.wait()

    bar = pltpu.get_barrier_semaphore()
    for target in (partner, beside, after, before):
        pl.semaphore_signal(bar, inc=1, device_id=target, device_id_type=MESH)
    pl.semaphore_wait(bar, 4)

    half = ds(core * (width // 2), width // 2)
    wc_copy = remote(wc.at[half], WC0.at[half], wc_s, wc_r, partner)
    wc_share = remote(WC0.at[half], WC0.at[half], wh_s, wh_r, beside)

    def mrows(m): return ds(m * length, length)
    def st_copy(m): return remote(ST.at[mrows(m)], ST.at[mrows(m)], st_s.at[m], st_r.at[m], partner)
    ds_copy = remote(DST.at[mrows(1)], DST.at[mrows(1)], ds_s, ds_r, partner)
    def dk_copy(m): return remote(DKV.at[mrows(m)], DKV.at[mrows(m)], dk_s.at[m], dk_r.at[m], partner)

    @pl.when(enc)
    def _(): wc_copy.start()

    PG[...] = jnp.zeros_like(PG)
    PB[...] = jnp.zeros_like(PB)

    def gain_at(i): return GN[i]
    def bias_at(i): return BS[i]

    def add_norm_grads(i, grad, unit):
        at = pl.ds(i, 1)
        PG[at, :] = PG[at, :] + jnp.sum(grad * unit, axis=0, keepdims=True)
        PB[at, :] = PB[at, :] + jnp.sum(grad, axis=0, keepdims=True)

    lane_low = lax.broadcasted_iota(jnp.int32, (length, 128), 1) < 64
    lane_row = lax.broadcasted_iota(jnp.int32, (1, 128), 1) < 64
    head_masks = (jnp.where(lane_row, 1.0, 0.0).astype(BF), jnp.where(lane_row, 0.0, 1.0).astype(BF))
    query_masks = (jnp.where(lane_row, 0.125, 0.0).astype(BF), jnp.where(lane_row, 0.0, 0.125).astype(BF))

    def attention(m, q, q0, k, k0, v, v0, P, out_ref):
        rows = mrows(m)
        usable = lax.broadcasted_iota(jnp.int32, (length, length), 0) < lens[0, m]
        def pair(j):
            def cols(c0): return ds(c0 + j * 128, 128)
            q2, k2, vt = q[rows, cols(q0)], k[rows, cols(k0)], v[rows, cols(v0)].T
            parts = []
            for e in (0, 1):
                s = jnp.where(usable, dot_nt(k2, q2 * query_masks[e]), -1e30)
                w = jnp.exp(s - jnp.max(s, axis=0, keepdims=True))
                p = (w * (1.0 / jnp.sum(w, axis=0, keepdims=True))).astype(BF)
                P[m * heads + 2 * j + e] = p
                parts.append(dot(vt[64 * e:64 * (e + 1)], p))
            out_ref[rows, cols(0)] = jnp.concatenate(parts, axis=0).T.astype(BF)
        loop(0, pairs, pair, unroll=4)

    def attention_back(m, do, q, q0, k, k0, v, v0, P, dq, dq0, dk, dk0, dv, dv0):
        rows = mrows(m)
        def pair(j):
            def cols(c0): return ds(c0 + j * 128, 128)
            q2, k2, v2, do2 = q[rows, cols(q0)], k[rows, cols(k0)], v[rows, cols(v0)], do[rows, cols(0)]
            kt = k2.T
            dvs, dks, dqs = [], [], []
            for e in (0, 1):
                p = P[m * heads + 2 * j + e]
                pf = p.astype(F4)
                t = pf * dot_nt(v2, do2 * head_masks[e])
                dsc = (t - pf * jnp.sum(t, axis=0, keepdims=True)).astype(BF)
                dvs.append(dot(p, do2))
                dks.append(dot(dsc, q2))
                dqs.append(dot(kt[64 * e:64 * (e + 1)], dsc))
            dv[rows, cols(dv0)] = jnp.where(lane_low, dvs[0], dvs[1]).astype(BF)
            dk[rows, cols(dk0)] = (jnp.where(lane_low, dks[0], dks[1]) * 0.125).astype(BF)
            dq[rows, cols(dq0)] = (jnp.concatenate(dqs, axis=0).T * 0.125).astype(BF)
        loop(0, pairs, pair, unroll=4)

    def tiles(count): return [(t, pl.ds(t * TILE, TILE)) for t in range(count // TILE)]
    def tile_of(ref, b0, t): return block(ref, b0 + t * TILE // SIDE)[:, pl.ds(t * TILE % SIDE, TILE)]
    def rows_of(ref, b0, t): return block(ref, b0 + t * TILE // SIDE)[pl.ds(t * TILE % SIDE, TILE), :]

    def norm_into(source, m, index, target):
        rows = mrows(m)
        unit, _ = normalize(source[rows, :])
        target[rows, :] = (unit * gain_at(index) + bias_at(index)).astype(BF)

    def self_forward(m):
        rows = mrows(m)
        unit, _ = normalize(X[m].astype(F4))
        H1[rows, :] = (unit * gain_at(0) + bias_at(0)).astype(BF)
        for t, at in tiles(3 * width): QKV[rows, at] = dot(H1[rows, :], tile_of(WR, 0, t)).astype(BF)
        attention(m, QKV, 0, QKV, width, QKV, 2 * width, PT, O)
        for t, at in tiles(width): RR[0, rows, at] = dot(O[rows, :], tile_of(WR, 3, t)) + X[m, :, at].astype(F4)

    def ffn_forward(m, source, index):
        rows = mrows(m)
        norm_into(source, m, index, N2)
        for t, at in tiles(hidden):
            A[rows, at], GP[rows, at] = (part.astype(BF) for part in gelu_parts(dot(N2[rows, :], tile_of(WF, 0, t))))
        for t, at in tiles(width):
            total = source[rows, at]
            for b in range(hidden // SIDE): total = total + dot(A[rows, columns(b)], tile_of(WF, 4 + b, t))
            AFT[rows, at] = total

    arrived("first")

    def front(m):
        self_forward(m)
        @pl.when(enc)
        def _():
            @pl.when(m == 0)
            def _(): arrived("ffn")
            ffn_forward(m, RR.at[0], 1)
            norm_into(AFT, m, 2, ST)
            st_copy(m).start()
            OUT[m] = ST[mrows(m), :]
    loop(0, 2, front)
    arrived("cross")

    @pl.when(dec)
    def _():
        arrived("ffn")
        wc_copy.wait_recv()
        wc_share.start()
        wc_share.wait_recv()

    def middle(m):
        rows = mrows(m)
        @pl.when(enc)
        def _():
            @pl.when(m == 0)
            def _():
                dk_copy(0).wait_recv()
                for t, at in tiles(width):
                    total = dot_nt(DKV[rows, columns(0)], rows_of(WR, 4, t)) + dot_nt(DKV[rows, columns(1)], rows_of(WR, 5, t))
                    DST[rows, at] = total.astype(BF)
            @pl.when(m == 1)
            def _(): ds_copy.wait_recv()
            unit, scale = normalize(AFT[rows, :])
            grad = CT[m].astype(F4) + DST[rows, :].astype(F4)
            add_norm_grads(2, grad, unit)
            back = norm_back(grad, unit, scale, gain_at(2))
            D[rows, :] = back
            LOW[rows, :] = back.astype(BF)
        @pl.when(dec)
        def _():
            norm_into(RR.at[0], m, 1, HQ)
            for t, at in tiles(width): CQ[rows, at] = dot(HQ[rows, :], tile_of(WR, 4, t)).astype(BF)
            st_copy(m).wait_recv()
            for t, at in tiles(2 * width): KV[rows, at] = dot(ST[rows, :], WC0[:, at]).astype(BF)
            attention(m, CQ, 0, KV, 0, KV, width, PT2, O2)
            for t, at in tiles(width): RR[1, rows, at] = dot(O2[rows, :], tile_of(WR, 5, t)) + RR[0, rows, at]
            ffn_forward(m, RR.at[1], 2)
            OUT[m] = AFT[rows, :].astype(BF)
            D[rows, :] = CT[m].astype(F4)
            LOW[rows, :] = CT[m]
        for t, at in tiles(hidden): GP[rows, at] = (dot_nt(LOW[rows, :], rows_of(WF, 4, t)) * GP[rows, at].astype(F4)).astype(BF)
        for t, at in tiles(width):
            total = dot_nt(GP[rows, columns(0)], rows_of(WF, 0, t))
            for b in range(1, hidden // SIDE): total = total + dot_nt(GP[rows, columns(b)], rows_of(WF, b, t))
            AFT[rows, at] = total
        unit, scale = normalize(RR[sec, rows, :])
        grad = AFT[rows, :]
        add_norm_grads(1 + sec, grad, unit)
        D[rows, :] = D[rows, :] + norm_back(grad, unit, scale, gain_at(1 + sec))
        @pl.when(dec)
        def _():
            LOWC[rows, :] = D[rows, :].astype(BF)
            for t, at in tiles(width): DO[rows, at] = dot_nt(LOWC[rows, :], rows_of(WR, 5, t)).astype(BF)
            attention_back(m, DO, CQ, 0, KV, 0, KV, width, PT2, DCQ, 0, DKV, 0, DKV, width)
            @pl.when(m == 1)
            def _():
                for t, at in tiles(width): DST[rows, at] = dot_nt(DKV[rows, :], WC0[at, :]).astype(BF)
                ds_copy.start()
            dk_copy(m).start()
            for t, at in tiles(width): AFT[rows, at] = dot_nt(DCQ[rows, :], rows_of(WR, 4, t))
            unit, scale = normalize(RR[0, rows, :])
            grad = AFT[rows, :]
            add_norm_grads(1, grad, unit)
            D[rows, :] = D[rows, :] + norm_back(grad, unit, scale, gain_at(1))
    loop(0, 2, middle)

    part = 16 * n
    other_rows = ds((1 - core) * 2 * part, 2 * part)
    def rows_at(d, k, c): return ds((c * 2 + d) * part + k * 16, 16)
    streams = []
    for g, (G, S, R, E) in enumerate(((G0, S0, R0, WF), (G1, S1, R1, WR))):
        for d in (0, 1):
            st = Stream()
            st.i, st.d, st.g, st.to = len(streams), d, g, after if d == 0 else before
            st.own = lambda k, G=G, d=d: G.at[:, rows_at(d, k, core), :]
            st.sib = lambda k, S=S, d=d: S.at[:, rows_at(d, k, 0), :]
            st.slot = lambda s, R=R, d=d: R.at[d, s]
            st.res = lambda k, E=E, d=d: E.at[:, rows_at(d, k, core), :]
            streams.append(st)
    st = Stream()
    st.i, st.d, st.g, st.to = 4, 0, 1, after
    st.own, st.sib, st.slot, st.res = (lambda k: NG.at[core, k]), (lambda k: NS.at[k]), (lambda s: NR.at[s]), (lambda k: EN.at[core, k])
    streams.append(st)
    group = [[st for st in streams if st.g == g] for g in (0, 1)]

    def chunk(st, s): return lax.rem(pos - s + 2 * n, n) if st.d == 0 else lax.rem(pos + s, n)
    def rs_copy(st, s): return remote(st.own(chunk(st, s)), st.slot(s), rs_s.at[st.i, s], rs_r.at[st.i, s], st.to)
    def ag_copy(st, t):
        res = st.res(chunk(st, t + n - 1))
        return remote(res, res, ag_s.at[st.i, t], ag_r.at[st.i, t], st.to)
    def sh_copy(st, t):
        res = st.res(chunk(st, t + n - 1))
        return remote(res, res, sh_s.at[st.i, t], sh_r.at[st.i, t], beside)
    sib_copies = [[remote(G.at[u, other_rows], S.at[u], sib_s.at[g, u], sib_r.at[g, u], beside) for u in range(G.shape[0])]
                  for g, (G, S) in enumerate(((G0, S0), (G1, S1)))]
    sib_copies[1].append(remote(NG.at[1 - core], NS, sib_s.at[1, G1.shape[0]], sib_r.at[1, G1.shape[0]], beside))

    def reduce_step(g, s, first=False, last=False):
        for st in group[g]:
            own = st.own(chunk(st, s))
            total = own[...].astype(F4) + st.sib(chunk(st, s))[...].astype(F4)
            if not first:
                rs_copy(st, s - 1).wait_recv()
                total = total + st.slot(s - 1)[...].astype(F4)
            if last:
                st.res(chunk(st, s))[...] = total.astype(own.dtype)
                ag_copy(st, 0).start()
                sh_copy(st, 0).start()
            else:
                own[...] = total.astype(own.dtype)
                rs_copy(st, s).start()

    def gather_step(g, t):
        for st in group[g]:
            ag_copy(st, t).wait_recv()
            @pl.when(t < n - 2)
            def _(): ag_copy(st, t + 1).start()
            sh_copy(st, t + 1).start()

    def begin(g):
        for copy in sib_copies[g]: copy.wait_recv()
        reduce_step(g, 0, first=True)

    def done_blocks(g, G, count):
        per = G.shape[1] // SIDE
        for u in range(G.shape[0]):
            if count == min((u + 1) * per, (8, 6)[g]): sib_copies[g][u].start()

    def weight_grads(g, G, source, grad, count, b0):
        T[...] = source[...].T
        for b in range(count):
            block(G, b0 + b)[...] = dot(T[...], grad[:, columns(b)]).astype(BF)
            done_blocks(g, G, b0 + b + 1)

    weight_grads(0, G0, N2, GP, 4, 0)
    for b in range(4):
        block(G0, 4 + b)[...] = dot(A[:, columns(b)].T, LOW[...]).astype(BF)
        done_blocks(0, G0, 4 + b + 1)
    begin(0)

    def bottom(m):
        rows = mrows(m)
        LOW[rows, :] = D[rows, :].astype(BF)
        for t, at in tiles(width): DO[rows, at] = dot_nt(LOW[rows, :], rows_of(WR, 3, t)).astype(BF)
        attention_back(m, DO, QKV, 0, QKV, width, QKV, 2 * width, PT, DQKV, 0, DQKV, width, DQKV, 2 * width)
        for t, at in tiles(width):
            total = dot_nt(DQKV[rows, columns(0)], rows_of(WR, 0, t))
            for b in (1, 2): total = total + dot_nt(DQKV[rows, columns(b)], rows_of(WR, b, t))
            AFT[rows, at] = total
        unit, scale = normalize(X[m].astype(F4))
        grad = AFT[rows, :]
        add_norm_grads(0, grad, unit)
        GIN[m] = (D[rows, :] + norm_back(grad, unit, scale, gain_at(0))).astype(BF)
        reduce_step(0, m + 1)
    loop(0, 2, bottom)
    NG[...] = jnp.zeros_like(NG)
    for j in range(4):
        NG[0, j] = PG[:, 128 * j:128 * (j + 1)]
        NG[1, j] = PB[:, 128 * j:128 * (j + 1)]
    sib_copies[1][-1].start()
    weight_grads(1, G1, H1, DQKV, 3, 0)
    weight_grads(1, G1, O, LOW, 1, 3)
    @pl.when(enc)
    def _():
        dk_copy(1).wait_recv()
        T[...] = ST[...].T
        for b in range(2): block(G1, 4 + b)[...] = dot(T[...], DKV[:, columns(b)]).astype(BF)
    @pl.when(dec)
    def _():
        for b, (source, grad) in enumerate(((HQ, DCQ), (O2, LOWC))):
            T[...] = source[...].T
            block(G1, 4 + b)[...] = dot(T[...], grad[...]).astype(BF)
    for b in range(2): done_blocks(1, G1, 5 + b)
    reduce_step(0, 3)
    ahead = 4
    begin(1)
    if n - 1 > ahead:
        reduce_step(0, ahead)
        def both(i):
            reduce_step(1, i)
            reduce_step(0, i + ahead)
        loop(1, n - 1 - ahead, both)
        reduce_step(1, n - 1 - ahead)
    reduce_step(0, n - 1, last=True)
    def cross_over(i):
        reduce_step(1, n - ahead + i)
        gather_step(0, i)
    loop(0, ahead - 1, cross_over)
    reduce_step(1, n - 1, last=True)
    gather_step(0, ahead - 1)
    def both_out(i):
        gather_step(0, ahead + i)
        gather_step(1, i)
    loop(0, n - 1 - ahead, both_out)
    loop(n - 1 - ahead, n - 1, lambda t: gather_step(1, t))

    def drain(s):
        for st in streams:
            sh_copy(st, s).wait()
            @pl.when(s < n - 1)
            def _():
                rs_copy(st, s).wait_send()
                ag_copy(st, s).wait_send()
    loop(0, n, drain)
    for copy in sib_copies[0] + sib_copies[1]: copy.wait_send()

    @pl.when(enc)
    def _():
        wc_copy.wait_send()
        for m in (0, 1): st_copy(m).wait_send()
    @pl.when(dec)
    def _():
        wc_share.wait_send()
        ds_copy.wait_send()
        for m in (0, 1): dk_copy(m).wait_send()


def finish_kernel(e0, e1, en, out, gin, o_out, o_gin, o_qkv, o_wo, o_up, o_down, o_cross, o_gain, o_bias, F, sem, sem2):
    copies = [pltpu.make_async_copy(out, o_out, sem2.at[0]), pltpu.make_async_copy(gin, o_gin, sem2.at[1])]
    for copy in copies: copy.start()
    for j in range(4):
        at = pl.ds(128 * j, 128)
        for i in range(3):
            o_gain[i, :, at] = en[0, j, i:i + 1, :]
            o_bias[i, :, at] = en[1, j, i:i + 1, :]
    def columns(b): return pl.ds(b * SIDE, SIDE)
    targets = [(e0, b, o_up.at[0, :, columns(b)]) for b in range(4)] + [(e0, 4 + b, o_down.at[0, columns(b), :]) for b in range(4)]
    targets += [(e1, b, o_qkv.at[0, :, columns(b)]) for b in range(3)] + [(e1, 3, o_wo.at[0])]
    targets += [(e1, 4 + b, o_cross.at[0, :, columns(b)]) for b in range(2)]
    slots = F.shape[0]
    flight = []
    for i, (e, b, target) in enumerate(targets):
        if i >= slots: flight[i - slots].wait()
        F[i % slots] = block(e, b)[...].astype(F4)
        flight.append(pltpu.make_async_copy(F.at[i % slots], target, sem.at[i % slots]))
        flight[-1].start()
    for copy in flight[-slots:] + copies: copy.wait()


def layers(lens, x, ct, wq, wo, w1, w2, wc, gn, bs, n):
    micro, length, width = x.shape
    rows, hidden = micro * length, w1.shape[1]
    any_ = pl.BlockSpec(memory_space=pl.ANY)
    vmem = pl.BlockSpec(memory_space=pltpu.VMEM)
    V, DMA = pltpu.VMEM, pltpu.SemaphoreType.DMA
    def units(count): return (-(-count * SIDE // (64 * n)), 64 * n, SIDE)
    s0, s1 = units(8), units(6)
    norm = (2, n, 8, 128)
    def own(s): return (s[0], s[1] // 2, SIDE)
    def slots(s): return (2, n - 1, s[0], 16, SIDE)
    sq = V((rows, width), BF)
    probs = V((micro * width // 64, length, length), BF)
    scratch = [V(x.shape, BF), V(x.shape, BF), V(wc.shape, BF), V(gn.shape, F4), V(bs.shape, F4)]
    scratch += [sq, V((rows, 3 * width), BF), probs, sq, V((2, rows, width), F4), sq, sq, sq, V((rows, 2 * width), BF), probs, sq, sq,
                V((rows, hidden), BF), V((rows, hidden), BF), V((rows, width), F4), V((rows, width), F4),
                sq, sq, sq, V((rows, 3 * width), BF), sq, V((rows, 2 * width), BF), sq, V((width, rows), BF)]
    scratch += [V(s0, BF), V(s1, BF), V(norm, F4), V(own(s0), BF), V(own(s1), BF), V(norm[1:], F4), V(slots(s0), BF), V(slots(s1), BF), V((n - 1, 8, 128), F4),
                V((8, width), F4), V((8, width), F4)]
    scratch += [DMA((18,)), DMA, DMA, DMA, DMA, DMA((2,)), DMA((2,)), DMA, DMA, DMA((2,)), DMA((2,)), DMA((2, 9)), DMA((2, 9))] + [DMA((5, n))] * 6
    results = [V(s0, BF), V(s1, BF), V(norm, F4), V(x.shape, BF), V(x.shape, BF)]
    e0, e1, en, out, gin = pl.pallas_call(
        functools.partial(layers_kernel, n), out_shape=results,
        in_specs=[pl.BlockSpec(memory_space=pltpu.SMEM)] + [any_] * 9, out_specs=[vmem] * 5, scratch_shapes=scratch,
        compiler_params=pltpu.CompilerParams(collective_id=1, has_side_effects=True, vmem_limit_bytes=52 * 2**20),
        name="layers",
    )(lens, x, ct, wq, wo, w1, w2, wc, gn, bs)
    def f4(*shape): return jax.ShapeDtypeStruct(shape, F4)
    return pl.pallas_call(
        finish_kernel,
        out_shape=[jax.ShapeDtypeStruct(x.shape, BF)] * 2 + [f4(1, width, 3 * width), f4(1, width, width), f4(1, width, hidden), f4(1, hidden, width),
                                                            f4(1, width, 2 * width), f4(3, 1, width), f4(3, 1, width)],
        in_specs=[vmem] * 5, out_specs=[any_] * 7 + [vmem] * 2,
        scratch_shapes=[V((4, SIDE, SIDE), F4), DMA((4,)), DMA((2,))],
        compiler_params=pltpu.CompilerParams(vmem_limit_bytes=6 * 2**20),
        name="finish",
    )(e0, e1, en, out, gin)


def local(layer_input, lengths, attn_qkv, attn_out, ffn_in, ffn_out, cross_weight, norm_gain, norm_bias, cotangent):
    def flat(a): return a.reshape(a.shape[1:])
    n = lax.axis_size("dp") // 2
    data = (layer_input.shape[1],) + layer_input.shape[3:]
    out, gin, *grads, gain, bias = layers(lengths.T, layer_input.reshape(data), cotangent.reshape(data), flat(attn_qkv), flat(attn_out), flat(ffn_in), flat(ffn_out),
                              flat(cross_weight), norm_gain.transpose(1, 0, 2), norm_bias.transpose(1, 0, 2), n)
    return (out.reshape(layer_input.shape), gin.reshape(layer_input.shape), *grads, gain.transpose(1, 0, 2), bias.transpose(1, 0, 2))


def solution(mesh):
    data = P("section", None, "dp", None, None)
    weight = P("section", None, None)
    return jax.shard_map(
        local, mesh=mesh,
        in_specs=(data, P(None, "dp")) + (weight,) * 7 + (data,),
        out_specs=(data, data) + (weight,) * 7,
        check_vma=False,
    )
```

```python
import functools

import jax
import jax.numpy as jnp
from jax import lax
from jax.experimental import pallas as pl
from jax.experimental.pallas import tpu as pltpu
from jax.sharding import PartitionSpec as P

MESH = pl.DeviceIdType.MESH
BF = jnp.bfloat16
F4 = jnp.float32
SIDE = 512
TILE = 256


def dot(a, b):
    return jnp.dot(a, b, preferred_element_type=F4)


def dot_nt(a, b):
    return lax.dot_general(a, b, (((1,), (1,)), ((), ())), preferred_element_type=F4)


def gelu_parts(u):
    size = jnp.abs(u)
    t = 1.0 / (1.0 + (0.3275911 * 0.5 ** 0.5) * size)
    bell = jnp.exp(-0.5 * u * u)
    poly = t * (0.127414796 + t * (-0.142248368 + t * (0.7107068705 + t * (-0.7265760135 + t * 0.5307027145))))
    tail = poly * bell
    cdf = jnp.where(u >= 0, 1.0 - tail, tail)
    return u * cdf, cdf + u * bell * 0.3989422804014327


def normalize(value):
    center = value - jnp.mean(value, axis=-1, keepdims=True)
    spread = jnp.mean(center * center, axis=-1, keepdims=True)
    scale = lax.rsqrt(spread + 1e-05)
    return center * scale, scale


def norm_back(grad, unit, scale, gain):
    inner = grad * gain
    mean = jnp.mean(inner, axis=-1, keepdims=True)
    along = jnp.mean(inner * unit, axis=-1, keepdims=True)
    return scale * (inner - mean - unit * along)


def loop(start, stop, body, unroll=1):
    lax.fori_loop(start, stop, lambda i, carry: (body(i), carry)[1], 0, unroll=unroll)


def ds(start, size):
    return pl.ds(pl.multiple_of(start, size), size)


def block(ref, b):
    rows = ref.shape[1]
    return ref.at[b * SIDE // rows, pl.ds(b * SIDE % rows, SIDE)]


def remote(src, dst, ss, rs, to):
    return pltpu.make_async_remote_copy(src_ref=src, dst_ref=dst, send_sem=ss, recv_sem=rs, device_id=to, device_id_type=MESH)


class Flow:
    pass


def layers_kernel(n, lens, x, ct, wq, wo, w1, w2, wc, gn, bs,
                  WF, WR, EN, OUT, GIN,
                  X, CT, WC0, GN, BS, H1, QKV, PT, O, RR, ST, HQ, CQ, KV, PT2, O2, N2, A, GP, AFT, D, LOW, LOWC, LOWS, DO, DQKV, DCQ, DKV, DST, T,
                  G0, G1, NG, CG, CS, S0, S1, NS, R0, R1, NR, PG, PB,
                  ld, wc_s, wc_r, wh_s, wh_r, st_s, st_r, ds_s, ds_r, dk_s, dk_r, cg_s, cg_r,
                  sib_s, sib_r, rs_s, rs_r, ag_s, ag_r, sh_s, sh_r):
    sec, dp = lax.axis_index("section"), lax.axis_index("dp")
    core, chip = lax.rem(dp, 2), dp // 2
    side, line = lax.rem(chip, 2), chip // 2
    pos = jnp.where(side == 0, line, n - 1 - line)

    def ring_at(q):
        q = lax.rem(q + n, n)
        return (jnp.where(q < n // 2, q, n - 1 - q) * 2 + jnp.where(q < n // 2, 0, 1)) * 2 + core

    sibling = dp + 1 - 2 * core
    partner, beside, after, before = (1 - sec, dp), (sec, sibling), (sec, ring_at(pos + 1)), (sec, ring_at(pos - 1))
    across = (sec, dp + 2 - 4 * side)
    enc, dec = sec == 0, sec == 1
    direct = 64 * n == SIDE
    length, width = X.shape[1], X.shape[2]
    hidden = A.shape[1]
    heads = width // 64
    pairs = heads // 2

    loads = {}

    def load(name, src, dst):
        loads.setdefault(name, []).append(pltpu.make_async_copy(src, dst, ld.at[sum(map(len, loads.values()))]))
        loads[name][-1].start()

    def columns(b): return pl.ds(b * SIDE, SIDE)
    load("first", x, X)
    load("first", gn, GN)
    load("first", bs, BS)
    for b in range(3): load("first", wq.at[:, columns(b)], block(WR, b))
    load("first", wo, block(WR, 3))
    for b in range(4): load("ffn", w1.at[:, columns(b)], block(WF, b))
    for b in range(4): load("ffn", w2.at[columns(b), :], block(WF, 4 + b))
    for b in range(2): load("cross", wc.at[:, columns(b)], block(WR, 4 + b))
    load("cross", ct, CT)

    def arrived(name):
        for copy in loads[name]: copy.wait()

    bar = pltpu.get_barrier_semaphore()
    for target in (partner, beside, after, before, across):
        pl.semaphore_signal(bar, inc=1, device_id=target, device_id_type=MESH)
    pl.semaphore_wait(bar, 5)

    def quarter(x, c): return WC0.at[ds((2 * x + c) * (width // 4), width // 4)]
    wc_copy = remote(wc.at[ds((2 * side + core) * (width // 4), width // 4)], quarter(side, core), wc_s, wc_r, partner)
    wc_trades = [remote(quarter(side, core), quarter(side, core), wh_s.at[0], wh_r.at[0], across),
                 remote(quarter(side, core), quarter(side, core), wh_s.at[1], wh_r.at[1], beside),
                 remote(quarter(1 - side, core), quarter(1 - side, core), wh_s.at[2], wh_r.at[2], beside)]

    def mrows(m): return ds(m * length, length)
    def st_copy(m): return remote(ST.at[mrows(m)], ST.at[mrows(m)], st_s.at[m], st_r.at[m], partner)
    def ds_copy(m): return remote(DST.at[mrows(m)], DST.at[mrows(m)], ds_s.at[m], ds_r.at[m], partner)
    def dk_copy(m): return remote(DKV.at[mrows(m)], DKV.at[mrows(m)], dk_s.at[m], dk_r.at[m], partner)

    @pl.when(enc)
    def _(): wc_copy.start()

    PG[...] = jnp.zeros_like(PG)
    PB[...] = jnp.zeros_like(PB)

    def gain_at(i): return GN[i]
    def bias_at(i): return BS[i]

    def add_norm_grads(i, grad, unit):
        at = pl.ds(i, 1)
        PG[at, :] = PG[at, :] + jnp.sum(grad * unit, axis=0, keepdims=True)
        PB[at, :] = PB[at, :] + jnp.sum(grad, axis=0, keepdims=True)

    lane_low = lax.broadcasted_iota(jnp.int32, (length, 128), 1) < 64
    lane_row = lax.broadcasted_iota(jnp.int32, (1, 128), 1) < 64
    head_masks = (jnp.where(lane_row, 1.0, 0.0).astype(BF), jnp.where(lane_row, 0.0, 1.0).astype(BF))
    query_masks = (jnp.where(lane_row, 0.125, 0.0).astype(BF), jnp.where(lane_row, 0.0, 0.125).astype(BF))

    def attention(m, q, q0, k, k0, v, v0, P, out_ref):
        rows = mrows(m)
        usable = lax.broadcasted_iota(jnp.int32, (length, length), 0) < lens[0, m]
        def cols(c0, j): return pl.ds(c0 + j * 128, 128)
        def score(h):
            j, e = h // 2, h % 2
            return dot_nt(k[rows, cols(k0, j)], q[rows, cols(q0, j)] * query_masks[e])
        def soft(s, h):
            s = jnp.where(usable, s, -1e30)
            w = jnp.exp(s - jnp.max(s, axis=0, keepdims=True))
            p = (w * (1.0 / jnp.sum(w, axis=0, keepdims=True))).astype(BF)
            P[m * heads + h] = p
        for h in range(heads): soft(score(h), h)
        for j in range(pairs):
            vt = v[rows, cols(v0, j)].T
            parts = [dot(vt[64 * e:64 * (e + 1)], P[m * heads + 2 * j + e]) for e in (0, 1)]
            out_ref[rows, cols(0, j)] = jnp.concatenate(parts, axis=0).T.astype(BF)

    def attention_back(m, do, q, q0, k, k0, v, v0, P, dq, dq0, dk, dk0, dv, dv0):
        rows = mrows(m)
        def cols(c0, j): return pl.ds(c0 + j * 128, 128)
        def weights(h): return P.at[m * heads + h]
        def grad_scores(h):
            j, e = h // 2, h % 2
            pf = weights(h)[...].astype(F4)
            t = pf * dot_nt(v[rows, cols(v0, j)], do[rows, cols(0, j)] * head_masks[e])
            return (t - pf * jnp.sum(t, axis=0, keepdims=True)).astype(BF)
        def put_v(j):
            do2 = do[rows, cols(0, j)]
            dv[rows, cols(dv0, j)] = jnp.where(lane_low, dot(weights(2 * j)[...], do2), dot(weights(2 * j + 1)[...], do2)).astype(BF)
        def put_k(j):
            q2 = q[rows, cols(q0, j)]
            dk[rows, cols(dk0, j)] = (jnp.where(lane_low, dot(weights(2 * j)[...], q2), dot(weights(2 * j + 1)[...], q2)) * 0.125).astype(BF)
        def put_q(j):
            kt = k[rows, cols(k0, j)].T
            parts = [dot(kt[64 * e:64 * (e + 1)], weights(2 * j + e)[...]) for e in (0, 1)]
            dq[rows, cols(dq0, j)] = (jnp.concatenate(parts, axis=0).T * 0.125).astype(BF)
        for j in range(pairs):
            put_v(j)
            for h in (2 * j, 2 * j + 1): weights(h)[...] = grad_scores(h)
        for j in range(pairs):
            put_k(j)
            put_q(j)

    def tiles(count): return [(t, pl.ds(t * TILE, TILE)) for t in range(count // TILE)]
    def tile_of(ref, b0, t): return block(ref, b0 + t * TILE // SIDE)[:, pl.ds(t * TILE % SIDE, TILE)]
    def rows_of(ref, b0, t): return block(ref, b0 + t * TILE // SIDE)[pl.ds(t * TILE % SIDE, TILE), :]

    def norm_into(source, m, index, target):
        rows = mrows(m)
        unit, _ = normalize(source[rows, :])
        target[rows, :] = (unit * gain_at(index) + bias_at(index)).astype(BF)

    def self_forward(m):
        rows = mrows(m)
        unit, _ = normalize(X[m].astype(F4))
        H1[rows, :] = (unit * gain_at(0) + bias_at(0)).astype(BF)
        for t, at in tiles(3 * width): QKV[rows, at] = dot(H1[rows, :], tile_of(WR, 0, t)).astype(BF)
        attention(m, QKV, 0, QKV, width, QKV, 2 * width, PT, O)
        for t, at in tiles(width): RR[0, rows, at] = dot(O[rows, :], tile_of(WR, 3, t)) + X[m, :, at].astype(F4)

    def ffn_forward(m, source, index):
        rows = mrows(m)
        norm_into(source, m, index, N2)
        for t, at in tiles(hidden):
            A[rows, at], GP[rows, at] = (part.astype(BF) for part in gelu_parts(dot(N2[rows, :], tile_of(WF, 0, t))))
        for t, at in tiles(width):
            total = source[rows, at]
            for b in range(hidden // SIDE): total = total + dot(A[rows, columns(b)], tile_of(WF, 4 + b, t))
            AFT[rows, at] = total

    arrived("first")

    def front(m):
        self_forward(m)
        @pl.when(enc)
        def _():
            @pl.when(m == 0)
            def _(): arrived("ffn")
            ffn_forward(m, RR.at[0], 1)
            norm_into(AFT, m, 2, ST)
            st_copy(m).start()
            OUT[m] = ST[mrows(m), :]
    loop(0, 2, front)
    arrived("cross")

    @pl.when(dec)
    def _():
        arrived("ffn")
        wc_copy.wait_recv()
        wc_trades[0].start()
        wc_trades[1].start()
        for m in (0, 1):
            norm_into(RR.at[0], m, 1, HQ)
            for t, at in tiles(width): CQ[mrows(m), at] = dot(HQ[mrows(m), :], tile_of(WR, 4, t)).astype(BF)
        wc_trades[0].wait_recv()
        wc_trades[2].start()
        wc_trades[1].wait_recv()
        wc_trades[2].wait_recv()

    def bottom(m, hook=None):
        rows = mrows(m)
        LOWS[rows, :] = D[rows, :].astype(BF)
        for t, at in tiles(width): DO[rows, at] = dot_nt(LOWS[rows, :], rows_of(WR, 3, t)).astype(BF)
        if hook is not None: hook(m, 0)
        attention_back(m, DO, QKV, 0, QKV, width, QKV, 2 * width, PT, DQKV, 0, DQKV, width, DQKV, 2 * width)
        if hook is not None: hook(m, 1)
        for t, at in tiles(width):
            total = dot_nt(DQKV[rows, columns(0)], rows_of(WR, 0, t))
            for b in (1, 2): total = total + dot_nt(DQKV[rows, columns(b)], rows_of(WR, b, t))
            AFT[rows, at] = total
        unit, scale = normalize(X[m].astype(F4))
        grad = AFT[rows, :]
        add_norm_grads(0, grad, unit)
        GIN[m] = (D[rows, :] + norm_back(grad, unit, scale, gain_at(0))).astype(BF)

    def middle(m):
        rows = mrows(m)
        @pl.when(enc)
        def _():
            ds_copy(m).wait_recv()
            unit, scale = normalize(AFT[rows, :])
            grad = CT[m].astype(F4) + DST[rows, :].astype(F4)
            add_norm_grads(2, grad, unit)
            back = norm_back(grad, unit, scale, gain_at(2))
            D[rows, :] = back
            LOW[rows, :] = back.astype(BF)
        @pl.when(dec)
        def _():
            st_copy(m).wait_recv()
            for t, at in tiles(2 * width): KV[rows, at] = dot(ST[rows, :], WC0[:, at]).astype(BF)
            attention(m, CQ, 0, KV, 0, KV, width, PT2, O2)
            for t, at in tiles(width): RR[1, rows, at] = dot(O2[rows, :], tile_of(WR, 5, t)) + RR[0, rows, at]
            ffn_forward(m, RR.at[1], 2)
            OUT[m] = AFT[rows, :].astype(BF)
            D[rows, :] = CT[m].astype(F4)
            LOW[rows, :] = CT[m]
        for t, at in tiles(hidden): GP[rows, at] = (dot_nt(LOW[rows, :], rows_of(WF, 4, t)) * GP[rows, at].astype(F4)).astype(BF)
        for t, at in tiles(width):
            total = dot_nt(GP[rows, columns(0)], rows_of(WF, 0, t))
            for b in range(1, hidden // SIDE): total = total + dot_nt(GP[rows, columns(b)], rows_of(WF, b, t))
            AFT[rows, at] = total
        unit, scale = normalize(RR[sec, rows, :])
        grad = AFT[rows, :]
        add_norm_grads(1 + sec, grad, unit)
        D[rows, :] = D[rows, :] + norm_back(grad, unit, scale, gain_at(1 + sec))
        @pl.when(dec)
        def _():
            LOWC[rows, :] = D[rows, :].astype(BF)
            for t, at in tiles(width): DO[rows, at] = dot_nt(LOWC[rows, :], rows_of(WR, 5, t)).astype(BF)
            attention_back(m, DO, CQ, 0, KV, 0, KV, width, PT2, DCQ, 0, DKV, 0, DKV, width)
            for t, at in tiles(width): DST[rows, at] = dot_nt(DKV[rows, :], WC0[at, :]).astype(BF)
            ds_copy(m).start()
            if not direct:
                @pl.when(m == 1)
                def _():
                    for i in (0, 1): dk_copy(i).start()
            for t, at in tiles(width): AFT[rows, at] = dot_nt(DCQ[rows, :], rows_of(WR, 4, t))
            unit, scale = normalize(RR[0, rows, :])
            grad = AFT[rows, :]
            add_norm_grads(1, grad, unit)
            D[rows, :] = D[rows, :] + norm_back(grad, unit, scale, gain_at(1))
        @pl.when(enc & (m == 0))
        def _(): bottom(m)
    loop(0, 2, middle)

    part = 16 * n
    far = n // 2
    other_rows = ds((1 - core) * 2 * part, 2 * part)
    def rows_at(d, k, c): return ds((c * 2 + d) * part + k * 16, 16)
    group = [[], []]
    for g, (G, S, R, E) in enumerate(((G0, S0, R0, WF), (G1, S1, R1, WR))):
        cuts = (0, G.shape[0] // 2, G.shape[0]) if G.shape[0] > 1 else (0, 1)
        for u, stop in zip(cuts, cuts[1:]):
            us = pl.ds(u, stop - u)
            for d in (0, 1):
                for way in (1, -1):
                    f = Flow()
                    f.way, f.far = way, far if (d == 0) == (way == 1) else far - 1
                    f.own = lambda k, G=G, d=d, us=us: G.at[us, rows_at(d, k, core), :]
                    f.sib = lambda k, S=S, d=d, us=us: S.at[us, rows_at(d, k, 0), :]
                    f.slot = lambda s, R=R, d=d, us=us, w=(1 - way) // 2: R.at[d, w, s, us]
                    f.res = lambda k, E=E, d=d, us=us: E.at[us, rows_at(d, k, core), :]
                    group[g].append(f)
    for way in (1, -1):
        f = Flow()
        f.way, f.far = way, far if way == 1 else far - 1
        f.own, f.sib, f.res = (lambda k: NG.at[core, k]), (lambda k: NS.at[k]), (lambda k: EN.at[core, k])
        f.slot = lambda s, w=(1 - way) // 2: NR.at[w, s]
        group[1].append(f)
    for i, f in enumerate(group[0] + group[1]): f.i, f.to = i, after if f.way == 1 else before

    def owner(f, steps): return lax.rem(pos + f.way * steps + n, n)
    def rs_copy(f, s): return remote(f.own(owner(f, far - s)), f.slot(s), rs_s.at[f.i, s], rs_r.at[f.i, s], f.to)
    def ag_copy(f, t):
        res = f.res(owner(f, -t))
        return remote(res, res, ag_s.at[f.i, t], ag_r.at[f.i, t], f.to)
    def sh_copy(f, t):
        res = f.res(owner(f, -t))
        return remote(res, res, sh_s.at[f.i, t], sh_r.at[f.i, t], beside)
    sib_copies = [[remote(G.at[u, other_rows], S.at[u], sib_s.at[g, u], sib_r.at[g, u], beside) for u in range(G.shape[0])]
                  for g, (G, S) in enumerate(((G0, S0), (G1, S1)))]
    sib_copies[1].append(remote(NG.at[1 - core], NS, sib_s.at[1, G1.shape[0]], sib_r.at[1, G1.shape[0]], beside))

    def reduce_round(g, s):
        for f in group[g]:
            start = far - f.far
            if isinstance(s, int) and s < start: continue
            own, sib = f.own(owner(f, far - s)), f.sib(owner(f, far - s))
            total = own[...].astype(F4) + sib[...].astype(F4)
            if not isinstance(s, int) or s > start:
                rs_copy(f, s - 1).wait_recv()
                total = total + f.slot(s - 1)[...].astype(F4)
            own[...] = total.astype(own.dtype)
            rs_copy(f, s).start()

    def settle(g):
        for f, b in zip(group[g][::2], group[g][1::2]):
            total = f.own(pos)[...].astype(F4) + f.sib(pos)[...].astype(F4)
            for side_flow in (f, b):
                rs_copy(side_flow, far - 1).wait_recv()
                total = total + side_flow.slot(far - 1)[...].astype(F4)
            f.res(pos)[...] = total.astype(f.own(pos).dtype)
            ag_copy(f, 0).start()
            ag_copy(b, 0).start()
            sh_copy(f, 0).start()

    def gather_round(g, t):
        for f in group[g]:
            if isinstance(t, int) and t > f.far: continue
            ag_copy(f, t - 1).wait_recv()
            if not isinstance(t, int) or t < f.far: ag_copy(f, t).start()
            sh_copy(f, t).start()
        for f in group[g]:
            if isinstance(t, int) and t > f.far: continue
            ag_copy(f, t - 1).wait_send()
            rs_copy(f, far - t).wait_send()

    def begin(g):
        for u, copy in enumerate(sib_copies[g]):
            if direct and g == 1 and u in (4, 5): pl.when(dec)(copy.wait_recv)
            else: copy.wait_recv()
        if direct and g == 1: pl.when(enc)(cg_copy.wait_recv)
        reduce_round(g, 0)

    def done_blocks(g, G, count):
        per = G.shape[1] // SIDE
        for u in range(G.shape[0]):
            if count == min((u + 1) * per, (8, 6)[g]): sib_copies[g][u].start()

    def weight_grads(g, G, source, grad, count, b0):
        T[...] = source[...].T
        for b in range(count):
            block(G, b0 + b)[...] = dot(T[...], grad[:, columns(b)]).astype(BF)
            done_blocks(g, G, b0 + b + 1)

    own_rows = ds(core * (SIDE // 2), SIDE // 2)
    cg_trade = remote(CG.at[:, ds((1 - core) * (SIDE // 2), SIDE // 2)], CS, cg_s.at[0], cg_r.at[0], beside)
    cg_copy = remote(CG.at[:, own_rows], G1.at[pl.ds(4, 2), own_rows], cg_s.at[1], cg_r.at[1], partner) if direct else None
    if direct:
        @pl.when(dec)
        def _():
            T[...] = ST[...].T
            for b in range(2): CG[b] = dot(T[...], DKV[:, columns(b)]).astype(BF)
            cg_trade.start()
        @pl.when(enc)
        def _(): S1[pl.ds(4, 2)] = jnp.zeros((2, SIDE // 2, SIDE), BF)
    weight_grads(0, G0, N2, GP, 4, 0)
    if direct:
        @pl.when(dec)
        def _():
            cg_trade.wait_recv()
            CG[:, own_rows, :] = (CG[:, own_rows, :].astype(F4) + CS[...].astype(F4)).astype(BF)
            cg_copy.start()
    for b in range(4):
        block(G0, 4 + b)[...] = dot(A[:, columns(b)].T, LOW[...]).astype(BF)
        done_blocks(0, G0, 4 + b + 1)
    first_left = jnp.where(enc, 1, 0)

    def start_ring(m, place):
        @pl.when(m == first_left)
        def _(): begin(0) if place == 0 else reduce_round(0, 1)
    loop(first_left, 2, lambda m: bottom(m, start_ring))
    NG[...] = jnp.zeros_like(NG)
    for j in range(4):
        NG[0, j] = PG[:, 128 * j:128 * (j + 1)]
        NG[1, j] = PB[:, 128 * j:128 * (j + 1)]
    sib_copies[1][-1].start()
    weight_grads(1, G1, H1, DQKV, 3, 0)
    weight_grads(1, G1, O, LOWS, 1, 3)
    if not direct:
        @pl.when(enc)
        def _():
            for m in (0, 1): dk_copy(m).wait_recv()
            T[...] = ST[...].T
            for b in range(2): block(G1, 4 + b)[...] = dot(T[...], DKV[:, columns(b)]).astype(BF)
    @pl.when(dec)
    def _():
        for b, (source, grad) in enumerate(((HQ, DCQ), (O2, LOWC))):
            T[...] = source[...].T
            block(G1, 4 + b)[...] = dot(T[...], grad[...]).astype(BF)
            if direct: done_blocks(1, G1, 5 + b)
    if not direct: done_blocks(1, G1, 6)
    begin(1)
    if far == 4:
        reduce_round(0, 2)
        reduce_round(1, 1)
        reduce_round(0, 3)
        reduce_round(1, 2)
        settle(0)
        reduce_round(1, 3)
        gather_round(0, 1)
        settle(1)
        gather_round(0, 2)
        gather_round(1, 1)
        gather_round(0, 3)
        gather_round(1, 2)
        gather_round(0, 4)
        gather_round(1, 3)
        gather_round(1, 4)
    else:
        reduce_round(1, 1)
        for g in (0, 1):
            loop(2, far, lambda s: reduce_round(g, s))
            settle(g)
            loop(1, far - 1, lambda t: gather_round(g, t))
            gather_round(g, far - 1)
            gather_round(g, far)
    for f in group[0] + group[1]:
        if f.way == 1: sh_copy(f, 0).wait()
        loop(1, f.far + 1, lambda t: sh_copy(f, t).wait())
    for g in (0, 1):
        for u, copy in enumerate(sib_copies[g]):
            if direct and g == 1 and u in (4, 5): pl.when(dec)(copy.wait_send)
            else: copy.wait_send()

    @pl.when(enc)
    def _():
        wc_copy.wait_send()
        for m in (0, 1): st_copy(m).wait_send()
    @pl.when(dec)
    def _():
        for trade in wc_trades: trade.wait_send()
        for m in (0, 1):
            ds_copy(m).wait_send()
            if not direct: dk_copy(m).wait_send()
        if direct:
            cg_trade.wait_send()
            cg_copy.wait_send()


def finish_kernel(e0, e1, en, out, gin, o_out, o_gin, o_qkv, o_wo, o_up, o_down, o_cross, o_gain, o_bias, F, sem, sem2):
    copies = [pltpu.make_async_copy(out, o_out, sem2.at[0]), pltpu.make_async_copy(gin, o_gin, sem2.at[1])]
    for copy in copies: copy.start()
    for j in range(4):
        at = pl.ds(128 * j, 128)
        for i in range(3):
            o_gain[i, :, at] = en[0, j, i:i + 1, :]
            o_bias[i, :, at] = en[1, j, i:i + 1, :]
    def columns(b): return pl.ds(b * SIDE, SIDE)
    targets = [(e0, b, o_up.at[0, :, columns(b)]) for b in range(4)] + [(e0, 4 + b, o_down.at[0, columns(b), :]) for b in range(4)]
    targets += [(e1, b, o_qkv.at[0, :, columns(b)]) for b in range(3)] + [(e1, 3, o_wo.at[0])]
    targets += [(e1, 4 + b, o_cross.at[0, :, columns(b)]) for b in range(2)]
    slots = F.shape[0]
    flight = []
    for i, (e, b, target) in enumerate(targets):
        if i >= slots: flight[i - slots].wait()
        F[i % slots] = block(e, b)[...].astype(F4)
        flight.append(pltpu.make_async_copy(F.at[i % slots], target, sem.at[i % slots]))
        flight[-1].start()
    for copy in flight[-slots:] + copies: copy.wait()


def layers(lens, x, ct, wq, wo, w1, w2, wc, gn, bs, n):
    micro, length, width = x.shape
    rows, hidden = micro * length, w1.shape[1]
    any_ = pl.BlockSpec(memory_space=pl.ANY)
    vmem = pl.BlockSpec(memory_space=pltpu.VMEM)
    V, DMA = pltpu.VMEM, pltpu.SemaphoreType.DMA
    def units(count): return (-(-count * SIDE // (64 * n)), 64 * n, SIDE)
    s0, s1 = units(8), units(6)
    norm = (2, n, 8, 128)
    def own(s): return (s[0], s[1] // 2, SIDE)
    def slots(s): return (2, 2, n // 2, s[0], 16, SIDE)
    sq = V((rows, width), BF)
    probs = V((micro * width // 64, length, length), BF)
    scratch = [V(x.shape, BF), V(x.shape, BF), V(wc.shape, BF), V(gn.shape, F4), V(bs.shape, F4)]
    scratch += [sq, V((rows, 3 * width), BF), probs, sq, V((2, rows, width), F4), sq, sq, sq, V((rows, 2 * width), BF), probs, sq, sq,
                V((rows, hidden), BF), V((rows, hidden), BF), V((rows, width), F4), V((rows, width), F4),
                sq, sq, sq, sq, V((rows, 3 * width), BF), sq, V((rows, 2 * width), BF), sq, V((width, rows), BF)]
    scratch += [V(s0, BF), V(s1, BF), V(norm, F4), V((2, SIDE, SIDE), BF), V((2, SIDE // 2, SIDE), BF), V(own(s0), BF), V(own(s1), BF), V(norm[1:], F4), V(slots(s0), BF), V(slots(s1), BF), V((2, n // 2, 8, 128), F4),
                V((8, width), F4), V((8, width), F4)]
    scratch += [DMA((18,)), DMA, DMA, DMA((3,)), DMA((3,)), DMA((2,)), DMA((2,)), DMA((2,)), DMA((2,)), DMA((2,)), DMA((2,)), DMA((2,)), DMA((2,)), DMA((2, 9)), DMA((2, 9))] + [DMA((18 if s0[0] > 1 else 10, n // 2 + 1))] * 6
    results = [V(s0, BF), V(s1, BF), V(norm, F4), V(x.shape, BF), V(x.shape, BF)]
    e0, e1, en, out, gin = pl.pallas_call(
        functools.partial(layers_kernel, n), out_shape=results,
        in_specs=[pl.BlockSpec(memory_space=pltpu.SMEM)] + [any_] * 9, out_specs=[vmem] * 5, scratch_shapes=scratch,
        compiler_params=pltpu.CompilerParams(collective_id=1, has_side_effects=True, vmem_limit_bytes=54 * 2**20),
        name="layers",
    )(lens, x, ct, wq, wo, w1, w2, wc, gn, bs)
    def f4(*shape): return jax.ShapeDtypeStruct(shape, F4)
    return pl.pallas_call(
        finish_kernel,
        out_shape=[jax.ShapeDtypeStruct(x.shape, BF)] * 2 + [f4(1, width, 3 * width), f4(1, width, width), f4(1, width, hidden), f4(1, hidden, width),
                                                            f4(1, width, 2 * width), f4(3, 1, width), f4(3, 1, width)],
        in_specs=[vmem] * 5, out_specs=[any_] * 7 + [vmem] * 2,
        scratch_shapes=[V((4, SIDE, SIDE), F4), DMA((4,)), DMA((2,))],
        compiler_params=pltpu.CompilerParams(vmem_limit_bytes=6 * 2**20),
        name="finish",
    )(e0, e1, en, out, gin)


def local(layer_input, lengths, attn_qkv, attn_out, ffn_in, ffn_out, cross_weight, norm_gain, norm_bias, cotangent):
    def flat(a): return a.reshape(a.shape[1:])
    n = lax.axis_size("dp") // 2
    data = (layer_input.shape[1],) + layer_input.shape[3:]
    out, gin, *grads, gain, bias = layers(lengths.T, layer_input.reshape(data), cotangent.reshape(data), flat(attn_qkv), flat(attn_out), flat(ffn_in), flat(ffn_out),
                              flat(cross_weight), norm_gain.transpose(1, 0, 2), norm_bias.transpose(1, 0, 2), n)
    return (out.reshape(layer_input.shape), gin.reshape(layer_input.shape), *grads, gain.transpose(1, 0, 2), bias.transpose(1, 0, 2))


def solution(mesh):
    data = P("section", None, "dp", None, None)
    weight = P("section", None, None)
    return jax.shard_map(
        local, mesh=mesh,
        in_specs=(data, P(None, "dp")) + (weight,) * 7 + (data,),
        out_specs=(data, data) + (weight,) * 7,
        check_vma=False,
    )
```

```python
import functools

import jax
import jax.numpy as jnp
from jax import lax
from jax.experimental import pallas as pl
from jax.experimental.pallas import tpu as pltpu
from jax.sharding import PartitionSpec as P

MESH = pl.DeviceIdType.MESH
BF = jnp.bfloat16
F4 = jnp.float32
SIDE = 512
TILE = 256


def dot(a, b):
    return jnp.dot(a, b, preferred_element_type=F4)


def dot_nt(a, b):
    return lax.dot_general(a, b, (((1,), (1,)), ((), ())), preferred_element_type=F4)


def gelu_parts(u):
    size = jnp.abs(u)
    t = 1.0 / (1.0 + (0.3275911 * 0.5 ** 0.5) * size)
    bell = jnp.exp(-0.5 * u * u)
    poly = t * (0.127414796 + t * (-0.142248368 + t * (0.7107068705 + t * (-0.7265760135 + t * 0.5307027145))))
    tail = poly * bell
    cdf = jnp.where(u >= 0, 1.0 - tail, tail)
    return u * cdf, cdf + u * bell * 0.3989422804014327


def normalize(value):
    center = value - jnp.mean(value, axis=-1, keepdims=True)
    spread = jnp.mean(center * center, axis=-1, keepdims=True)
    scale = lax.rsqrt(spread + 1e-05)
    return center * scale, scale


def norm_back(grad, unit, scale, gain):
    inner = grad * gain
    mean = jnp.mean(inner, axis=-1, keepdims=True)
    along = jnp.mean(inner * unit, axis=-1, keepdims=True)
    return scale * (inner - mean - unit * along)


def loop(start, stop, body, unroll=1):
    lax.fori_loop(start, stop, lambda i, carry: (body(i), carry)[1], 0, unroll=unroll)


def ds(start, size):
    return pl.ds(pl.multiple_of(start, size), size)


def block(ref, b):
    rows = ref.shape[1]
    return ref.at[b * SIDE // rows, pl.ds(b * SIDE % rows, SIDE)]


def remote(src, dst, ss, rs, to):
    return pltpu.make_async_remote_copy(src_ref=src, dst_ref=dst, send_sem=ss, recv_sem=rs, device_id=to, device_id_type=MESH)


class Flow:
    pass


def layers_kernel(n, lens, x, ct, wq, wo, w1, w2, wc, gn, bs,
                  WF, WR, EN, OUT, GIN,
                  X, CT, WC0, GN, BS, H1, QKV, PT, O, RR, ST, HQ, CQ, KV, PT2, O2, N2, A, GP, AFT, D, LOW, LOWC, LOWS, DO, DQKV, DCQ, DKV, DST, T,
                  G0, G1, NG, CG, CS, S0, S1, NS, R0, R1, NR, PG, PB,
                  ld, wc_s, wc_r, wh_s, wh_r, st_s, st_r, ds_s, ds_r, dk_s, dk_r, cg_s, cg_r,
                  sib_s, sib_r, rs_s, rs_r, ag_s, ag_r, sh_s, sh_r):
    sec, dp = lax.axis_index("section"), lax.axis_index("dp")
    core, chip = lax.rem(dp, 2), dp // 2
    side, line = lax.rem(chip, 2), chip // 2
    pos = jnp.where(side == 0, line, n - 1 - line)

    def ring_at(q):
        q = lax.rem(q + n, n)
        return (jnp.where(q < n // 2, q, n - 1 - q) * 2 + jnp.where(q < n // 2, 0, 1)) * 2 + core

    sibling = dp + 1 - 2 * core
    partner, beside, after, before = (1 - sec, dp), (sec, sibling), (sec, ring_at(pos + 1)), (sec, ring_at(pos - 1))
    across = (sec, dp + 2 - 4 * side)
    enc, dec = sec == 0, sec == 1
    direct = 64 * n == SIDE
    length, width = X.shape[1], X.shape[2]
    hidden = A.shape[1]
    heads = width // 64
    pairs = heads // 2

    loads = {}

    def load(name, src, dst):
        loads.setdefault(name, []).append(pltpu.make_async_copy(src, dst, ld.at[sum(map(len, loads.values()))]))
        loads[name][-1].start()

    def columns(b): return pl.ds(b * SIDE, SIDE)
    load("first", x, X)
    load("first", gn, GN)
    load("first", bs, BS)
    for b in range(3): load("first", wq.at[:, columns(b)], block(WR, b))
    load("first", wo, block(WR, 3))
    for b in range(4): load("ffn", w1.at[:, columns(b)], block(WF, b))
    for b in range(4): load("ffn", w2.at[columns(b), :], block(WF, 4 + b))
    for b in range(2): load("cross", wc.at[:, columns(b)], block(WR, 4 + b))
    load("cross", ct, CT)

    def arrived(name):
        for copy in loads[name]: copy.wait()

    bar = pltpu.get_barrier_semaphore()
    for target in (partner, beside, after, before, across):
        pl.semaphore_signal(bar, inc=1, device_id=target, device_id_type=MESH)
    pl.semaphore_wait(bar, 5)

    def quarter(x, c): return WC0.at[ds((2 * x + c) * (width // 4), width // 4)]
    wc_copy = remote(wc.at[ds((2 * side + core) * (width // 4), width // 4)], quarter(side, core), wc_s, wc_r, partner)
    wc_trades = [remote(quarter(side, core), quarter(side, core), wh_s.at[0], wh_r.at[0], across),
                 remote(quarter(side, core), quarter(side, core), wh_s.at[1], wh_r.at[1], beside),
                 remote(quarter(1 - side, core), quarter(1 - side, core), wh_s.at[2], wh_r.at[2], beside)]

    def mrows(m): return ds(m * length, length)
    def st_copy(m): return remote(ST.at[mrows(m)], ST.at[mrows(m)], st_s.at[m], st_r.at[m], partner)
    def ds_copy(m): return remote(DST.at[mrows(m)], DST.at[mrows(m)], ds_s.at[m], ds_r.at[m], partner)
    def dk_copy(m): return remote(DKV.at[mrows(m)], DKV.at[mrows(m)], dk_s.at[m], dk_r.at[m], partner)

    @pl.when(enc)
    def _(): wc_copy.start()

    PG[...] = jnp.zeros_like(PG)
    PB[...] = jnp.zeros_like(PB)

    def gain_at(i): return GN[i]
    def bias_at(i): return BS[i]

    def add_norm_grads(i, grad, unit):
        at = pl.ds(i, 1)
        PG[at, :] = PG[at, :] + jnp.sum(grad * unit, axis=0, keepdims=True)
        PB[at, :] = PB[at, :] + jnp.sum(grad, axis=0, keepdims=True)

    lane_low = lax.broadcasted_iota(jnp.int32, (length, 128), 1) < 64
    lane_row = lax.broadcasted_iota(jnp.int32, (1, 128), 1) < 64
    head_masks = (jnp.where(lane_row, 1.0, 0.0).astype(BF), jnp.where(lane_row, 0.0, 1.0).astype(BF))
    query_masks = (jnp.where(lane_row, 0.125, 0.0).astype(BF), jnp.where(lane_row, 0.0, 0.125).astype(BF))

    def attention(m, q, q0, k, k0, v, v0, P, out_ref):
        rows = mrows(m)
        usable = lax.broadcasted_iota(jnp.int32, (length, length), 0) < lens[0, m]
        def cols(c0, j): return pl.ds(c0 + j * 128, 128)
        def score(h):
            j, e = h // 2, h % 2
            return dot_nt(k[rows, cols(k0, j)], q[rows, cols(q0, j)] * query_masks[e])
        def soft(s, h):
            s = jnp.where(usable, s, -1e30)
            w = jnp.exp(s - jnp.max(s, axis=0, keepdims=True))
            p = (w * (1.0 / jnp.sum(w, axis=0, keepdims=True))).astype(BF)
            P[m * heads + h] = p
        for h in range(heads): soft(score(h), h)
        for j in range(pairs):
            vt = v[rows, cols(v0, j)].T
            parts = [dot(vt[64 * e:64 * (e + 1)], P[m * heads + 2 * j + e]) for e in (0, 1)]
            out_ref[rows, cols(0, j)] = jnp.concatenate(parts, axis=0).T.astype(BF)

    def attention_back(m, do, q, q0, k, k0, v, v0, P, dq, dq0, dk, dk0, dv, dv0):
        rows = mrows(m)
        def cols(c0, j): return pl.ds(c0 + j * 128, 128)
        def weights(h): return P.at[m * heads + h]
        def grad_scores(h):
            j, e = h // 2, h % 2
            pf = weights(h)[...].astype(F4)
            t = pf * dot_nt(v[rows, cols(v0, j)], do[rows, cols(0, j)] * head_masks[e])
            return (t - pf * jnp.sum(t, axis=0, keepdims=True)).astype(BF)
        def put_v(j):
            do2 = do[rows, cols(0, j)]
            dv[rows, cols(dv0, j)] = jnp.where(lane_low, dot(weights(2 * j)[...], do2), dot(weights(2 * j + 1)[...], do2)).astype(BF)
        def put_k(j):
            q2 = q[rows, cols(q0, j)]
            dk[rows, cols(dk0, j)] = (jnp.where(lane_low, dot(weights(2 * j)[...], q2), dot(weights(2 * j + 1)[...], q2)) * 0.125).astype(BF)
        def put_q(j):
            kt = k[rows, cols(k0, j)].T
            parts = [dot(kt[64 * e:64 * (e + 1)], weights(2 * j + e)[...]) for e in (0, 1)]
            dq[rows, cols(dq0, j)] = (jnp.concatenate(parts, axis=0).T * 0.125).astype(BF)
        for j in range(pairs):
            put_v(j)
            for h in (2 * j, 2 * j + 1): weights(h)[...] = grad_scores(h)
        for j in range(pairs):
            put_k(j)
            put_q(j)

    def tiles(count): return [(t, pl.ds(t * TILE, TILE)) for t in range(count // TILE)]
    def tile_of(ref, b0, t): return block(ref, b0 + t * TILE // SIDE)[:, pl.ds(t * TILE % SIDE, TILE)]
    def rows_of(ref, b0, t): return block(ref, b0 + t * TILE // SIDE)[pl.ds(t * TILE % SIDE, TILE), :]

    def norm_into(source, m, index, target):
        rows = mrows(m)
        unit, _ = normalize(source[rows, :])
        target[rows, :] = (unit * gain_at(index) + bias_at(index)).astype(BF)

    def self_forward(m):
        rows = mrows(m)
        unit, _ = normalize(X[m].astype(F4))
        H1[rows, :] = (unit * gain_at(0) + bias_at(0)).astype(BF)
        for t, at in tiles(3 * width): QKV[rows, at] = dot(H1[rows, :], tile_of(WR, 0, t)).astype(BF)
        attention(m, QKV, 0, QKV, width, QKV, 2 * width, PT, O)
        for t, at in tiles(width): RR[0, rows, at] = dot(O[rows, :], tile_of(WR, 3, t)) + X[m, :, at].astype(F4)

    def ffn_forward(m, source, index):
        rows = mrows(m)
        norm_into(source, m, index, N2)
        for t, at in tiles(hidden):
            A[rows, at], GP[rows, at] = (part.astype(BF) for part in gelu_parts(dot(N2[rows, :], tile_of(WF, 0, t))))
        for t, at in tiles(width):
            total = source[rows, at]
            for b in range(hidden // SIDE): total = total + dot(A[rows, columns(b)], tile_of(WF, 4 + b, t))
            AFT[rows, at] = total

    arrived("first")

    def front(m):
        self_forward(m)
        @pl.when(enc)
        def _():
            @pl.when(m == 0)
            def _(): arrived("ffn")
            ffn_forward(m, RR.at[0], 1)
            norm_into(AFT, m, 2, ST)
            st_copy(m).start()
            OUT[m] = ST[mrows(m), :]
    loop(0, 2, front)
    arrived("cross")

    @pl.when(dec)
    def _():
        arrived("ffn")
        wc_copy.wait_recv()
        wc_trades[0].start()
        wc_trades[1].start()
        for m in (0, 1):
            norm_into(RR.at[0], m, 1, HQ)
            for t, at in tiles(width): CQ[mrows(m), at] = dot(HQ[mrows(m), :], tile_of(WR, 4, t)).astype(BF)
        wc_trades[0].wait_recv()
        wc_trades[2].start()
        wc_trades[1].wait_recv()
        wc_trades[2].wait_recv()

    def bottom(m, hook=None):
        rows = mrows(m)
        LOWS[rows, :] = D[rows, :].astype(BF)
        for t, at in tiles(width): DO[rows, at] = dot_nt(LOWS[rows, :], rows_of(WR, 3, t)).astype(BF)
        if hook is not None: hook(m, 0)
        attention_back(m, DO, QKV, 0, QKV, width, QKV, 2 * width, PT, DQKV, 0, DQKV, width, DQKV, 2 * width)
        if hook is not None: hook(m, 1)
        for t, at in tiles(width):
            total = dot_nt(DQKV[rows, columns(0)], rows_of(WR, 0, t))
            for b in (1, 2): total = total + dot_nt(DQKV[rows, columns(b)], rows_of(WR, b, t))
            AFT[rows, at] = total
        unit, scale = normalize(X[m].astype(F4))
        grad = AFT[rows, :]
        add_norm_grads(0, grad, unit)
        GIN[m] = (D[rows, :] + norm_back(grad, unit, scale, gain_at(0))).astype(BF)

    def middle(m):
        rows = mrows(m)
        @pl.when(enc)
        def _():
            ds_copy(m).wait_recv()
            unit, scale = normalize(AFT[rows, :])
            grad = CT[m].astype(F4) + DST[rows, :].astype(F4)
            add_norm_grads(2, grad, unit)
            back = norm_back(grad, unit, scale, gain_at(2))
            D[rows, :] = back
            LOW[rows, :] = back.astype(BF)
        @pl.when(dec)
        def _():
            st_copy(m).wait_recv()
            for t, at in tiles(2 * width): KV[rows, at] = dot(ST[rows, :], WC0[:, at]).astype(BF)
            attention(m, CQ, 0, KV, 0, KV, width, PT2, O2)
            for t, at in tiles(width): RR[1, rows, at] = dot(O2[rows, :], tile_of(WR, 5, t)) + RR[0, rows, at]
            ffn_forward(m, RR.at[1], 2)
            OUT[m] = AFT[rows, :].astype(BF)
            D[rows, :] = CT[m].astype(F4)
            LOW[rows, :] = CT[m]
        for t, at in tiles(hidden): GP[rows, at] = (dot_nt(LOW[rows, :], rows_of(WF, 4, t)) * GP[rows, at].astype(F4)).astype(BF)
        for t, at in tiles(width):
            total = dot_nt(GP[rows, columns(0)], rows_of(WF, 0, t))
            for b in range(1, hidden // SIDE): total = total + dot_nt(GP[rows, columns(b)], rows_of(WF, b, t))
            AFT[rows, at] = total
        unit, scale = normalize(RR[sec, rows, :])
        grad = AFT[rows, :]
        add_norm_grads(1 + sec, grad, unit)
        D[rows, :] = D[rows, :] + norm_back(grad, unit, scale, gain_at(1 + sec))
        @pl.when(dec)
        def _():
            LOWC[rows, :] = D[rows, :].astype(BF)
            for t, at in tiles(width): DO[rows, at] = dot_nt(LOWC[rows, :], rows_of(WR, 5, t)).astype(BF)
            attention_back(m, DO, CQ, 0, KV, 0, KV, width, PT2, DCQ, 0, DKV, 0, DKV, width)
            for t, at in tiles(width): DST[rows, at] = dot_nt(DKV[rows, :], WC0[at, :]).astype(BF)
            ds_copy(m).start()
            if not direct:
                @pl.when(m == 1)
                def _():
                    for i in (0, 1): dk_copy(i).start()
            for t, at in tiles(width): AFT[rows, at] = dot_nt(DCQ[rows, :], rows_of(WR, 4, t))
            unit, scale = normalize(RR[0, rows, :])
            grad = AFT[rows, :]
            add_norm_grads(1, grad, unit)
            D[rows, :] = D[rows, :] + norm_back(grad, unit, scale, gain_at(1))
        @pl.when(enc & (m == 0))
        def _(): bottom(m)
    loop(0, 2, middle)

    far = n // 2
    def half_rows(c): return ds(c * 32 * n, 32 * n)
    def rows_at(k, c, lo, count): return pl.ds(pl.multiple_of(c * 32 * n + k * 32 + lo, 16), count)
    group = [[], []]
    for g, (G, S, R, E) in enumerate(((G0, S0, R0, WF), (G1, S1, R1, WR))):
        cuts = (0, G.shape[0] // 2, G.shape[0]) if G.shape[0] > 1 else (0, 1)
        for sub, (u, stop) in enumerate(zip(cuts, cuts[1:])):
            us = pl.ds(u, stop - u)
            for way in (1, -1):
                f = Flow()
                f.way, f.norm, f.g, f.sub = way, False, g, sub
                f.own = lambda k, lo, count, G=G, us=us: G.at[us, rows_at(k, core, lo, count), :]
                f.sib = lambda k, lo, count, S=S, us=us: S.at[us, rows_at(k, 0, lo, count), :]
                f.slot = lambda s, lo, count, R=R, us=us, w=(1 - way) // 2: R.at[w, s, us, pl.ds(lo, count)]
                f.res = lambda k, lo, count, E=E, us=us: E.at[us, rows_at(k, core, lo, count), :]
                group[g].append(f)
    for way in (1, -1):
        f = Flow()
        f.way, f.norm, f.g, f.sub = way, True, 2, 2
        f.own, f.sib, f.res = (lambda k, *_: NG.at[core, k]), (lambda k, *_: NS.at[k]), (lambda k, *_: EN.at[core, k])
        f.slot = lambda s, *_, w=(1 - way) // 2: NR.at[w, s]
        group[1].append(f)
    for i, f in enumerate(group[0] + group[1]): f.i, f.to, f.lo = i, after if f.way == 1 else before, 0 if f.way == 1 else 16

    def owner(f, steps): return lax.rem(pos + f.way * steps + n, n)
    def piece(f, outer): return (f.lo, 16) if outer else (0, 32)
    def rs_copy(f, s):
        at = piece(f, isinstance(s, int) and s == 0)
        return remote(f.own(owner(f, far - s), *at), f.slot(s, *at), rs_s.at[f.g], rs_r.at[f.i, s], f.to)
    def ag_piece(f, t): return piece(f, isinstance(t, int) and t == far - 1)
    def ag_copy(f, t):
        res = f.res(owner(f, -t), *ag_piece(f, t))
        return remote(res, res, ag_s.at[f.g], ag_r.at[f.i, t], f.to)
    def sh_start(f, t, at):
        res = f.res(owner(f, -t), *at)
        remote(res, res, sh_s.at[f.g], sh_r.at[f.g], beside).start()

    def sib_key(g, u): return g * 3 + (0 if G0.shape[0] == 1 else u // 4 if g == 0 else (0, 0, 0, 1, 2, 2)[u])
    def sib_copy(g, u):
        G, S = ((G0, S0), (G1, S1))[g]
        return remote(G.at[u, half_rows(1 - core)], S.at[u], sib_s.at[sib_key(g, u)], sib_r.at[sib_key(g, u)], beside)
    sib_norm = remote(NG.at[1 - core], NS, sib_s.at[6], sib_r.at[6], beside)
    def sib_all(g, key):
        G, S = ((G0, S0), (G1, S1))[g]
        us = [u for u in range(G.shape[0]) if sib_key(g, u) == g * 3 + key]
        if not us: return None
        us = pl.ds(us[0], len(us))
        return remote(G.at[us, half_rows(1 - core)], S.at[us], sib_s.at[g * 3 + key], sib_r.at[g * 3 + key], beside)
    def sib_wait(g, sub):
        for key in ((0,), (1, 2))[sub]:
            copy = sib_all(g, key)
            if copy is None: continue
            if direct and g == 1 and key == 2: pl.when(dec)(copy.wait_recv)
            else: copy.wait_recv()

    def reduce_round(g, s, subs=(0, 1, 2)):
        for f in group[g]:
            if f.sub not in subs: continue
            k = owner(f, far - s)
            def partial(at, received):
                own = f.own(k, *at)
                total = own[...].astype(F4) + f.sib(k, *at)[...].astype(F4)
                if received: total = total + f.slot(s - 1, *at)[...].astype(F4)
                own[...] = total.astype(own.dtype)
            first, second = isinstance(s, int) and s == 0, isinstance(s, int) and s == 1
            if first and f.norm and f.way == -1: continue
            if not first and not (second and f.norm and f.way == -1): rs_copy(f, s - 1).wait_recv()
            if first: partial(piece(f, True), False)
            elif second and f.norm: partial((0, 32), f.way == 1)
            elif second:
                partial((f.lo, 16), True)
                partial((16 - f.lo, 16), False)
            else: partial((0, 32), True)
            rs_copy(f, s).start()

    def settle(g):
        for f, b in zip(group[g][::2], group[g][1::2]):
            total = f.own(pos, 0, 32)[...].astype(F4) + f.sib(pos, 0, 32)[...].astype(F4)
            for flow in (f, b):
                rs_copy(flow, far - 1).wait_recv()
                total = total + flow.slot(far - 1, 0, 32)[...].astype(F4)
            f.res(pos, 0, 32)[...] = total.astype(f.res(pos, 0, 32).dtype)
            ag_copy(f, 0).start()
            ag_copy(b, 0).start()
            sh_start(f, 0, (0, 32))

    def gather_round(g, t):
        for f in group[g]:
            def active(t): return not (isinstance(t, int) and f.norm and f.way == -1 and t == far - 1)
            if not active(t - 1): continue
            ag_copy(f, t - 1).wait_recv()
            if not (isinstance(t, int) and t == far) and active(t): ag_copy(f, t).start()
            sh_start(f, t, ag_piece(f, t - 1))

    def begin(g, subs=(0, 1, 2)):
        for sub in (0, 1):
            if sub in subs and (sub == 0 or G0.shape[0] > 1):
                sib_wait(g, sub)
                if direct and g == 1 and sub == 1: pl.when(enc)(cg_copy.wait_recv)
                reduce_round(g, 0, (sub,))
        if g == 1:
            sib_norm.wait_recv()
            reduce_round(1, 0, (2,))

    def close_ring():
        for g, (G, E) in enumerate(((G0, WF), (G1, WR))):
            sent = pl.ds(0, 32 * n - 32)
            remote(E.at[:, half_rows(core)], E.at[:, half_rows(1 - core)], sh_s.at[g], sh_r.at[g], beside).wait()
            remote(G.at[:, sent], G.at[:, sent], rs_s.at[g], rs_r.at[0, 0], after).wait_send()
            remote(E.at[:, sent], E.at[:, sent], ag_s.at[g], ag_r.at[0, 0], after).wait_send()
            for key in range(3):
                copy = sib_all(g, key)
                if copy is None: continue
                if direct and g == 1 and key == 2: pl.when(dec)(copy.wait_send)
                else: copy.wait_send()
        sent = pl.ds(0, n - 1)
        remote(EN.at[core], EN.at[1 - core], sh_s.at[2], sh_r.at[2], beside).wait()
        remote(NG.at[0, sent], NG.at[0, sent], rs_s.at[2], rs_r.at[0, 0], after).wait_send()
        remote(EN.at[0, sent], EN.at[0, sent], ag_s.at[2], ag_r.at[0, 0], after).wait_send()
        sib_norm.wait_send()

    def done_blocks(g, G, count):
        per = G.shape[1] // SIDE
        for u in range(G.shape[0]):
            if count == min((u + 1) * per, (8, 6)[g]): sib_copy(g, u).start()

    def weight_grads(g, G, source, grad, count, b0):
        T[...] = source[...].T
        for b in range(count):
            block(G, b0 + b)[...] = dot(T[...], grad[:, columns(b)]).astype(BF)
            done_blocks(g, G, b0 + b + 1)

    own_rows = ds(core * (SIDE // 2), SIDE // 2)
    cg_trade = remote(CG.at[:, ds((1 - core) * (SIDE // 2), SIDE // 2)], CS, cg_s.at[0], cg_r.at[0], beside)
    cg_copy = remote(CG.at[:, own_rows], G1.at[pl.ds(4, 2), own_rows], cg_s.at[1], cg_r.at[1], partner) if direct else None
    if direct:
        @pl.when(dec)
        def _():
            T[...] = ST[...].T
            for b in range(2): CG[b] = dot(T[...], DKV[:, columns(b)]).astype(BF)
            cg_trade.start()
        @pl.when(enc)
        def _(): S1[pl.ds(4, 2)] = jnp.zeros((2, SIDE // 2, SIDE), BF)
    weight_grads(0, G0, N2, GP, 4, 0)
    if direct:
        @pl.when(dec)
        def _():
            cg_trade.wait_recv()
            CG[:, own_rows, :] = (CG[:, own_rows, :].astype(F4) + CS[...].astype(F4)).astype(BF)
            cg_copy.start()
    for b in range(4):
        block(G0, 4 + b)[...] = dot(A[:, columns(b)].T, LOW[...]).astype(BF)
        done_blocks(0, G0, 4 + b + 1)
        if b == 1 and G0.shape[0] > 1: begin(0, (0,))
    first_left = jnp.where(enc, 1, 0)

    def start_ring(m, place):
        @pl.when(m == first_left)
        def _(): begin(0, (1,) if G0.shape[0] > 1 else (0,)) if place == 0 else reduce_round(0, 1)
    loop(first_left, 2, lambda m: bottom(m, start_ring))
    NG[...] = jnp.zeros_like(NG)
    for j in range(4):
        NG[0, j] = PG[:, 128 * j:128 * (j + 1)]
        NG[1, j] = PB[:, 128 * j:128 * (j + 1)]
    sib_norm.start()
    weight_grads(1, G1, H1, DQKV, 3, 0)
    weight_grads(1, G1, O, LOWS, 1, 3)
    if not direct:
        @pl.when(enc)
        def _():
            for m in (0, 1): dk_copy(m).wait_recv()
            T[...] = ST[...].T
            for b in range(2): block(G1, 4 + b)[...] = dot(T[...], DKV[:, columns(b)]).astype(BF)
    @pl.when(dec)
    def _():
        for b, (source, grad) in enumerate(((HQ, DCQ), (O2, LOWC))):
            T[...] = source[...].T
            block(G1, 4 + b)[...] = dot(T[...], grad[...]).astype(BF)
            if direct: done_blocks(1, G1, 5 + b)
    if not direct: done_blocks(1, G1, 6)
    begin(1)
    if far == 4:
        reduce_round(0, 2)
        reduce_round(1, 1)
        reduce_round(0, 3)
        reduce_round(1, 2)
        settle(0)
        reduce_round(1, 3)
        gather_round(0, 1)
        settle(1)
        gather_round(0, 2)
        gather_round(1, 1)
        gather_round(0, 3)
        gather_round(1, 2)
        gather_round(0, 4)
        gather_round(1, 3)
        gather_round(1, 4)
    else:
        reduce_round(1, 1)
        for g in (0, 1):
            loop(2, far, lambda s: reduce_round(g, s))
            settle(g)
            loop(1, far - 1, lambda t: gather_round(g, t))
            gather_round(g, far - 1)
            gather_round(g, far)
    close_ring()

    @pl.when(enc)
    def _():
        wc_copy.wait_send()
        for m in (0, 1): st_copy(m).wait_send()
    @pl.when(dec)
    def _():
        for trade in wc_trades: trade.wait_send()
        for m in (0, 1):
            ds_copy(m).wait_send()
            if not direct: dk_copy(m).wait_send()
        if direct:
            cg_trade.wait_send()
            cg_copy.wait_send()


def finish_kernel(e0, e1, en, out, gin, o_out, o_gin, o_qkv, o_wo, o_up, o_down, o_cross, o_gain, o_bias, F, sem, sem2):
    copies = [pltpu.make_async_copy(out, o_out, sem2.at[0]), pltpu.make_async_copy(gin, o_gin, sem2.at[1])]
    for copy in copies: copy.start()
    for j in range(4):
        at = pl.ds(128 * j, 128)
        for i in range(3):
            o_gain[i, :, at] = en[0, j, i:i + 1, :]
            o_bias[i, :, at] = en[1, j, i:i + 1, :]
    def columns(b): return pl.ds(b * SIDE, SIDE)
    targets = [(e0, b, o_up.at[0, :, columns(b)]) for b in range(4)] + [(e0, 4 + b, o_down.at[0, columns(b), :]) for b in range(4)]
    targets += [(e1, b, o_qkv.at[0, :, columns(b)]) for b in range(3)] + [(e1, 3, o_wo.at[0])]
    targets += [(e1, 4 + b, o_cross.at[0, :, columns(b)]) for b in range(2)]
    slots = F.shape[0]
    flight = []
    for i, (e, b, target) in enumerate(targets):
        if i >= slots: flight[i - slots].wait()
        F[i % slots] = block(e, b)[...].astype(F4)
        flight.append(pltpu.make_async_copy(F.at[i % slots], target, sem.at[i % slots]))
        flight[-1].start()
    for copy in flight[-slots:] + copies: copy.wait()


def layers(lens, x, ct, wq, wo, w1, w2, wc, gn, bs, n):
    micro, length, width = x.shape
    rows, hidden = micro * length, w1.shape[1]
    any_ = pl.BlockSpec(memory_space=pl.ANY)
    vmem = pl.BlockSpec(memory_space=pltpu.VMEM)
    V, DMA = pltpu.VMEM, pltpu.SemaphoreType.DMA
    def units(count): return (-(-count * SIDE // (64 * n)), 64 * n, SIDE)
    s0, s1 = units(8), units(6)
    norm = (2, n, 8, 128)
    def own(s): return (s[0], s[1] // 2, SIDE)
    def slots(s): return (2, n // 2, s[0], 32, SIDE)
    sq = V((rows, width), BF)
    probs = V((micro * width // 64, length, length), BF)
    scratch = [V(x.shape, BF), V(x.shape, BF), V(wc.shape, BF), V(gn.shape, F4), V(bs.shape, F4)]
    scratch += [sq, V((rows, 3 * width), BF), probs, sq, V((2, rows, width), F4), sq, sq, sq, V((rows, 2 * width), BF), probs, sq, sq,
                V((rows, hidden), BF), V((rows, hidden), BF), V((rows, width), F4), V((rows, width), F4),
                sq, sq, sq, sq, V((rows, 3 * width), BF), sq, V((rows, 2 * width), BF), sq, V((width, rows), BF)]
    scratch += [V(s0, BF), V(s1, BF), V(norm, F4), V((2, SIDE, SIDE), BF), V((2, SIDE // 2, SIDE), BF), V(own(s0), BF), V(own(s1), BF), V(norm[1:], F4), V(slots(s0), BF), V(slots(s1), BF), V((2, n // 2, 8, 128), F4),
                V((8, width), F4), V((8, width), F4)]
    scratch += [DMA((18,)), DMA, DMA, DMA((3,)), DMA((3,)), DMA((2,)), DMA((2,)), DMA((2,)), DMA((2,)), DMA((2,)), DMA((2,)), DMA((2,)), DMA((2,)), DMA((7,)), DMA((7,)), DMA((3,)), DMA((10, n // 2)), DMA((3,)), DMA((10, n // 2)), DMA((3,)), DMA((3,))]
    results = [V(s0, BF), V(s1, BF), V(norm, F4), V(x.shape, BF), V(x.shape, BF)]
    e0, e1, en, out, gin = pl.pallas_call(
        functools.partial(layers_kernel, n), out_shape=results,
        in_specs=[pl.BlockSpec(memory_space=pltpu.SMEM)] + [any_] * 9, out_specs=[vmem] * 5, scratch_shapes=scratch,
        compiler_params=pltpu.CompilerParams(collective_id=1, has_side_effects=True, vmem_limit_bytes=54 * 2**20),
        name="layers",
    )(lens, x, ct, wq, wo, w1, w2, wc, gn, bs)
    def f4(*shape): return jax.ShapeDtypeStruct(shape, F4)
    return pl.pallas_call(
        finish_kernel,
        out_shape=[jax.ShapeDtypeStruct(x.shape, BF)] * 2 + [f4(1, width, 3 * width), f4(1, width, width), f4(1, width, hidden), f4(1, hidden, width),
                                                            f4(1, width, 2 * width), f4(3, 1, width), f4(3, 1, width)],
        in_specs=[vmem] * 5, out_specs=[any_] * 7 + [vmem] * 2,
        scratch_shapes=[V((4, SIDE, SIDE), F4), DMA((4,)), DMA((2,))],
        compiler_params=pltpu.CompilerParams(vmem_limit_bytes=6 * 2**20),
        name="finish",
    )(e0, e1, en, out, gin)


def local(layer_input, lengths, attn_qkv, attn_out, ffn_in, ffn_out, cross_weight, norm_gain, norm_bias, cotangent):
    def flat(a): return a.reshape(a.shape[1:])
    n = lax.axis_size("dp") // 2
    data = (layer_input.shape[1],) + layer_input.shape[3:]
    out, gin, *grads, gain, bias = layers(lengths.T, layer_input.reshape(data), cotangent.reshape(data), flat(attn_qkv), flat(attn_out), flat(ffn_in), flat(ffn_out),
                              flat(cross_weight), norm_gain.transpose(1, 0, 2), norm_bias.transpose(1, 0, 2), n)
    return (out.reshape(layer_input.shape), gin.reshape(layer_input.shape), *grads, gain.transpose(1, 0, 2), bias.transpose(1, 0, 2))


def solution(mesh):
    data = P("section", None, "dp", None, None)
    weight = P("section", None, None)
    return jax.shard_map(
        local, mesh=mesh,
        in_specs=(data, P(None, "dp")) + (weight,) * 7 + (data,),
        out_specs=(data, data) + (weight,) * 7,
        check_vma=False,
    )
```

```python
import functools

import jax
import jax.numpy as jnp
from jax import lax
from jax.experimental import pallas as pl
from jax.experimental.pallas import tpu as pltpu
from jax.sharding import PartitionSpec as P

MESH = pl.DeviceIdType.MESH
BF = jnp.bfloat16
F4 = jnp.float32
SIDE = 512
TILE = 256


def dot(a, b):
    return jnp.dot(a, b, preferred_element_type=F4)


def dot_nt(a, b):
    return lax.dot_general(a, b, (((1,), (1,)), ((), ())), preferred_element_type=F4)


def gelu_parts(u):
    cdf = 0.5 + 0.5 * lax.erf(u * 0.5 ** 0.5)
    return u * cdf, cdf + u * (jnp.exp(-0.5 * u * u) * 0.3989422804014327)


def normalize(value):
    center = value - jnp.mean(value, axis=-1, keepdims=True)
    spread = jnp.mean(center * center, axis=-1, keepdims=True)
    scale = lax.rsqrt(spread + 1e-05)
    return center * scale, scale


def norm_back(grad, unit, scale, gain):
    inner = grad * gain
    mean = jnp.mean(inner, axis=-1, keepdims=True)
    along = jnp.mean(inner * unit, axis=-1, keepdims=True)
    return scale * (inner - mean - unit * along)


def loop(start, stop, body, unroll=1):
    lax.fori_loop(start, stop, lambda i, carry: (body(i), carry)[1], 0, unroll=unroll)


def ds(start, size):
    return pl.ds(pl.multiple_of(start, size), size)


def block(ref, b):
    rows = ref.shape[1]
    return ref.at[b * SIDE // rows, pl.ds(b * SIDE % rows, SIDE)]


def remote(src, dst, ss, rs, to):
    return pltpu.make_async_remote_copy(src_ref=src, dst_ref=dst, send_sem=ss, recv_sem=rs, device_id=to, device_id_type=MESH)


class Flow:
    pass


def layers_kernel(n, lens, x, ct, wq, wo, w1, w2, wc, gn, bs,
                  WF, WR, EN, OUT, GIN,
                  X, CT, WC0, GN, BS, H1, QKV, PT, O, RR, ST, HQ, CQ, KV, PT2, O2, N2, A, GP, AFT, D, LOW, LOWC, LOWS, DO, DQKV, DCQ, DKV, DST, T,
                  G0, G1, NG, CG, CS, S0, S1, NS, R0, R1, NR, PG, PB,
                  ld, wc_s, wc_r, wh_s, wh_r, st_s, st_r, ds_s, ds_r, dk_s, dk_r, cg_s, cg_r,
                  sib_s, sib_r, rs_s, rs_r, ag_s, ag_r, sh_s, sh_r):
    sec, dp = lax.axis_index("section"), lax.axis_index("dp")
    core, chip = lax.rem(dp, 2), dp // 2
    side, line = lax.rem(chip, 2), chip // 2
    pos = jnp.where(side == 0, line, n - 1 - line)

    def ring_at(q):
        q = lax.rem(q + n, n)
        return (jnp.where(q < n // 2, q, n - 1 - q) * 2 + jnp.where(q < n // 2, 0, 1)) * 2 + core

    sibling = dp + 1 - 2 * core
    partner, beside, after, before = (1 - sec, dp), (sec, sibling), (sec, ring_at(pos + 1)), (sec, ring_at(pos - 1))
    across = (sec, dp + 2 - 4 * side)
    enc, dec = sec == 0, sec == 1
    direct = 64 * n == SIDE
    length, width = X.shape[1], X.shape[2]
    hidden = A.shape[1]
    heads = width // 64
    pairs = heads // 2

    loads = {}

    def load(name, src, dst):
        loads.setdefault(name, []).append(pltpu.make_async_copy(src, dst, ld.at[sum(map(len, loads.values()))]))
        loads[name][-1].start()

    def columns(b): return pl.ds(b * SIDE, SIDE)
    load("first", x, X)
    load("first", gn, GN)
    load("first", bs, BS)
    for b in range(3): load("first", wq.at[:, columns(b)], block(WR, b))
    load("first", wo, block(WR, 3))
    def arrived(name):
        for copy in loads[name]: copy.wait()

    bar = pltpu.get_barrier_semaphore()
    for target in (partner, beside, after, before, across):
        pl.semaphore_signal(bar, inc=1, device_id=target, device_id_type=MESH)
    pl.semaphore_wait(bar, 5)

    def quarter(x, c): return WC0.at[ds((2 * x + c) * (width // 4), width // 4)]
    wc_copy = remote(wc.at[ds((2 * side + core) * (width // 4), width // 4)], quarter(side, core), wc_s, wc_r, partner)
    wc_trades = [remote(quarter(side, core), quarter(side, core), wh_s.at[0], wh_r.at[0], across),
                 remote(quarter(side, core), quarter(side, core), wh_s.at[1], wh_r.at[1], beside),
                 remote(quarter(1 - side, core), quarter(1 - side, core), wh_s.at[2], wh_r.at[2], beside)]

    def mrows(m): return ds(m * length, length)
    def st_copy(m): return remote(ST.at[mrows(m)], ST.at[mrows(m)], st_s.at[m], st_r.at[m], partner)
    def ds_copy(m): return remote(DST.at[mrows(m)], DST.at[mrows(m)], ds_s.at[m], ds_r.at[m], partner)
    def dk_copy(m): return remote(DKV.at[mrows(m)], DKV.at[mrows(m)], dk_s.at[m], dk_r.at[m], partner)

    @pl.when(enc)
    def _(): wc_copy.start()

    PG[...] = jnp.zeros_like(PG)
    PB[...] = jnp.zeros_like(PB)

    def gain_at(i): return GN[i]
    def bias_at(i): return BS[i]

    def add_norm_grads(i, grad, unit):
        at = pl.ds(i, 1)
        PG[at, :] = PG[at, :] + jnp.sum(grad * unit, axis=0, keepdims=True)
        PB[at, :] = PB[at, :] + jnp.sum(grad, axis=0, keepdims=True)

    lane_low = lax.broadcasted_iota(jnp.int32, (length, 128), 1) < 64
    lane_row = lax.broadcasted_iota(jnp.int32, (1, 128), 1) < 64
    head_masks = (jnp.where(lane_row, 1.0, 0.0).astype(BF), jnp.where(lane_row, 0.0, 1.0).astype(BF))
    query_masks = (jnp.where(lane_row, 0.125, 0.0).astype(BF), jnp.where(lane_row, 0.0, 0.125).astype(BF))

    def attention(m, q, q0, k, k0, v, v0, P, out_ref):
        rows = mrows(m)
        usable = lax.broadcasted_iota(jnp.int32, (length, length), 0) < lens[0, m]
        def cols(c0, j): return pl.ds(c0 + j * 128, 128)
        def score(h):
            j, e = h // 2, h % 2
            return dot_nt(k[rows, cols(k0, j)], q[rows, cols(q0, j)] * query_masks[e])
        def soft(s, h):
            s = jnp.where(usable, s, -1e30)
            w = jnp.exp(s - jnp.max(s, axis=0, keepdims=True))
            p = (w * (1.0 / jnp.sum(w, axis=0, keepdims=True))).astype(BF)
            P[m * heads + h] = p
        for h in range(heads): soft(score(h), h)
        for j in range(pairs):
            vt = v[rows, cols(v0, j)].T
            parts = [dot(vt[64 * e:64 * (e + 1)], P[m * heads + 2 * j + e]) for e in (0, 1)]
            out_ref[rows, cols(0, j)] = jnp.concatenate(parts, axis=0).T.astype(BF)

    def attention_back(m, do, q, q0, k, k0, v, v0, P, dq, dq0, dk, dk0, dv, dv0):
        rows = mrows(m)
        def cols(c0, j): return pl.ds(c0 + j * 128, 128)
        def weights(h): return P.at[m * heads + h]
        def grad_scores(h):
            j, e = h // 2, h % 2
            pf = weights(h)[...].astype(F4)
            t = pf * dot_nt(v[rows, cols(v0, j)], do[rows, cols(0, j)] * head_masks[e])
            return (t - pf * jnp.sum(t, axis=0, keepdims=True)).astype(BF)
        def put_v(j):
            do2 = do[rows, cols(0, j)]
            dv[rows, cols(dv0, j)] = jnp.where(lane_low, dot(weights(2 * j)[...], do2), dot(weights(2 * j + 1)[...], do2)).astype(BF)
        def put_k(j):
            q2 = q[rows, cols(q0, j)]
            dk[rows, cols(dk0, j)] = (jnp.where(lane_low, dot(weights(2 * j)[...], q2), dot(weights(2 * j + 1)[...], q2)) * 0.125).astype(BF)
        def put_q(j):
            kt = k[rows, cols(k0, j)].T
            parts = [dot(kt[64 * e:64 * (e + 1)], weights(2 * j + e)[...]) for e in (0, 1)]
            dq[rows, cols(dq0, j)] = (jnp.concatenate(parts, axis=0).T * 0.125).astype(BF)
        for j in range(pairs):
            put_v(j)
            for h in (2 * j, 2 * j + 1): weights(h)[...] = grad_scores(h)
        for j in range(pairs):
            put_k(j)
            put_q(j)

    def tiles(count): return [(t, pl.ds(t * TILE, TILE)) for t in range(count // TILE)]
    def tile_of(ref, b0, t): return block(ref, b0 + t * TILE // SIDE)[:, pl.ds(t * TILE % SIDE, TILE)]
    def rows_of(ref, b0, t): return block(ref, b0 + t * TILE // SIDE)[pl.ds(t * TILE % SIDE, TILE), :]

    def norm_into(source, m, index, target):
        rows = mrows(m)
        unit, _ = normalize(source[rows, :])
        target[rows, :] = (unit * gain_at(index) + bias_at(index)).astype(BF)

    def self_forward(m):
        rows = mrows(m)
        unit, _ = normalize(X[m].astype(F4))
        H1[rows, :] = (unit * gain_at(0) + bias_at(0)).astype(BF)
        for t, at in tiles(3 * width): QKV[rows, at] = dot(H1[rows, :], tile_of(WR, 0, t)).astype(BF)
        attention(m, QKV, 0, QKV, width, QKV, 2 * width, PT, O)
        for t, at in tiles(width): RR[0, rows, at] = dot(O[rows, :], tile_of(WR, 3, t)) + X[m, :, at].astype(F4)

    def ffn_forward(m, source, index):
        rows = mrows(m)
        norm_into(source, m, index, N2)
        for t, at in tiles(hidden):
            A[rows, at], GP[rows, at] = (part.astype(BF) for part in gelu_parts(dot(N2[rows, :], tile_of(WF, 0, t))))
        for t, at in tiles(width):
            total = source[rows, at]
            for b in range(hidden // SIDE): total = total + dot(A[rows, columns(b)], tile_of(WF, 4 + b, t))
            AFT[rows, at] = total

    arrived("first")
    for b in range(4): load("ffn", w1.at[:, columns(b)], block(WF, b))
    for b in range(4): load("ffn", w2.at[columns(b), :], block(WF, 4 + b))
    for b in range(2): load("cross", wc.at[:, columns(b)], block(WR, 4 + b))
    load("cross", ct, CT)

    def front(m):
        self_forward(m)
        @pl.when(enc)
        def _():
            @pl.when(m == 0)
            def _(): arrived("ffn")
            ffn_forward(m, RR.at[0], 1)
            norm_into(AFT, m, 2, ST)
            st_copy(m).start()
            OUT[m] = ST[mrows(m), :]
    loop(0, 2, front)
    arrived("cross")

    @pl.when(dec)
    def _():
        arrived("ffn")
        wc_copy.wait_recv()
        wc_trades[0].start()
        wc_trades[1].start()
        for m in (0, 1):
            norm_into(RR.at[0], m, 1, HQ)
            for t, at in tiles(width): CQ[mrows(m), at] = dot(HQ[mrows(m), :], tile_of(WR, 4, t)).astype(BF)
        wc_trades[0].wait_recv()
        wc_trades[2].start()
        wc_trades[1].wait_recv()
        wc_trades[2].wait_recv()

    def bottom(m, hook=None):
        rows = mrows(m)
        LOWS[rows, :] = D[rows, :].astype(BF)
        for t, at in tiles(width): DO[rows, at] = dot_nt(LOWS[rows, :], rows_of(WR, 3, t)).astype(BF)
        if hook is not None: hook(m, 0)
        attention_back(m, DO, QKV, 0, QKV, width, QKV, 2 * width, PT, DQKV, 0, DQKV, width, DQKV, 2 * width)
        if hook is not None: hook(m, 1)
        for t, at in tiles(width):
            total = dot_nt(DQKV[rows, columns(0)], rows_of(WR, 0, t))
            for b in (1, 2): total = total + dot_nt(DQKV[rows, columns(b)], rows_of(WR, b, t))
            AFT[rows, at] = total
        unit, scale = normalize(X[m].astype(F4))
        grad = AFT[rows, :]
        add_norm_grads(0, grad, unit)
        GIN[m] = (D[rows, :] + norm_back(grad, unit, scale, gain_at(0))).astype(BF)

    first, second = pl.ds(0, length), pl.ds(length, length)

    def middle(m):
        rows = mrows(m)
        @pl.when(enc)
        def _():
            ds_copy(m).wait_recv()
            unit, scale = normalize(AFT[rows, :])
            grad = CT[m].astype(F4) + DST[rows, :].astype(F4)
            add_norm_grads(2, grad, unit)
            back = norm_back(grad, unit, scale, gain_at(2))
            D[rows, :] = back
            LOW[rows, :] = back.astype(BF)
        @pl.when(dec)
        def _():
            st_copy(m).wait_recv()
            for t, at in tiles(2 * width): KV[rows, at] = dot(ST[rows, :], WC0[:, at]).astype(BF)
            attention(m, CQ, 0, KV, 0, KV, width, PT2, O2)
            for t, at in tiles(width): RR[1, rows, at] = dot(O2[rows, :], tile_of(WR, 5, t)) + RR[0, rows, at]
            ffn_forward(m, RR.at[1], 2)
            OUT[m] = AFT[rows, :].astype(BF)
            D[rows, :] = CT[m].astype(F4)
            LOW[rows, :] = CT[m]
        for t, at in tiles(hidden): GP[rows, at] = (dot_nt(LOW[rows, :], rows_of(WF, 4, t)) * GP[rows, at].astype(F4)).astype(BF)
        for t, at in tiles(width):
            total = dot_nt(GP[rows, columns(0)], rows_of(WF, 0, t))
            for b in range(1, hidden // SIDE): total = total + dot_nt(GP[rows, columns(b)], rows_of(WF, b, t))
            AFT[rows, at] = total
        unit, scale = normalize(RR[sec, rows, :])
        grad = AFT[rows, :]
        add_norm_grads(1 + sec, grad, unit)
        D[rows, :] = D[rows, :] + norm_back(grad, unit, scale, gain_at(1 + sec))
        @pl.when(dec)
        def _():
            LOWC[rows, :] = D[rows, :].astype(BF)
            for t, at in tiles(width): DO[rows, at] = dot_nt(LOWC[rows, :], rows_of(WR, 5, t)).astype(BF)
            attention_back(m, DO, CQ, 0, KV, 0, KV, width, PT2, DCQ, 0, DKV, 0, DKV, width)
            for t, at in tiles(width): DST[rows, at] = dot_nt(DKV[rows, :], WC0[at, :]).astype(BF)
            ds_copy(m).start()
            if not direct:
                @pl.when(m == 1)
                def _():
                    for i in (0, 1): dk_copy(i).start()
        @pl.when(enc & (m == 0))
        def _():
            bottom(m)
            T[:, first] = N2[first, :].T
            for b in range(4):
                block(G0, b)[...] = dot(T[:, first], GP[first, columns(b)]).astype(BF)
                block(G0, 4 + b)[...] = dot(A[first, columns(b)].T, LOW[first, :]).astype(BF)
    loop(0, 2, middle)

    def cross_query_back(m):
        rows = mrows(m)
        for t, at in tiles(width): AFT[rows, at] = dot_nt(DCQ[rows, :], rows_of(WR, 4, t))
        unit, scale = normalize(RR[0, rows, :])
        grad = AFT[rows, :]
        add_norm_grads(1, grad, unit)
        D[rows, :] = D[rows, :] + norm_back(grad, unit, scale, gain_at(1))

    far = n // 2
    def half_rows(c): return ds(c * 32 * n, 32 * n)
    def rows_at(k, c, lo, count): return pl.ds(pl.multiple_of(c * 32 * n + k * 32 + lo, 16), count)
    group = [[], []]
    for g, (G, S, R, E) in enumerate(((G0, S0, R0, WF), (G1, S1, R1, WR))):
        cuts = (0, G.shape[0] // 2, G.shape[0]) if G.shape[0] > 1 else (0, 1)
        for sub, (u, stop) in enumerate(zip(cuts, cuts[1:])):
            us = pl.ds(u, stop - u)
            for way in (1, -1):
                f = Flow()
                f.way, f.norm, f.g, f.sub = way, False, g, sub
                f.own = lambda k, lo, count, G=G, us=us: G.at[us, rows_at(k, core, lo, count), :]
                f.sib = lambda k, lo, count, S=S, us=us: S.at[us, rows_at(k, 0, lo, count), :]
                f.slot = lambda s, lo, count, R=R, us=us, w=(1 - way) // 2: R.at[w, s, us, pl.ds(lo, count)]
                f.res = lambda k, lo, count, E=E, us=us: E.at[us, rows_at(k, core, lo, count), :]
                group[g].append(f)
    for way in (1, -1):
        f = Flow()
        f.way, f.norm, f.g, f.sub = way, True, 2, 2
        f.own, f.sib, f.res = (lambda k, *_: NG.at[core, k]), (lambda k, *_: NS.at[k]), (lambda k, *_: EN.at[core, k])
        f.slot = lambda s, *_, w=(1 - way) // 2: NR.at[w, s]
        group[1].append(f)
    for i, f in enumerate(group[0] + group[1]): f.i, f.to, f.lo = i, after if f.way == 1 else before, 0 if f.way == 1 else 16

    def owner(f, steps): return lax.rem(pos + f.way * steps + n, n)
    def piece(f, outer): return (f.lo, 16) if outer else (0, 32)
    def rs_copy(f, s):
        at = piece(f, isinstance(s, int) and s == 0)
        return remote(f.own(owner(f, far - s), *at), f.slot(s, *at), rs_s.at[f.g], rs_r.at[f.i, s], f.to)
    def ag_piece(f, t): return piece(f, isinstance(t, int) and t == far - 1)
    def ag_copy(f, t):
        res = f.res(owner(f, -t), *ag_piece(f, t))
        return remote(res, res, ag_s.at[f.g], ag_r.at[f.i, t], f.to)
    def sh_start(f, t, at):
        res = f.res(owner(f, -t), *at)
        remote(res, res, sh_s.at[f.g], sh_r.at[f.g], beside).start()

    def sib_key(g, u): return g * 3 + (0 if G0.shape[0] == 1 else u // 4 if g == 0 else (0, 0, 0, 1, 2, 2)[u])
    def sib_copy(g, u):
        G, S = ((G0, S0), (G1, S1))[g]
        return remote(G.at[u, half_rows(1 - core)], S.at[u], sib_s.at[sib_key(g, u)], sib_r.at[sib_key(g, u)], beside)
    sib_norm = remote(NG.at[1 - core], NS, sib_s.at[6], sib_r.at[6], beside)
    def sib_all(g, key):
        G, S = ((G0, S0), (G1, S1))[g]
        us = [u for u in range(G.shape[0]) if sib_key(g, u) == g * 3 + key]
        if not us: return None
        us = pl.ds(us[0], len(us))
        return remote(G.at[us, half_rows(1 - core)], S.at[us], sib_s.at[g * 3 + key], sib_r.at[g * 3 + key], beside)
    def sib_wait(g, sub):
        for key in ((0,), (1, 2))[sub]:
            copy = sib_all(g, key)
            if copy is None: continue
            if direct and g == 1 and key == 2: pl.when(dec)(copy.wait_recv)
            else: copy.wait_recv()

    def reduce_round(g, s, subs=(0, 1, 2)):
        for f in group[g]:
            if f.sub not in subs: continue
            k = owner(f, far - s)
            def partial(at, received):
                own = f.own(k, *at)
                total = own[...].astype(F4) + f.sib(k, *at)[...].astype(F4)
                if received: total = total + f.slot(s - 1, *at)[...].astype(F4)
                own[...] = total.astype(own.dtype)
            first, second = isinstance(s, int) and s == 0, isinstance(s, int) and s == 1
            if first and f.norm and f.way == -1: continue
            if not first and not (second and f.norm and f.way == -1): rs_copy(f, s - 1).wait_recv()
            if first: partial(piece(f, True), False)
            elif second and f.norm: partial((0, 32), f.way == 1)
            elif second:
                partial((f.lo, 16), True)
                partial((16 - f.lo, 16), False)
            else: partial((0, 32), True)
            rs_copy(f, s).start()

    def settle(g):
        for f, b in zip(group[g][::2], group[g][1::2]):
            total = f.own(pos, 0, 32)[...].astype(F4) + f.sib(pos, 0, 32)[...].astype(F4)
            for flow in (f, b):
                rs_copy(flow, far - 1).wait_recv()
                total = total + flow.slot(far - 1, 0, 32)[...].astype(F4)
            f.res(pos, 0, 32)[...] = total.astype(f.res(pos, 0, 32).dtype)
            ag_copy(f, 0).start()
            ag_copy(b, 0).start()
            sh_start(f, 0, (0, 32))

    def gather_round(g, t):
        for f in group[g]:
            def active(t): return not (isinstance(t, int) and f.norm and f.way == -1 and t == far - 1)
            if not active(t - 1): continue
            ag_copy(f, t - 1).wait_recv()
            if not (isinstance(t, int) and t == far) and active(t): ag_copy(f, t).start()
            sh_start(f, t, ag_piece(f, t - 1))

    def begin(g, subs=(0, 1, 2)):
        for sub in (0, 1):
            if sub in subs and (sub == 0 or G0.shape[0] > 1):
                sib_wait(g, sub)
                if direct and g == 1 and sub == 1: pl.when(enc)(cg_copy.wait_recv)
                reduce_round(g, 0, (sub,))
        if g == 1:
            sib_norm.wait_recv()
            reduce_round(1, 0, (2,))

    def close_ring():
        for g, (G, E) in enumerate(((G0, WF), (G1, WR))):
            sent = pl.ds(0, 32 * n - 32)
            remote(E.at[:, half_rows(core)], E.at[:, half_rows(1 - core)], sh_s.at[g], sh_r.at[g], beside).wait()
            remote(G.at[:, sent], G.at[:, sent], rs_s.at[g], rs_r.at[0, 0], after).wait_send()
            remote(E.at[:, sent], E.at[:, sent], ag_s.at[g], ag_r.at[0, 0], after).wait_send()
            for key in range(3):
                copy = sib_all(g, key)
                if copy is None: continue
                if direct and g == 1 and key == 2: pl.when(dec)(copy.wait_send)
                else: copy.wait_send()
        sent = pl.ds(0, n - 1)
        remote(EN.at[core], EN.at[1 - core], sh_s.at[2], sh_r.at[2], beside).wait()
        remote(NG.at[0, sent], NG.at[0, sent], rs_s.at[2], rs_r.at[0, 0], after).wait_send()
        remote(EN.at[0, sent], EN.at[0, sent], ag_s.at[2], ag_r.at[0, 0], after).wait_send()
        sib_norm.wait_send()

    def done_blocks(g, G, count):
        per = G.shape[1] // SIDE
        for u in range(G.shape[0]):
            if count == min((u + 1) * per, (8, 6)[g]): sib_copy(g, u).start()

    def weight_grads(g, G, source, grad, count, b0):
        T[...] = source[...].T
        for b in range(count):
            block(G, b0 + b)[...] = dot(T[...], grad[:, columns(b)]).astype(BF)
            done_blocks(g, G, b0 + b + 1)

    own_rows = ds(core * (SIDE // 2), SIDE // 2)
    cg_trade = remote(CG.at[:, ds((1 - core) * (SIDE // 2), SIDE // 2)], CS, cg_s.at[0], cg_r.at[0], beside)
    cg_copy = remote(CG.at[:, own_rows], G1.at[pl.ds(4, 2), own_rows], cg_s.at[1], cg_r.at[1], partner) if direct else None
    if direct:
        @pl.when(dec)
        def _():
            T[...] = ST[...].T
            for b in range(2): CG[b] = dot(T[...], DKV[:, columns(b)]).astype(BF)
            cg_trade.start()
        @pl.when(enc)
        def _(): S1[pl.ds(4, 2)] = jnp.zeros((2, SIDE // 2, SIDE), BF)
    def grad_block(b, whole, rest):
        out = block(G0, b)
        @pl.when(dec)
        def _(): out[...] = whole().astype(BF)
        @pl.when(enc)
        def _(): out[...] = (out[...].astype(F4) + rest()).astype(BF)
        done_blocks(0, G0, b + 1)

    @pl.when(dec)
    def _(): T[...] = N2[...].T
    @pl.when(enc)
    def _(): T[:, second] = N2[second, :].T
    for b in range(4):
        grad_block(b, lambda: dot(T[...], GP[:, columns(b)]), lambda: dot(T[:, second], GP[second, columns(b)]))
    if direct:
        @pl.when(dec)
        def _():
            cg_trade.wait_recv()
            CG[:, own_rows, :] = (CG[:, own_rows, :].astype(F4) + CS[...].astype(F4)).astype(BF)
            cg_copy.start()
    for b in range(4):
        grad_block(4 + b, lambda: dot(A[:, columns(b)].T, LOW[...]), lambda: dot(A[second, columns(b)].T, LOW[second, :]))
        if b == 1 and G0.shape[0] > 1: begin(0, (0,))

    @pl.when(dec)
    def _(): loop(0, 2, cross_query_back)

    first_left = jnp.where(enc, 1, 0)

    def start_ring(m, place):
        @pl.when(m == first_left)
        def _(): begin(0, (1,) if G0.shape[0] > 1 else (0,)) if place == 0 else reduce_round(0, 1)
    loop(first_left, 2, lambda m: bottom(m, start_ring))
    NG[...] = jnp.zeros_like(NG)
    for j in range(4):
        NG[0, j] = PG[:, 128 * j:128 * (j + 1)]
        NG[1, j] = PB[:, 128 * j:128 * (j + 1)]
    sib_norm.start()
    weight_grads(1, G1, H1, DQKV, 3, 0)
    weight_grads(1, G1, O, LOWS, 1, 3)
    if not direct:
        @pl.when(enc)
        def _():
            for m in (0, 1): dk_copy(m).wait_recv()
            T[...] = ST[...].T
            for b in range(2): block(G1, 4 + b)[...] = dot(T[...], DKV[:, columns(b)]).astype(BF)
    @pl.when(dec)
    def _():
        for b, (source, grad) in enumerate(((HQ, DCQ), (O2, LOWC))):
            T[...] = source[...].T
            block(G1, 4 + b)[...] = dot(T[...], grad[...]).astype(BF)
            if direct: done_blocks(1, G1, 5 + b)
    if not direct: done_blocks(1, G1, 6)
    begin(1)
    if far == 4:
        reduce_round(0, 2)
        reduce_round(1, 1)
        reduce_round(0, 3)
        reduce_round(1, 2)
        settle(0)
        reduce_round(1, 3)
        gather_round(0, 1)
        settle(1)
        gather_round(0, 2)
        gather_round(1, 1)
        gather_round(0, 3)
        gather_round(1, 2)
        gather_round(0, 4)
        gather_round(1, 3)
        gather_round(1, 4)
    else:
        reduce_round(1, 1)
        for g in (0, 1):
            loop(2, far, lambda s: reduce_round(g, s))
            settle(g)
            loop(1, far - 1, lambda t: gather_round(g, t))
            gather_round(g, far - 1)
            gather_round(g, far)
    close_ring()

    @pl.when(enc)
    def _():
        wc_copy.wait_send()
        for m in (0, 1): st_copy(m).wait_send()
    @pl.when(dec)
    def _():
        for trade in wc_trades: trade.wait_send()
        for m in (0, 1):
            ds_copy(m).wait_send()
            if not direct: dk_copy(m).wait_send()
        if direct:
            cg_trade.wait_send()
            cg_copy.wait_send()


def finish_kernel(e0, e1, en, out, gin, o_out, o_gin, o_qkv, o_wo, o_up, o_down, o_cross, o_gain, o_bias, F, sem, sem2):
    copies = [pltpu.make_async_copy(out, o_out, sem2.at[0]), pltpu.make_async_copy(gin, o_gin, sem2.at[1])]
    for copy in copies: copy.start()
    for j in range(4):
        at = pl.ds(128 * j, 128)
        for i in range(3):
            o_gain[i, :, at] = en[0, j, i:i + 1, :]
            o_bias[i, :, at] = en[1, j, i:i + 1, :]
    def columns(b): return pl.ds(b * SIDE, SIDE)
    targets = [(e0, b, o_up.at[0, :, columns(b)]) for b in range(4)] + [(e0, 4 + b, o_down.at[0, columns(b), :]) for b in range(4)]
    targets += [(e1, b, o_qkv.at[0, :, columns(b)]) for b in range(3)] + [(e1, 3, o_wo.at[0])]
    targets += [(e1, 4 + b, o_cross.at[0, :, columns(b)]) for b in range(2)]
    slots = F.shape[0]
    flight = []
    for i, (e, b, target) in enumerate(targets):
        if i >= slots: flight[i - slots].wait()
        F[i % slots] = block(e, b)[...].astype(F4)
        flight.append(pltpu.make_async_copy(F.at[i % slots], target, sem.at[i % slots]))
        flight[-1].start()
    for copy in flight[-slots:] + copies: copy.wait()


def layers(lens, x, ct, wq, wo, w1, w2, wc, gn, bs, n):
    micro, length, width = x.shape
    rows, hidden = micro * length, w1.shape[1]
    any_ = pl.BlockSpec(memory_space=pl.ANY)
    vmem = pl.BlockSpec(memory_space=pltpu.VMEM)
    V, DMA = pltpu.VMEM, pltpu.SemaphoreType.DMA
    def units(count): return (-(-count * SIDE // (64 * n)), 64 * n, SIDE)
    s0, s1 = units(8), units(6)
    norm = (2, n, 8, 128)
    def own(s): return (s[0], s[1] // 2, SIDE)
    def slots(s): return (2, n // 2, s[0], 32, SIDE)
    sq = V((rows, width), BF)
    probs = V((micro * width // 64, length, length), BF)
    scratch = [V(x.shape, BF), V(x.shape, BF), V(wc.shape, BF), V(gn.shape, F4), V(bs.shape, F4)]
    scratch += [sq, V((rows, 3 * width), BF), probs, sq, V((2, rows, width), F4), sq, sq, sq, V((rows, 2 * width), BF), probs, sq, sq,
                V((rows, hidden), BF), V((rows, hidden), BF), V((rows, width), F4), V((rows, width), F4),
                sq, sq, sq, sq, V((rows, 3 * width), BF), sq, V((rows, 2 * width), BF), sq, V((width, rows), BF)]
    scratch += [V(s0, BF), V(s1, BF), V(norm, F4), V((2, SIDE, SIDE), BF), V((2, SIDE // 2, SIDE), BF), V(own(s0), BF), V(own(s1), BF), V(norm[1:], F4), V(slots(s0), BF), V(slots(s1), BF), V((2, n // 2, 8, 128), F4),
                V((8, width), F4), V((8, width), F4)]
    scratch += [DMA((18,)), DMA, DMA, DMA((3,)), DMA((3,)), DMA((2,)), DMA((2,)), DMA((2,)), DMA((2,)), DMA((2,)), DMA((2,)), DMA((2,)), DMA((2,)), DMA((7,)), DMA((7,)), DMA((3,)), DMA((10, n // 2)), DMA((3,)), DMA((10, n // 2)), DMA((3,)), DMA((3,))]
    results = [V(s0, BF), V(s1, BF), V(norm, F4), V(x.shape, BF), V(x.shape, BF)]
    e0, e1, en, out, gin = pl.pallas_call(
        functools.partial(layers_kernel, n), out_shape=results,
        in_specs=[pl.BlockSpec(memory_space=pltpu.SMEM)] + [any_] * 9, out_specs=[vmem] * 5, scratch_shapes=scratch,
        compiler_params=pltpu.CompilerParams(collective_id=1, has_side_effects=True, vmem_limit_bytes=54 * 2**20),
        name="layers",
    )(lens, x, ct, wq, wo, w1, w2, wc, gn, bs)
    def f4(*shape): return jax.ShapeDtypeStruct(shape, F4)
    return pl.pallas_call(
        finish_kernel,
        out_shape=[jax.ShapeDtypeStruct(x.shape, BF)] * 2 + [f4(1, width, 3 * width), f4(1, width, width), f4(1, width, hidden), f4(1, hidden, width),
                                                            f4(1, width, 2 * width), f4(3, 1, width), f4(3, 1, width)],
        in_specs=[vmem] * 5, out_specs=[any_] * 7 + [vmem] * 2,
        scratch_shapes=[V((4, SIDE, SIDE), F4), DMA((4,)), DMA((2,))],
        compiler_params=pltpu.CompilerParams(vmem_limit_bytes=6 * 2**20),
        name="finish",
    )(e0, e1, en, out, gin)


def local(layer_input, lengths, attn_qkv, attn_out, ffn_in, ffn_out, cross_weight, norm_gain, norm_bias, cotangent):
    def flat(a): return a.reshape(a.shape[1:])
    n = lax.axis_size("dp") // 2
    data = (layer_input.shape[1],) + layer_input.shape[3:]
    out, gin, *grads, gain, bias = layers(lengths.T, layer_input.reshape(data), cotangent.reshape(data), flat(attn_qkv), flat(attn_out), flat(ffn_in), flat(ffn_out),
                              flat(cross_weight), norm_gain.transpose(1, 0, 2), norm_bias.transpose(1, 0, 2), n)
    return (out.reshape(layer_input.shape), gin.reshape(layer_input.shape), *grads, gain.transpose(1, 0, 2), bias.transpose(1, 0, 2))


def solution(mesh):
    data = P("section", None, "dp", None, None)
    weight = P("section", None, None)
    return jax.shard_map(
        local, mesh=mesh,
        in_specs=(data, P(None, "dp")) + (weight,) * 7 + (data,),
        out_specs=(data, data) + (weight,) * 7,
        check_vma=False,
    )
```

```python
import functools

import jax
import jax.numpy as jnp
from jax import lax
from jax.experimental import pallas as pl
from jax.experimental.pallas import tpu as pltpu
from jax.sharding import PartitionSpec as P

MESH = pl.DeviceIdType.MESH
BF = jnp.bfloat16
F4 = jnp.float32
SIDE = 512
TILE = 256


def dot(a, b):
    return jnp.dot(a, b, preferred_element_type=F4)


def dot_nt(a, b):
    return lax.dot_general(a, b, (((1,), (1,)), ((), ())), preferred_element_type=F4)


def gelu_parts(u):
    cdf = 0.5 + 0.5 * lax.erf(u * 0.5 ** 0.5)
    return u * cdf, cdf + u * (jnp.exp(-0.5 * u * u) * 0.3989422804014327)


def normalize(value):
    center = value - jnp.mean(value, axis=-1, keepdims=True)
    spread = jnp.mean(center * center, axis=-1, keepdims=True)
    scale = lax.rsqrt(spread + 1e-05)
    return center * scale, scale


def norm_back(grad, unit, scale, gain):
    inner = grad * gain
    mean = jnp.mean(inner, axis=-1, keepdims=True)
    along = jnp.mean(inner * unit, axis=-1, keepdims=True)
    return scale * (inner - mean - unit * along)


def loop(start, stop, body, unroll=1):
    lax.fori_loop(start, stop, lambda i, carry: (body(i), carry)[1], 0, unroll=unroll)


def ds(start, size):
    return pl.ds(pl.multiple_of(start, size), size)


def block(ref, b):
    rows = ref.shape[1]
    return ref.at[b * SIDE // rows, pl.ds(b * SIDE % rows, SIDE)]


def remote(src, dst, ss, rs, to):
    return pltpu.make_async_remote_copy(src_ref=src, dst_ref=dst, send_sem=ss, recv_sem=rs, device_id=to, device_id_type=MESH)


class Flow:
    pass


def layers_kernel(n, lens, x, ct, wq, wo, w1, w2, wc, gn, bs,
                  WF, WR, EN, OUT, GIN,
                  X, CT, WC0, GN, BS, H1, QKV, PT, O, RR, ST, HQ, CQ, KV, PT2, O2, N2, A, GP, DA, AFT, D, LOW, LOWC, LOWS, DO, DQKV, DCQ, DKV, DST, T,
                  G0, G1, NG, CG, CS, S0, S1, NS, R0, R1, NR, PG, PB,
                  ld, wc_s, wc_r, wh_s, wh_r, st_s, st_r, ds_s, ds_r, dk_s, dk_r, cg_s, cg_r,
                  sib_s, sib_r, rs_s, rs_r, ag_s, ag_r, sh_s, sh_r):
    sec, dp = lax.axis_index("section"), lax.axis_index("dp")
    core, chip = lax.rem(dp, 2), dp // 2
    side, line = lax.rem(chip, 2), chip // 2
    pos = jnp.where(side == 0, line, n - 1 - line)

    def ring_at(q):
        q = lax.rem(q + n, n)
        return (jnp.where(q < n // 2, q, n - 1 - q) * 2 + jnp.where(q < n // 2, 0, 1)) * 2 + core

    sibling = dp + 1 - 2 * core
    partner, beside, after, before = (1 - sec, dp), (sec, sibling), (sec, ring_at(pos + 1)), (sec, ring_at(pos - 1))
    across = (sec, dp + 2 - 4 * side)
    enc, dec = sec == 0, sec == 1
    direct = 64 * n == SIDE
    length, width = X.shape[1], X.shape[2]
    hidden = A.shape[1]
    heads = width // 64
    pairs = heads // 2

    loads = {}

    def load(name, src, dst):
        loads.setdefault(name, []).append(pltpu.make_async_copy(src, dst, ld.at[sum(map(len, loads.values()))]))
        loads[name][-1].start()

    def columns(b): return pl.ds(b * SIDE, SIDE)
    load("first", x, X)
    load("first", gn, GN)
    load("first", bs, BS)
    for b in range(3): load("first", wq.at[:, columns(b)], block(WR, b))
    load("first", wo, block(WR, 3))
    def arrived(name):
        for copy in loads[name]: copy.wait()

    bar = pltpu.get_barrier_semaphore()
    for target in (partner, beside, after, before, across):
        pl.semaphore_signal(bar, inc=1, device_id=target, device_id_type=MESH)
    pl.semaphore_wait(bar, 5)

    def quarter(x, c): return WC0.at[ds((2 * x + c) * (width // 4), width // 4)]
    wc_copy = remote(wc.at[ds((2 * side + core) * (width // 4), width // 4)], quarter(side, core), wc_s, wc_r, partner)
    wc_trades = [remote(quarter(side, core), quarter(side, core), wh_s.at[0], wh_r.at[0], across),
                 remote(quarter(side, core), quarter(side, core), wh_s.at[1], wh_r.at[1], beside),
                 remote(quarter(1 - side, core), quarter(1 - side, core), wh_s.at[2], wh_r.at[2], beside)]

    def mrows(m): return ds(m * length, length)
    def st_copy(m): return remote(ST.at[mrows(m)], ST.at[mrows(m)], st_s.at[m], st_r.at[m], partner)
    def ds_copy(m): return remote(DST.at[mrows(m)], DST.at[mrows(m)], ds_s.at[m], ds_r.at[m], partner)
    def dk_copy(m): return remote(DKV.at[mrows(m)], DKV.at[mrows(m)], dk_s.at[m], dk_r.at[m], partner)

    @pl.when(enc)
    def _(): wc_copy.start()

    PG[...] = jnp.zeros_like(PG)
    PB[...] = jnp.zeros_like(PB)

    def gain_at(i): return GN[i]
    def bias_at(i): return BS[i]

    def add_norm_grads(i, grad, unit):
        at = pl.ds(i, 1)
        PG[at, :] = PG[at, :] + jnp.sum(grad * unit, axis=0, keepdims=True)
        PB[at, :] = PB[at, :] + jnp.sum(grad, axis=0, keepdims=True)

    lane_low = lax.broadcasted_iota(jnp.int32, (length, 128), 1) < 64
    lane_row = lax.broadcasted_iota(jnp.int32, (1, 128), 1) < 64
    head_masks = (jnp.where(lane_row, 1.0, 0.0).astype(BF), jnp.where(lane_row, 0.0, 1.0).astype(BF))
    query_masks = (jnp.where(lane_row, 0.125, 0.0).astype(BF), jnp.where(lane_row, 0.0, 0.125).astype(BF))

    def attention(m, q, q0, k, k0, v, v0, P, out_ref):
        rows = mrows(m)
        usable = lax.broadcasted_iota(jnp.int32, (length, length), 0) < lens[0, m]
        def cols(c0, j): return pl.ds(c0 + j * 128, 128)
        def score(h):
            j, e = h // 2, h % 2
            return dot_nt(k[rows, cols(k0, j)], q[rows, cols(q0, j)] * query_masks[e])
        def soft(s, h):
            s = jnp.where(usable, s, -1e30)
            w = jnp.exp(s - jnp.max(s, axis=0, keepdims=True))
            p = (w * (1.0 / jnp.sum(w, axis=0, keepdims=True))).astype(BF)
            P[m * heads + h] = p
        for h in range(heads): soft(score(h), h)
        for j in range(pairs):
            vt = v[rows, cols(v0, j)].T
            parts = [dot(vt[64 * e:64 * (e + 1)], P[m * heads + 2 * j + e]) for e in (0, 1)]
            out_ref[rows, cols(0, j)] = jnp.concatenate(parts, axis=0).T.astype(BF)

    def attention_back(m, do, q, q0, k, k0, v, v0, P, dq, dq0, dk, dk0, dv, dv0):
        rows = mrows(m)
        def cols(c0, j): return pl.ds(c0 + j * 128, 128)
        def weights(h): return P.at[m * heads + h]
        def grad_scores(h):
            j, e = h // 2, h % 2
            pf = weights(h)[...].astype(F4)
            t = pf * dot_nt(v[rows, cols(v0, j)], do[rows, cols(0, j)] * head_masks[e])
            return (t - pf * jnp.sum(t, axis=0, keepdims=True)).astype(BF)
        def put_v(j):
            do2 = do[rows, cols(0, j)]
            dv[rows, cols(dv0, j)] = jnp.where(lane_low, dot(weights(2 * j)[...], do2), dot(weights(2 * j + 1)[...], do2)).astype(BF)
        def put_k(j):
            q2 = q[rows, cols(q0, j)]
            dk[rows, cols(dk0, j)] = (jnp.where(lane_low, dot(weights(2 * j)[...], q2), dot(weights(2 * j + 1)[...], q2)) * 0.125).astype(BF)
        def put_q(j):
            kt = k[rows, cols(k0, j)].T
            parts = [dot(kt[64 * e:64 * (e + 1)], weights(2 * j + e)[...]) for e in (0, 1)]
            dq[rows, cols(dq0, j)] = (jnp.concatenate(parts, axis=0).T * 0.125).astype(BF)
        for j in range(pairs):
            put_v(j)
            for h in (2 * j, 2 * j + 1): weights(h)[...] = grad_scores(h)
        for j in range(pairs):
            put_k(j)
            put_q(j)

    def tiles(count): return [(t, pl.ds(t * TILE, TILE)) for t in range(count // TILE)]
    def tile_of(ref, b0, t): return block(ref, b0 + t * TILE // SIDE)[:, pl.ds(t * TILE % SIDE, TILE)]
    def rows_of(ref, b0, t): return block(ref, b0 + t * TILE // SIDE)[pl.ds(t * TILE % SIDE, TILE), :]

    def norm_into(source, m, index, target):
        rows = mrows(m)
        unit, _ = normalize(source[rows, :])
        target[rows, :] = (unit * gain_at(index) + bias_at(index)).astype(BF)

    def self_forward(m):
        rows = mrows(m)
        unit, _ = normalize(X[m].astype(F4))
        H1[rows, :] = (unit * gain_at(0) + bias_at(0)).astype(BF)
        for t, at in tiles(3 * width): QKV[rows, at] = dot(H1[rows, :], tile_of(WR, 0, t)).astype(BF)
        attention(m, QKV, 0, QKV, width, QKV, 2 * width, PT, O)
        for t, at in tiles(width): RR[0, rows, at] = dot(O[rows, :], tile_of(WR, 3, t)) + X[m, :, at].astype(F4)

    def ffn_up(m, source, index, grad=None):
        rows = mrows(m)
        norm_into(source, m, index, N2)
        for t, at in tiles(hidden):
            act, slope = gelu_parts(dot(N2[rows, :], tile_of(WF, 0, t)))
            A[rows, at] = act.astype(BF)
            GP[rows, at] = (slope if grad is None else slope * grad[rows, at].astype(F4)).astype(BF)

    def ffn_down(m, source):
        rows = mrows(m)
        for t, at in tiles(width):
            total = source[rows, at]
            for b in range(hidden // SIDE): total = total + dot(A[rows, columns(b)], tile_of(WF, 4 + b, t))
            AFT[rows, at] = total

    arrived("first")
    for b in range(4): load("ffn", w1.at[:, columns(b)], block(WF, b))
    for b in range(4): load("ffn", w2.at[columns(b), :], block(WF, 4 + b))
    for b in range(2): load("cross", wc.at[:, columns(b)], block(WR, 4 + b))
    load("cross", ct, CT)

    def front(m):
        self_forward(m)
        @pl.when(enc)
        def _():
            @pl.when(m == 0)
            def _(): arrived("ffn")
            ffn_up(m, RR.at[0], 1)
            ffn_down(m, RR.at[0])
            norm_into(AFT, m, 2, ST)
            st_copy(m).start()
            OUT[m] = ST[mrows(m), :]
    loop(0, 2, front)
    arrived("cross")

    @pl.when(dec)
    def _():
        arrived("ffn")
        wc_copy.wait_recv()
        wc_trades[0].start()
        wc_trades[1].start()
        for m in (0, 1):
            norm_into(RR.at[0], m, 1, HQ)
            for t, at in tiles(width): CQ[mrows(m), at] = dot(HQ[mrows(m), :], tile_of(WR, 4, t)).astype(BF)
            for t, at in tiles(hidden): DA[mrows(m), at] = dot_nt(CT[m], rows_of(WF, 4, t)).astype(BF)
        wc_trades[0].wait_recv()
        wc_trades[2].start()
        wc_trades[1].wait_recv()
        wc_trades[2].wait_recv()

    far = n // 2
    def half_rows(c): return ds(c * 32 * n, 32 * n)
    def rows_at(k, c, lo, count): return pl.ds(pl.multiple_of(c * 32 * n + k * 32 + lo, 16), count)
    group = [[], []]
    for g, (G, S, R, E) in enumerate(((G0, S0, R0, WF), (G1, S1, R1, WR))):
        cuts = (0, G.shape[0] // 2, G.shape[0]) if direct else (0, 1)
        for sub, (u, stop) in enumerate(zip(cuts, cuts[1:])):
            us = pl.ds(u, stop - u)
            for way in (1, -1):
                f = Flow()
                f.way, f.norm, f.g, f.sub = way, False, g, sub
                f.own = lambda k, lo, count, G=G, us=us: G.at[us, rows_at(k, core, lo, count), :]
                f.sib = lambda k, lo, count, S=S, us=us: S.at[us, rows_at(k, 0, lo, count), :]
                f.slot = lambda s, lo, count, R=R, us=us, w=(1 - way) // 2: R.at[w, s, us, pl.ds(lo, count)]
                f.res = lambda k, lo, count, E=E, us=us: E.at[us, rows_at(k, core, lo, count), :]
                group[g].append(f)
    for way in (1, -1):
        f = Flow()
        f.way, f.norm, f.g, f.sub = way, True, 2, 2
        f.own, f.sib, f.res = (lambda k, *_: NG.at[core, k]), (lambda k, *_: NS.at[k]), (lambda k, *_: EN.at[core, k])
        f.slot = lambda s, *_, w=(1 - way) // 2: NR.at[w, s]
        group[1].append(f)
    for i, f in enumerate(group[0] + group[1]): f.i, f.to, f.lo = i, after if f.way == 1 else before, 0 if f.way == 1 else 16

    def owner(f, steps): return lax.rem(pos + f.way * steps + n, n)
    def piece(f, outer): return (f.lo, 16) if outer else (0, 32)
    def rs_copy(f, s):
        at = piece(f, isinstance(s, int) and s == 0)
        return remote(f.own(owner(f, far - s), *at), f.slot(s, *at), rs_s.at[f.g], rs_r.at[f.i, s], f.to)
    def ag_piece(f, t): return piece(f, isinstance(t, int) and t == far - 1)
    def ag_copy(f, t):
        res = f.res(owner(f, -t), *ag_piece(f, t))
        return remote(res, res, ag_s.at[f.g], ag_r.at[f.i, t], f.to)
    def sh_start(f, t, at):
        res = f.res(owner(f, -t), *at)
        remote(res, res, sh_s.at[f.g], sh_r.at[f.g], beside).start()

    def sib_key(g, u): return g * 3 + (0 if not direct else u // 4 if g == 0 else (0, 0, 0, 1, 2, 2)[u])
    def sib_copy(g, u):
        G, S = ((G0, S0), (G1, S1))[g]
        return remote(G.at[u, half_rows(1 - core)], S.at[u], sib_s.at[sib_key(g, u)], sib_r.at[sib_key(g, u)], beside)
    sib_norm = remote(NG.at[1 - core], NS, sib_s.at[6], sib_r.at[6], beside)
    def sib_all(g, key):
        G, S = ((G0, S0), (G1, S1))[g]
        us = [u for u in range(G.shape[0]) if sib_key(g, u) == g * 3 + key]
        if not us: return None
        us = pl.ds(us[0], len(us))
        return remote(G.at[us, half_rows(1 - core)], S.at[us], sib_s.at[g * 3 + key], sib_r.at[g * 3 + key], beside)
    def sib_wait(g, sub):
        for key in ((0,), (1, 2))[sub]:
            copy = sib_all(g, key)
            if copy is None: continue
            if direct and g == 1 and key == 2: pl.when(dec)(copy.wait_recv)
            else: copy.wait_recv()

    def reduce_round(g, s, subs=(0, 1, 2)):
        for f in group[g]:
            if f.sub not in subs: continue
            k = owner(f, far - s)
            def partial(at, received):
                own = f.own(k, *at)
                total = own[...].astype(F4) + f.sib(k, *at)[...].astype(F4)
                if received: total = total + f.slot(s - 1, *at)[...].astype(F4)
                own[...] = total.astype(own.dtype)
            first, second = isinstance(s, int) and s == 0, isinstance(s, int) and s == 1
            if first and f.norm and f.way == -1: continue
            if not first and not (second and f.norm and f.way == -1): rs_copy(f, s - 1).wait_recv()
            if first: partial(piece(f, True), False)
            elif second and f.norm: partial((0, 32), f.way == 1)
            elif second:
                partial((f.lo, 16), True)
                partial((16 - f.lo, 16), False)
            else: partial((0, 32), True)
            rs_copy(f, s).start()

    def settle(g):
        for f, b in zip(group[g][::2], group[g][1::2]):
            total = f.own(pos, 0, 32)[...].astype(F4) + f.sib(pos, 0, 32)[...].astype(F4)
            for flow in (f, b):
                rs_copy(flow, far - 1).wait_recv()
                total = total + flow.slot(far - 1, 0, 32)[...].astype(F4)
            f.res(pos, 0, 32)[...] = total.astype(f.res(pos, 0, 32).dtype)
            ag_copy(f, 0).start()
            ag_copy(b, 0).start()
            sh_start(f, 0, (0, 32))

    def gather_round(g, t):
        for f in group[g]:
            def active(t): return not (isinstance(t, int) and f.norm and f.way == -1 and t == far - 1)
            if not active(t - 1): continue
            ag_copy(f, t - 1).wait_recv()
            if not (isinstance(t, int) and t == far) and active(t): ag_copy(f, t).start()
            sh_start(f, t, ag_piece(f, t - 1))

    def begin(g, subs=(0, 1, 2)):
        for sub in (0, 1):
            if sub in subs and (sub == 0 or direct):
                sib_wait(g, sub)
                if direct and g == 1 and sub == 1: pl.when(enc)(cg_copy.wait_recv)
                reduce_round(g, 0, (sub,))
        if g == 1:
            sib_norm.wait_recv()
            reduce_round(1, 0, (2,))

    def close_ring():
        for g, (G, E) in enumerate(((G0, WF), (G1, WR))):
            sent = pl.ds(0, 32 * n - 32)
            remote(E.at[:, half_rows(core)], E.at[:, half_rows(1 - core)], sh_s.at[g], sh_r.at[g], beside).wait()
            remote(G.at[:, sent], G.at[:, sent], rs_s.at[g], rs_r.at[0, 0], after).wait_send()
            remote(E.at[:, sent], E.at[:, sent], ag_s.at[g], ag_r.at[0, 0], after).wait_send()
            for key in range(3):
                copy = sib_all(g, key)
                if copy is None: continue
                if direct and g == 1 and key == 2: pl.when(dec)(copy.wait_send)
                else: copy.wait_send()
        sent = pl.ds(0, n - 1)
        remote(EN.at[core], EN.at[1 - core], sh_s.at[2], sh_r.at[2], beside).wait()
        remote(NG.at[0, sent], NG.at[0, sent], rs_s.at[2], rs_r.at[0, 0], after).wait_send()
        remote(EN.at[0, sent], EN.at[0, sent], ag_s.at[2], ag_r.at[0, 0], after).wait_send()
        sib_norm.wait_send()

    def done_blocks(g, G, count):
        per = G.shape[1] // SIDE
        for u in range(G.shape[0]):
            if count == min((u + 1) * per, (8, 6)[g]): sib_copy(g, u).start()

    def weight_grads(g, G, source, grad, count, b0):
        T[...] = source[...].T
        for b in range(count):
            block(G, b0 + b)[...] = dot(T[...], grad[:, columns(b)]).astype(BF)
            done_blocks(g, G, b0 + b + 1)

    own_rows = ds(core * (SIDE // 2), SIDE // 2)
    cg_trade = remote(CG.at[:, ds((1 - core) * (SIDE // 2), SIDE // 2)], CS, cg_s.at[0], cg_r.at[0], beside)
    cg_copy = remote(CG.at[:, own_rows], G1.at[pl.ds(4, 2), own_rows], cg_s.at[1], cg_r.at[1], partner) if direct else None
    early = direct

    def bottom(m, hook=None):
        rows = mrows(m)
        LOWS[rows, :] = D[rows, :].astype(BF)
        for t, at in tiles(width): DO[rows, at] = dot_nt(LOWS[rows, :], rows_of(WR, 3, t)).astype(BF)
        if hook is not None: hook(m, 0)
        attention_back(m, DO, QKV, 0, QKV, width, QKV, 2 * width, PT, DQKV, 0, DQKV, width, DQKV, 2 * width)
        if hook is not None: hook(m, 1)
        for t, at in tiles(width):
            total = dot_nt(DQKV[rows, columns(0)], rows_of(WR, 0, t))
            for b in (1, 2): total = total + dot_nt(DQKV[rows, columns(b)], rows_of(WR, b, t))
            AFT[rows, at] = total
        unit, scale = normalize(X[m].astype(F4))
        grad = AFT[rows, :]
        add_norm_grads(0, grad, unit)
        GIN[m] = (D[rows, :] + norm_back(grad, unit, scale, gain_at(0))).astype(BF)

    first, second = pl.ds(0, length), pl.ds(length, length)

    def middle(m):
        rows = mrows(m)
        @pl.when(enc)
        def _():
            ds_copy(m).wait_recv()
            unit, scale = normalize(AFT[rows, :])
            grad = CT[m].astype(F4) + DST[rows, :].astype(F4)
            add_norm_grads(2, grad, unit)
            back = norm_back(grad, unit, scale, gain_at(2))
            D[rows, :] = back
            LOW[rows, :] = back.astype(BF)
            if early:
                @pl.when(m == 1)
                def _():
                    for b in range(4):
                        out = block(G0, 4 + b)
                        out[...] = (out[...].astype(F4) + dot(A[second, columns(b)].T, LOW[second, :])).astype(BF)
                        done_blocks(0, G0, 5 + b)
        @pl.when(dec)
        def _():
            st_copy(m).wait_recv()
            for t, at in tiles(2 * width): KV[rows, at] = dot(ST[rows, :], WC0[:, at]).astype(BF)
            attention(m, CQ, 0, KV, 0, KV, width, PT2, O2)
            for t, at in tiles(width): RR[1, rows, at] = dot(O2[rows, :], tile_of(WR, 5, t)) + RR[0, rows, at]
            ffn_up(m, RR.at[1], 2, DA)
            D[rows, :] = CT[m].astype(F4)
            LOW[rows, :] = CT[m]
        @pl.when(enc)
        def _():
            for t, at in tiles(hidden): GP[rows, at] = (dot_nt(LOW[rows, :], rows_of(WF, 4, t)) * GP[rows, at].astype(F4)).astype(BF)
            if early: pl.when(m == 1)(lambda: begin(0, (1,)))
        for t, at in tiles(width):
            total = dot_nt(GP[rows, columns(0)], rows_of(WF, 0, t))
            for b in range(1, hidden // SIDE): total = total + dot_nt(GP[rows, columns(b)], rows_of(WF, b, t))
            AFT[rows, at] = total
        unit, scale = normalize(RR[sec, rows, :])
        grad = AFT[rows, :]
        add_norm_grads(1 + sec, grad, unit)
        D[rows, :] = D[rows, :] + norm_back(grad, unit, scale, gain_at(1 + sec))
        @pl.when(dec)
        def _():
            LOWC[rows, :] = D[rows, :].astype(BF)
            for t, at in tiles(width): DO[rows, at] = dot_nt(LOWC[rows, :], rows_of(WR, 5, t)).astype(BF)
            attention_back(m, DO, CQ, 0, KV, 0, KV, width, PT2, DCQ, 0, DKV, 0, DKV, width)
            for t, at in tiles(width): DST[rows, at] = dot_nt(DKV[rows, :], WC0[at, :]).astype(BF)
            ds_copy(m).start()
            if not direct:
                @pl.when(m == 1)
                def _():
                    for i in (0, 1): dk_copy(i).start()
        @pl.when(enc & (m == 0))
        def _():
            bottom(m)
            T[:, first] = N2[first, :].T
            for b in range(4):
                block(G0, b)[...] = dot(T[:, first], GP[first, columns(b)]).astype(BF)
                block(G0, 4 + b)[...] = dot(A[first, columns(b)].T, LOW[first, :]).astype(BF)
    loop(0, 2, middle)

    def decoder_rest(m):
        rows = mrows(m)
        ffn_down(m, RR.at[1])
        OUT[m] = AFT[rows, :].astype(BF)
        for t, at in tiles(width): AFT[rows, at] = dot_nt(DCQ[rows, :], rows_of(WR, 4, t))
        unit, scale = normalize(RR[0, rows, :])
        grad = AFT[rows, :]
        add_norm_grads(1, grad, unit)
        D[rows, :] = D[rows, :] + norm_back(grad, unit, scale, gain_at(1))

    if direct:
        @pl.when(dec)
        def _():
            T[...] = ST[...].T
            for b in range(2): CG[b] = dot(T[...], DKV[:, columns(b)]).astype(BF)
            cg_trade.start()
        @pl.when(enc)
        def _(): S1[pl.ds(4, 2)] = jnp.zeros((2, SIDE // 2, SIDE), BF)
    def grad_block(b, whole, rest):
        out = block(G0, b)
        @pl.when(dec)
        def _(): out[...] = whole().astype(BF)
        @pl.when(enc)
        def _(): out[...] = (out[...].astype(F4) + rest()).astype(BF)
        done_blocks(0, G0, b + 1)

    @pl.when(dec)
    def _(): T[...] = N2[...].T
    @pl.when(enc)
    def _(): T[:, second] = N2[second, :].T
    for b in range(4):
        grad_block(b, lambda: dot(T[...], GP[:, columns(b)]), lambda: dot(T[:, second], GP[second, columns(b)]))
    if direct:
        @pl.when(dec)
        def _():
            cg_trade.wait_recv()
            CG[:, own_rows, :] = (CG[:, own_rows, :].astype(F4) + CS[...].astype(F4)).astype(BF)
            cg_copy.start()
    def down_block(b): return dot(A[:, columns(b)].T, LOW[...])
    if early:
        @pl.when(dec)
        def _():
            for b in range(4):
                block(G0, 4 + b)[...] = down_block(b).astype(BF)
                done_blocks(0, G0, 5 + b)
                if b == 1: begin(0, (0,))
    else:
        for b in range(4): grad_block(4 + b, lambda: down_block(b), lambda: dot(A[second, columns(b)].T, LOW[second, :]))

    @pl.when(dec)
    def _(): loop(0, 2, decoder_rest)

    first_left = jnp.where(enc, 1, 0)

    def start_ring(m, place):
        @pl.when(m == first_left)
        def _():
            if not early: begin(0) if place == 0 else reduce_round(0, 1)
            elif place == 0:
                @pl.when(enc)
                def _():
                    begin(0, (0,))
                    reduce_round(0, 1, (1,))
                pl.when(dec)(lambda: begin(0, (1,)))
            else: pl.when(dec)(lambda: reduce_round(0, 1))
    loop(first_left, 2, lambda m: bottom(m, start_ring))
    if early: pl.when(enc)(lambda: reduce_round(0, 1, (0,)))
    NG[...] = jnp.zeros_like(NG)
    for j in range(4):
        NG[0, j] = PG[:, 128 * j:128 * (j + 1)]
        NG[1, j] = PB[:, 128 * j:128 * (j + 1)]
    sib_norm.start()
    weight_grads(1, G1, H1, DQKV, 3, 0)
    weight_grads(1, G1, O, LOWS, 1, 3)
    if not direct:
        @pl.when(enc)
        def _():
            for m in (0, 1): dk_copy(m).wait_recv()
            T[...] = ST[...].T
            for b in range(2): block(G1, 4 + b)[...] = dot(T[...], DKV[:, columns(b)]).astype(BF)
    @pl.when(dec)
    def _():
        for b, (source, grad) in enumerate(((HQ, DCQ), (O2, LOWC))):
            T[...] = source[...].T
            block(G1, 4 + b)[...] = dot(T[...], grad[...]).astype(BF)
            if direct: done_blocks(1, G1, 5 + b)
    if not direct: done_blocks(1, G1, 6)
    if early: reduce_round(0, 2, (1,))
    begin(1)
    if far == 4:
        reduce_round(0, 2, (0,))
        reduce_round(1, 1)
        reduce_round(0, 3)
        reduce_round(1, 2)
        settle(0)
        reduce_round(1, 3)
        gather_round(0, 1)
        settle(1)
        gather_round(0, 2)
        gather_round(1, 1)
        gather_round(0, 3)
        gather_round(1, 2)
        gather_round(0, 4)
        gather_round(1, 3)
        gather_round(1, 4)
    else:
        reduce_round(1, 1)
        for g in (0, 1):
            loop(2, far, lambda s: reduce_round(g, s))
            settle(g)
            loop(1, far - 1, lambda t: gather_round(g, t))
            gather_round(g, far - 1)
            gather_round(g, far)
    close_ring()

    @pl.when(enc)
    def _():
        wc_copy.wait_send()
        for m in (0, 1): st_copy(m).wait_send()
    @pl.when(dec)
    def _():
        for trade in wc_trades: trade.wait_send()
        for m in (0, 1):
            ds_copy(m).wait_send()
            if not direct: dk_copy(m).wait_send()
        if direct:
            cg_trade.wait_send()
            cg_copy.wait_send()


def finish_kernel(e0, e1, en, out, gin, o_out, o_gin, o_qkv, o_wo, o_up, o_down, o_cross, o_gain, o_bias, F, sem, sem2):
    copies = [pltpu.make_async_copy(out, o_out, sem2.at[0]), pltpu.make_async_copy(gin, o_gin, sem2.at[1])]
    for copy in copies: copy.start()
    for j in range(4):
        at = pl.ds(128 * j, 128)
        for i in range(3):
            o_gain[i, :, at] = en[0, j, i:i + 1, :]
            o_bias[i, :, at] = en[1, j, i:i + 1, :]
    def columns(b): return pl.ds(b * SIDE, SIDE)
    targets = [(e0, b, o_up.at[0, :, columns(b)]) for b in range(4)] + [(e0, 4 + b, o_down.at[0, columns(b), :]) for b in range(4)]
    targets += [(e1, b, o_qkv.at[0, :, columns(b)]) for b in range(3)] + [(e1, 3, o_wo.at[0])]
    targets += [(e1, 4 + b, o_cross.at[0, :, columns(b)]) for b in range(2)]
    slots = F.shape[0]
    flight = []
    for i, (e, b, target) in enumerate(targets):
        if i >= slots: flight[i - slots].wait()
        F[i % slots] = block(e, b)[...].astype(F4)
        flight.append(pltpu.make_async_copy(F.at[i % slots], target, sem.at[i % slots]))
        flight[-1].start()
    for copy in flight[-slots:] + copies: copy.wait()


def layers(lens, x, ct, wq, wo, w1, w2, wc, gn, bs, n):
    micro, length, width = x.shape
    rows, hidden = micro * length, w1.shape[1]
    any_ = pl.BlockSpec(memory_space=pl.ANY)
    vmem = pl.BlockSpec(memory_space=pltpu.VMEM)
    V, DMA = pltpu.VMEM, pltpu.SemaphoreType.DMA
    def units(count): return (-(-count * SIDE // (64 * n)), 64 * n, SIDE)
    s0, s1 = units(8), units(6)
    norm = (2, n, 8, 128)
    def own(s): return (s[0], s[1] // 2, SIDE)
    def slots(s): return (2, n // 2, s[0], 32, SIDE)
    sq = V((rows, width), BF)
    probs = V((micro * width // 64, length, length), BF)
    scratch = [V(x.shape, BF), V(x.shape, BF), V(wc.shape, BF), V(gn.shape, F4), V(bs.shape, F4)]
    scratch += [sq, V((rows, 3 * width), BF), probs, sq, V((2, rows, width), F4), sq, sq, sq, V((rows, 2 * width), BF), probs, sq, sq,
                V((rows, hidden), BF), V((rows, hidden), BF), V((rows, hidden), BF), V((rows, width), F4), V((rows, width), F4),
                sq, sq, sq, sq, V((rows, 3 * width), BF), sq, V((rows, 2 * width), BF), sq, V((width, rows), BF)]
    scratch += [V(s0, BF), V(s1, BF), V(norm, F4), V((2, SIDE, SIDE), BF), V((2, SIDE // 2, SIDE), BF), V(own(s0), BF), V(own(s1), BF), V(norm[1:], F4), V(slots(s0), BF), V(slots(s1), BF), V((2, n // 2, 8, 128), F4),
                V((8, width), F4), V((8, width), F4)]
    scratch += [DMA((18,)), DMA, DMA, DMA((3,)), DMA((3,)), DMA((2,)), DMA((2,)), DMA((2,)), DMA((2,)), DMA((2,)), DMA((2,)), DMA((2,)), DMA((2,)), DMA((7,)), DMA((7,)), DMA((3,)), DMA((10, n // 2)), DMA((3,)), DMA((10, n // 2)), DMA((3,)), DMA((3,))]
    results = [V(s0, BF), V(s1, BF), V(norm, F4), V(x.shape, BF), V(x.shape, BF)]
    e0, e1, en, out, gin = pl.pallas_call(
        functools.partial(layers_kernel, n), out_shape=results,
        in_specs=[pl.BlockSpec(memory_space=pltpu.SMEM)] + [any_] * 9, out_specs=[vmem] * 5, scratch_shapes=scratch,
        compiler_params=pltpu.CompilerParams(collective_id=1, has_side_effects=True, vmem_limit_bytes=53 * 2**20),
        name="layers",
    )(lens, x, ct, wq, wo, w1, w2, wc, gn, bs)
    def f4(*shape): return jax.ShapeDtypeStruct(shape, F4)
    return pl.pallas_call(
        finish_kernel,
        out_shape=[jax.ShapeDtypeStruct(x.shape, BF)] * 2 + [f4(1, width, 3 * width), f4(1, width, width), f4(1, width, hidden), f4(1, hidden, width),
                                                            f4(1, width, 2 * width), f4(3, 1, width), f4(3, 1, width)],
        in_specs=[vmem] * 5, out_specs=[any_] * 7 + [vmem] * 2,
        scratch_shapes=[V((4, SIDE, SIDE), F4), DMA((4,)), DMA((2,))],
        compiler_params=pltpu.CompilerParams(vmem_limit_bytes=6 * 2**20),
        name="finish",
    )(e0, e1, en, out, gin)


def local(layer_input, lengths, attn_qkv, attn_out, ffn_in, ffn_out, cross_weight, norm_gain, norm_bias, cotangent):
    def flat(a): return a.reshape(a.shape[1:])
    n = lax.axis_size("dp") // 2
    data = (layer_input.shape[1],) + layer_input.shape[3:]
    out, gin, *grads, gain, bias = layers(lengths.T, layer_input.reshape(data), cotangent.reshape(data), flat(attn_qkv), flat(attn_out), flat(ffn_in), flat(ffn_out),
                              flat(cross_weight), norm_gain.transpose(1, 0, 2), norm_bias.transpose(1, 0, 2), n)
    return (out.reshape(layer_input.shape), gin.reshape(layer_input.shape), *grads, gain.transpose(1, 0, 2), bias.transpose(1, 0, 2))


def solution(mesh):
    data = P("section", None, "dp", None, None)
    weight = P("section", None, None)
    return jax.shard_map(
        local, mesh=mesh,
        in_specs=(data, P(None, "dp")) + (weight,) * 7 + (data,),
        out_specs=(data, data) + (weight,) * 7,
        check_vma=False,
    )
```
